256 devices in a mesh: dp: 4 (over x), expert: 64 (over y, z, core).
Axes of the slice: x: 4, y: 4, z: 8, core: 2. Of those that a mesh axis runs over, the one named last changes fastest.
Arguments:
- tokens: bfloat16 [8192, 3584], P(('dp', 'expert')), may hold values from -6 to 6
- routes: int32 [8192, 8], P(('dp', 'expert')), may hold values from 0 to 127, all different within a row; in each aligned block of 32 rows (0 to 31, 32 to 63, ...) at most 4 rows name the same one
- route_weight: float32 [8192, 8], P(('dp', 'expert')), may hold values from 0.1 to 1
- gate_weight: bfloat16 [128, 3584, 1024], P('expert', None, 'dp'), may hold values from -0.09375 to 0.09375
- up_weight: bfloat16 [128, 3584, 1024], P('expert', None, 'dp'), may hold values from -0.09375 to 0.09375
- down_weight: bfloat16 [128, 1024, 3584], P('expert', 'dp'), may hold values from -0.1875 to 0.1875
- gate_scale: float32 [128, 28, 8], P('expert', None, 'dp'), may hold values from 0.5 to 2
- up_scale: float32 [128, 28, 8], P('expert', None, 'dp'), may hold values from 0.5 to 2
- down_scale: float32 [128, 8, 28], P('expert', 'dp'), may hold values from 0.5 to 2
Outputs:
- mixed: bfloat16 [8192, 3584], P(('dp', 'expert'))
- load_share: float32 [128], replicated
The draws below stay inside these ranges and needn't reach their ends.
Inputs may be any that keep to these rules, and one draw needn't show every extreme that they name: `routes`: each row names 8 different experts. Within the rows of one device (32 aligned rows) no expert is named by more than 4 rows, and in every draw some expert is named by exactly 4 rows of some device.
All inputs are finite; a program needn't handle non-finite values.
Results may differ from the reference program's by a relative error of at most 0.015.
Values may be sent and summed in bfloat16 or wider, within the bound.
No kernel may reach another device: no remote copies, remote signals or barrier semaphores. Data moves between devices by JAX's collectives and lax.ppermute only.
A program may use at most 192 MiB of HBM per device.

```python
import math
import jax
import jax.numpy as jnp
import numpy as np
from jax import lax

D = 3584
FF = 1024
TOPK = 8
HOT = 2
BLOCK = 128
TOK_DEV = 32
EXPERTS = 128
TOKENS = 8192
CAP = 3
N_DP = 4
N_EXPERT = 64


def shard_levels(key, dims, split, least, high):
    def one(dim, parts):
        heights = jax.random.uniform(jax.random.fold_in(jax.random.fold_in(key, 6), dim), (parts,), jnp.float32, least / len(split), high / len(split))
        return jnp.repeat(jnp.exp(heights), dims[dim] // parts).reshape((-1,) + (1,) * (len(dims) - dim - 1))

    factor_of = one(*split[0])
    for cut in split[1:]:
        factor_of = factor_of * one(*cut)
    return factor_of


def assign_block(own_key, own, number, rows, count, top, limit, lean):
    ranking = jax.random.permutation(own_key, count)
    crowded, common = shares(count, rows * top, limit, lean, True), shares(count, rows * top, limit, lean, False)
    places = jnp.arange(count)

    def named(tallies, offset_by):
        used = int((tallies > 0).sum())
        fixed = max(1, used // 4)
        moved = fixed + (places - fixed + offset_by * (used - fixed)) % max(1, count - fixed)
        return jnp.zeros((count,), jnp.int32).at[ranking[jnp.where(places < fixed, places, moved)]].set(jnp.asarray(tallies, jnp.int32))

    tallies = jnp.where(number % 4 == 0, named(crowded, number // 4), named(common, number - number // 4 - 1))
    mixed = jax.random.permutation(jax.random.fold_in(own, 3), count)
    donor, taker = mixed[0:count // 2 * 2:2], mixed[1:count // 2 * 2:2]
    margin = jnp.minimum(tallies[donor] - 1, limit - tallies[taker]) // 2
    margin = jnp.where((donor == ranking[0]) | (taker == ranking[0]) | (tallies[taker] == 0), 0, jnp.maximum(margin, 0))
    moved = jax.random.randint(jax.random.fold_in(own, 4), (count // 2,), 0, 1 << 20) % (margin + 1)
    tallies = tallies.at[donor].add(-moved).at[taker].add(moved)
    members = jnp.searchsorted(jnp.cumsum(tallies), jnp.arange(rows * top), side="right").astype(jnp.int32)
    table = members.reshape(top, rows).T
    table = table[jax.random.permutation(jax.random.fold_in(own, 1), rows)]
    offset_by = jax.random.randint(jax.random.fold_in(own, 2), (rows, 1), 0, top)
    return jnp.take_along_axis(table, (jnp.arange(top)[None, :] + offset_by) % top, axis=1)


def shares(amount, total, bound, slope, full):
    loads = [(1 << 20) // math.isqrt(standing ** slope) + 1 for standing in range(1, amount + 1)]
    largest = bound if full else min(bound, max(-(-total // amount), total * loads[0] // sum(loads)))
    least = 1 if total - largest >= amount - 1 else 0
    given, rest = [largest] + [least] * (amount - 1), total - largest - least * (amount - 1)
    while rest > 0:
        free = [i for i in range(1, amount) if given[i] < largest] or [i for i in range(1, amount) if given[i] < bound]
        whole, remaining = sum([loads[i] for i in free]), rest
        for i in free:
            addition = min(bound - given[i], max(1, remaining * loads[i] // whole), rest)
            given[i] = given[i] + addition
            rest = rest - addition
    return np.array(given)


def bell_draw(rng, dims, deviation, reach, cuts=(), kind=jnp.bfloat16):
    entries = deviation * jax.random.normal(rng, dims, jnp.float32)
    if cuts:
        entries = entries * shard_levels(rng, dims, cuts, -0.22, 0.18)
    return jnp.clip(entries, -reach, reach).astype(kind)


def setup_inputs(seed: int = 0) -> dict:
    keys = jax.random.split(jax.random.key(seed), 10)
    tokens = bell_draw(keys[0], (TOKENS, D), 1.0, 6.0, ((0, 256),))
    routes_keys = jax.random.split(jax.random.fold_in(keys[1], 1), TOKENS // TOK_DEV)
    routes_turns = jax.random.permutation(jax.random.fold_in(keys[1], 3), TOKENS // TOK_DEV)
    routes = jax.vmap(lambda own, number: assign_block(jax.random.fold_in(keys[1], 2), own, number, TOK_DEV, EXPERTS, TOPK, CAP + 1, 2))(routes_keys, routes_turns).reshape((TOKENS, TOPK))
    route_weight = jnp.clip(0.1 + 0.9 * jax.random.uniform(keys[2], (TOKENS, TOPK), jnp.float32) ** shard_levels(keys[2], (TOKENS, TOPK), ((0, 256),), -0.2, 0.2), 0.1, 1.0)
    gate_weight = bell_draw(keys[3], (EXPERTS, D, FF), D ** -0.5, 0.09375, ((0, 64), (2, 4)))
    up_weight = bell_draw(keys[4], (EXPERTS, D, FF), D ** -0.5, 0.09375, ((0, 64), (2, 4)))
    down_weight = bell_draw(keys[5], (EXPERTS, FF, D), FF ** -0.5, 0.1875, ((0, 64), (1, 4)))
    gate_scale = jnp.clip(jnp.exp(math.log(2.0) - 1.3862944 * jax.random.uniform(keys[6], (EXPERTS, D // BLOCK, FF // BLOCK), jnp.float32) ** shard_levels(keys[6], (EXPERTS, D // BLOCK, FF // BLOCK), ((0, 64), (2, 4)), -0.2, 0.2)), 0.5, 2.0)
    up_scale = jnp.clip(jnp.exp(math.log(2.0) - 1.3862944 * jax.random.uniform(keys[7], (EXPERTS, D // BLOCK, FF // BLOCK), jnp.float32) ** shard_levels(keys[7], (EXPERTS, D // BLOCK, FF // BLOCK), ((0, 64), (2, 4)), -0.2, 0.2)), 0.5, 2.0)
    down_scale = jnp.clip(jnp.exp(math.log(2.0) - 1.3862944 * jax.random.uniform(keys[8], (EXPERTS, FF // BLOCK, D // BLOCK), jnp.float32) ** shard_levels(keys[8], (EXPERTS, FF // BLOCK, D // BLOCK), ((0, 64), (1, 4)), -0.2, 0.2)), 0.5, 2.0)
    return {"tokens": tokens, "routes": routes, "route_weight": route_weight, "gate_weight": gate_weight, "up_weight": up_weight, "down_weight": down_weight, "gate_scale": gate_scale, "up_scale": up_scale, "down_scale": down_scale}


def dequantize(weight, block_scale):
    rows_all, cols_all = weight.shape
    blocks = weight.astype(jnp.float32).reshape(rows_all // BLOCK, BLOCK, cols_all // BLOCK, BLOCK)
    blocks = blocks * block_scale[:, None, :, None]
    return blocks.reshape(rows_all, cols_all).astype(jnp.bfloat16)


def reference(tokens, routes, route_weight, gate_weight, up_weight, down_weight, gate_scale, up_scale, down_scale):
    experts = EXPERTS
    labels = jnp.arange(experts, dtype=jnp.int32)
    per_row = jnp.sum((routes[:, :, None] == labels[None, None, :]).astype(jnp.int32), axis=1)
    load_totals = jnp.sum(per_row, axis=0)
    load_share = load_totals.astype(jnp.float32) * (experts / (TOKENS * TOPK))
    _, hot_ids = lax.top_k(load_totals * experts + (experts - 1 - labels), HOT)
    blocked = per_row.reshape(TOKENS // TOK_DEV, TOK_DEV, experts)
    before = (jnp.cumsum(blocked, axis=1) - blocked).reshape(TOKENS, experts)
    rank_index = jnp.take_along_axis(before, routes, axis=1)
    is_hot = jnp.any(routes[:, :, None] == hot_ids[None, None, :], axis=-1)
    kept_mask = is_hot | (rank_index < CAP)
    weights = jnp.where(kept_mask, route_weight, 0.0).astype(jnp.float32)
    flat_routes = jnp.where(kept_mask, routes, experts).reshape(-1).astype(jnp.int32)
    row_limit = min(TOKENS, N_DP * N_EXPERT * (CAP + 1))
    quarter = FF // N_DP
    padded_tokens = jnp.concatenate([tokens, jnp.zeros((1, D), jnp.bfloat16)], axis=0)
    padded_weights = jnp.concatenate([weights.reshape(-1), jnp.zeros((1,), jnp.float32)], axis=0)

    def one_expert(running, inputs):
        expert_id, gate_raw, up_raw, down_raw, gate_blocks, up_blocks, down_blocks = inputs
        chosen = jnp.nonzero(flat_routes == expert_id, size=row_limit, fill_value=TOKENS * TOPK)[0].astype(jnp.int32)
        token_index = chosen // TOPK
        token_rows = padded_tokens[token_index]
        gate_val = jnp.dot(token_rows, dequantize(gate_raw, gate_blocks), preferred_element_type=jnp.float32)
        up_val = jnp.dot(token_rows, dequantize(up_raw, up_blocks), preferred_element_type=jnp.float32)
        hidden = (jax.nn.silu(gate_val) * up_val).astype(jnp.bfloat16)
        down_deq = dequantize(down_raw, down_blocks)
        partial_sums = jnp.einsum("rqf,qfd->rqd", hidden.reshape(row_limit, N_DP, quarter).astype(jnp.float32), down_deq.reshape(N_DP, quarter, D).astype(jnp.float32))
        partial_sums = lax.optimization_barrier(partial_sums.astype(jnp.bfloat16))
        result = jnp.sum(partial_sums.astype(jnp.float32), axis=1).astype(jnp.bfloat16)
        running = running.at[token_index].add(padded_weights[chosen][:, None] * result.astype(jnp.float32))
        return running, None

    inputs = (labels, gate_weight, up_weight, down_weight, gate_scale, up_scale, down_scale)
    running, _ = lax.scan(one_expert, jnp.zeros((TOKENS + 1, D), jnp.float32), inputs)
    return running[:TOKENS].astype(jnp.bfloat16), load_share
```

```python
import functools

import jax
import jax.numpy as jnp
from jax import lax
from jax.experimental import pallas as pl
from jax.experimental.pallas import tpu as pltpu
from jax.sharding import PartitionSpec as P

BLOCK = 128
CAP = 3
NY, NZ, NC, NX = 4, 8, 2, 4
SRC = NZ * NC
PIECE = SRC * CAP
META = 128
COLS = 512
BF = jnp.bfloat16
F32 = jnp.float32
VMEM = 48 * 1024 * 1024


def expert_move(value, dy=0, dz=0, flip=False, xor_y=0):
    pairs = []
    for y in range(NY):
        for z in range(NZ):
            for c in range(NC):
                to_y = (y + dy) % NY ^ xor_y
                to_z = (z + dz) % NZ
                to_c = c ^ 1 if flip else c
                pairs.append(((y * NZ + z) * NC + c, (to_y * NZ + to_z) * NC + to_c))
    return lax.ppermute(value, "expert", pairs)


def dp_move(value, dx=0, xor_x=0):
    return lax.ppermute(value, "dp", [(x, (x + dx) % NX ^ xor_x) for x in range(NX)])


def slot_values(metas, lanes):
    tokens = metas.shape[0]
    found = jnp.zeros((tokens, META), F32)
    for k in range(8):
        found += jnp.where(metas[:, k : k + 1] == lanes, 1.0, 0.0)
    row = lax.broadcasted_iota(jnp.int32, (tokens, tokens), 0)
    col = lax.broadcasted_iota(jnp.int32, (tokens, tokens), 1)
    earlier = jnp.where(((row >> 5) == (col >> 5)) & (col < row), 1.0, 0.0).astype(BF)
    rank = jnp.dot(earlier, found.astype(BF), preferred_element_type=F32)
    return found * (rank + 1.0)


def slot_parts(slots):
    lane = (slots * 1366) >> 16
    rest = slots - lane * PIECE
    return lane, rest >> 4, rest & 15


def gather_kernel(lanes_ref, *refs):
    pieces, outs, counts_ref = refs[:SRC], refs[SRC : SRC + 8], refs[SRC + 8]
    tokens, slots = SRC * 32, 8 * PIECE
    depth = outs[0].shape[1]
    metas = jnp.concatenate([p[:, depth : depth + META] for p in pieces], axis=0).astype(F32)
    values = slot_values(metas, lanes_ref[0:1, :])
    every = lax.broadcasted_iota(jnp.int32, (1, META), 1).astype(F32)
    total = jnp.zeros((tokens, META), F32)
    for k in range(8):
        total += jnp.where(metas[:, k : k + 1] == every, 1.0, 0.0)
    counts_ref[...] = jnp.broadcast_to(jnp.sum(total, axis=0, keepdims=True), (8, META))
    slot_lane, _, _ = slot_parts(lax.broadcasted_iota(jnp.int32, (slots, META), 0))
    spread = jnp.where(
        slot_lane == lax.broadcasted_iota(jnp.int32, (slots, META), 1), 1.0, 0.0
    ).astype(BF)
    picked = lax.dot_general(
        spread, values.astype(BF), (((1,), (1,)), ((), ())), preferred_element_type=F32
    )
    _, rank, source = slot_parts(lax.broadcasted_iota(jnp.int32, (slots, tokens), 0))
    token = lax.broadcasted_iota(jnp.int32, (slots, tokens), 1)
    choose = jnp.where(
        (picked == (rank + 1).astype(F32)) & (source == (token >> 5)), 1.0, 0.0
    ).astype(BF)
    for start in range(0, depth, COLS):
        block = jnp.concatenate([p[:, start : start + COLS] for p in pieces], axis=0)
        rows = jnp.dot(choose, block, preferred_element_type=F32).astype(BF)
        for j in range(8):
            outs[j][:, start : start + COLS] = rows[j * PIECE : (j + 1) * PIECE]


def scatter_kernel(lanes_ref, *refs):
    pieces, rows_in = refs[:SRC], refs[SRC : SRC + 8]
    own_ref, other_ref = refs[SRC + 8 :]
    tokens, slots = SRC * 32, 8 * PIECE
    depth = own_ref.shape[1]
    lanes = lanes_ref[0:1, :]
    metas = jnp.concatenate([p[:, depth : depth + META] for p in pieces], axis=0).astype(F32)
    values = slot_values(metas, lanes)
    high = jnp.zeros((tokens, META), F32)
    low = jnp.zeros((tokens, META), F32)
    for k in range(8):
        match = metas[:, k : k + 1] == lanes
        high += jnp.where(match, metas[:, 8 + k : 9 + k], 0.0)
        low += jnp.where(match, metas[:, 16 + k : 17 + k], 0.0)
    slot_lane, _, _ = slot_parts(lax.broadcasted_iota(jnp.int32, (META, slots), 1))
    spread = jnp.where(
        slot_lane == lax.broadcasted_iota(jnp.int32, (META, slots), 0), 1.0, 0.0
    ).astype(BF)
    picked = jnp.dot(values.astype(BF), spread, preferred_element_type=F32)
    _, rank, source = slot_parts(lax.broadcasted_iota(jnp.int32, (tokens, slots), 1))
    token = lax.broadcasted_iota(jnp.int32, (tokens, slots), 0)
    there = (picked == (rank + 1).astype(F32)) & (source == (token >> 5))
    high_at = jnp.dot(high.astype(BF), spread, preferred_element_type=F32)
    low_at = jnp.dot(low.astype(BF), spread, preferred_element_type=F32)
    high_at = jnp.where(there, high_at, 0.0).astype(BF)
    low_at = jnp.where(there, low_at, 0.0).astype(BF)
    half = tokens // 2
    for start in range(0, depth, COLS):
        block = jnp.concatenate([r[:, start : start + COLS] for r in rows_in], axis=0)
        sums = jnp.dot(high_at, block, preferred_element_type=F32)
        sums += jnp.dot(low_at, block, preferred_element_type=F32)
        sums = sums.astype(BF)
        own_ref[:, start : start + COLS] = sums[:half]
        other_ref[:, start : start + COLS] = sums[half:]


def whole(count):
    return [pl.BlockSpec(memory_space=pltpu.VMEM)] * count


def gather_rows(lanes, pieces, depth):
    out = [jax.ShapeDtypeStruct((PIECE, depth), BF)] * 8
    return pl.pallas_call(
        gather_kernel,
        out_shape=out + [jax.ShapeDtypeStruct((8, META), F32)],
        in_specs=whole(1 + SRC),
        out_specs=whole(9),
        compiler_params=pltpu.CompilerParams(vmem_limit_bytes=VMEM),
        cost_estimate=pl.CostEstimate(
            flops=2 * 384 * 512 * depth, bytes_accessed=7 * 1024 * 1024, transcendentals=0
        ),
        name="gather_rows",
    )(lanes, *pieces)


def scatter_rows(lanes, pieces, rows, depth):
    return pl.pallas_call(
        scatter_kernel,
        out_shape=[jax.ShapeDtypeStruct((SRC * 16, depth), BF)] * 2,
        in_specs=whole(1 + SRC + 8),
        out_specs=whole(2),
        compiler_params=pltpu.CompilerParams(vmem_limit_bytes=VMEM),
        cost_estimate=pl.CostEstimate(
            flops=4 * 384 * 512 * depth, bytes_accessed=10 * 1024 * 1024, transcendentals=0
        ),
        name="scatter_rows",
    )(lanes, *pieces, *rows)


def ffn_kernel(in_rows, out_rows, steps, masked, *refs):
    refs = list(refs)
    flags = refs.pop(0) if masked else None
    xs, refs = refs[: len(in_rows)], refs[len(in_rows) :]
    gate_w, up_w, down_w, gate_s, up_s, down_s = refs[:6]
    outs, (gate_acc, up_acc, hidden) = refs[6 : 6 + len(out_rows)], refs[6 + len(out_rows) :]
    step = pl.program_id(0)
    blocks = COLS // BLOCK

    def deq(w_ref, s_ref):
        parts = []
        for b in range(blocks):
            scale = s_ref[0, pl.ds(step * blocks + b, 1), :]
            part = w_ref[0, b * BLOCK : (b + 1) * BLOCK, :].astype(F32) * scale
            parts.append(part.astype(BF))
        return jnp.concatenate(parts, axis=0)

    @pl.when(step < steps)
    def _():
        x = jnp.concatenate([r[...] for r in xs], axis=0)
        gate = jnp.dot(x, deq(gate_w, gate_s), preferred_element_type=F32)
        up = jnp.dot(x, deq(up_w, up_s), preferred_element_type=F32)

        @pl.when(step == 0)
        def _():
            gate_acc[...] = gate
            up_acc[...] = up

        @pl.when(step > 0)
        def _():
            gate_acc[...] += gate
            up_acc[...] += up

    @pl.when(step == steps)
    def _():
        gate = gate_acc[...]
        value = gate * (1.0 / (1.0 + jnp.exp(-gate))) * up_acc[...]
        if masked:
            odd = lax.broadcasted_iota(jnp.int32, value.shape, 0) & 1
            value = jnp.where(jnp.where(odd == 1, flags[1], flags[0]) == 1, value, 0.0)
        hidden[...] = value.astype(BF)

    @pl.when(step >= steps)
    def _():
        parts = []
        for b in range(down_w.shape[1] // BLOCK):
            part = down_w[0, b * BLOCK : (b + 1) * BLOCK, :].astype(F32) * down_s[0, b : b + 1, :]
            parts.append(part.astype(BF))
        result = jnp.dot(
            hidden[...], jnp.concatenate(parts, axis=0), preferred_element_type=F32
        ).astype(BF)
        at = 0
        for ref, count in zip(outs, out_rows):
            ref[...] = result[at : at + count]
            at += count


def ffn(xs, out_rows, which, weights, flags=None):
    gate_w, up_w, down_w, gate_s, up_s, down_s = weights
    depth, units = gate_w.shape[1:]
    steps = depth // COLS
    in_rows = [x.shape[0] for x in xs]
    total = sum(in_rows)
    masked = flags is not None

    def early(i):
        return jnp.minimum(i, steps - 1)

    def late(i):
        return jnp.maximum(i - steps, 0)

    in_specs = [pl.BlockSpec(memory_space=pltpu.SMEM)] if masked else []
    in_specs += [pl.BlockSpec((r, COLS), lambda i: (0, early(i))) for r in in_rows]
    in_specs += [pl.BlockSpec((1, COLS, units), lambda i: (which, early(i), 0))] * 2
    in_specs += [pl.BlockSpec((1, units, COLS), lambda i: (which, 0, late(i)))]
    in_specs += [pl.BlockSpec((1,) + gate_s.shape[1:], lambda i: (which, 0, 0))] * 2
    in_specs += [pl.BlockSpec((1, down_s.shape[1], COLS), lambda i: (which, 0, late(i)))]
    return pl.pallas_call(
        functools.partial(ffn_kernel, in_rows, out_rows, steps, masked),
        grid=(2 * steps,),
        out_shape=[jax.ShapeDtypeStruct((r, depth), BF) for r in out_rows],
        in_specs=in_specs,
        out_specs=[pl.BlockSpec((r, COLS), lambda i: (0, late(i))) for r in out_rows],
        scratch_shapes=[
            pltpu.VMEM((total, units), F32),
            pltpu.VMEM((total, units), F32),
            pltpu.VMEM((total, units), BF),
        ],
        compiler_params=pltpu.CompilerParams(vmem_limit_bytes=VMEM),
        cost_estimate=pl.CostEstimate(
            flops=6 * total * units * depth,
            bytes_accessed=4 * total * depth + 6 * units * depth,
            transcendentals=total * units,
        ),
        name="ffn",
    )(*((flags,) if masked else ()), *xs, gate_w, up_w, down_w, gate_s, up_s, down_s)


def add(*values):
    total = values[0].astype(F32)
    for value in values[1:]:
        total = total + value.astype(F32)
    return total.astype(BF)


def gather_line(own):
    pieces = [own] + [None] * (NZ - 1)
    up = down = own
    for step in range(1, NZ // 2 + 1):
        up = expert_move(up, dz=-1)
        pieces[step] = up
        if step < NZ // 2:
            down = expert_move(down, dz=1)
            pieces[NZ - step] = down
    return pieces + [expert_move(piece, flip=True) for piece in pieces]


def scatter_line(own, other):
    arrived = expert_move(other, flip=True)

    def term(dz):
        return own[dz * 32 : dz * 32 + 32], arrived[dz * 32 : dz * 32 + 32]

    up = add(*term(NZ // 2))
    for dz in range(NZ // 2 - 1, 0, -1):
        up = add(expert_move(up, dz=1), *term(dz))
    down = add(*term(NZ // 2 + 1))
    for dz in range(NZ // 2 + 2, NZ):
        down = add(expert_move(down, dz=-1), *term(dz))
    return [expert_move(up, dz=1), expert_move(down, dz=-1), *term(0)]


def spread_dp(block):
    half = block.shape[0] // 2
    left = dp_move(block, 1)
    right = dp_move(block, -1)
    far_a = dp_move(left[:half], 1)
    far_b = dp_move(right[half:], -1)
    return [block, left, right, far_a, far_b]


def sum_dp(parts):
    own, left_a, left_b, right_a, right_b, far_a, far_b = parts
    from_a = dp_move(far_a, -1)
    from_b = dp_move(far_b, 1)
    got_left_b = dp_move(left_b, -1)
    got_right_a = dp_move(right_a, 1)
    got_left_a = dp_move(add(left_a, from_a), -1)
    got_right_b = dp_move(add(right_b, from_b), 1)
    half = own.shape[0] // 2
    result = []
    for j in range(NY):
        low = j * PIECE
        if low < half:
            terms = (got_left_a[low : low + PIECE], got_right_a[low : low + PIECE])
        else:
            at = low - half
            terms = (got_left_b[at : at + PIECE], got_right_b[at : at + PIECE])
        result.append(add(own[low : low + PIECE], *terms))
    return result


def per_device(
    tokens,
    routes,
    route_weight,
    gate_weight,
    up_weight,
    down_weight,
    gate_scale,
    up_scale,
    down_scale,
):
    rows, depth = tokens.shape
    top = routes.shape[1]
    experts = gate_weight.shape[0] * NY * NZ * NC
    all_rows = rows * NX * NY * NZ * NC
    place = lax.axis_index("expert")
    y, line = place // (NZ * NC), place % (NZ * NC)

    high = lax.reduce_precision(route_weight, 8, 7)
    low = lax.reduce_precision(route_weight - high, 8, 7)
    meta = jnp.concatenate(
        [routes.astype(BF), high.astype(BF), low.astype(BF), jnp.zeros((rows, META - 3 * top), BF)],
        axis=1,
    )
    pieces = gather_line(jnp.concatenate([tokens, meta], axis=1))

    lane = jnp.arange(META, dtype=jnp.int32)
    lane_expert = ((((y + lane % NY) % NY) * (NZ * NC) + line) * 2 + lane // NY).astype(F32)
    lanes = jnp.broadcast_to(jnp.where(lane < 8, lane_expert, -1.0)[None], (8, META))
    *blocks, counts = gather_rows(lanes, pieces, depth)

    weights = (
        gate_weight,
        up_weight,
        down_weight,
        jnp.repeat(gate_scale, BLOCK, axis=2),
        jnp.repeat(up_scale, BLOCK, axis=2),
        jnp.repeat(down_scale, BLOCK, axis=2),
    )
    half = NY * PIECE // 2
    parts = []
    for which in range(2):
        group = blocks[which * NY : (which + 1) * NY]
        group = [group[0]] + [expert_move(group[d], dy=d) for d in range(1, NY)]
        spread = spread_dp(jnp.concatenate(group, axis=0))
        parts.append(ffn(spread, [2 * half] + [half] * 6, which, weights))

    counts = counts + expert_move(counts, xor_y=1)
    counts = counts + expert_move(counts, xor_y=2)
    counts = counts + dp_move(counts, xor_x=1)
    counts = counts + dp_move(counts, xor_x=2)
    load_totals = counts[0, :experts]
    load_share = load_totals * (experts / (all_rows * top))
    label = jnp.arange(experts, dtype=jnp.int32)
    order = load_totals.astype(jnp.int32) * experts + (experts - 1 - label)
    first = experts - 1 - jnp.max(order) % experts
    second = experts - 1 - jnp.max(jnp.where(label == first, -1, order)) % experts
    hot = jnp.stack([first, second])

    named = routes[:, :, None] == hot[None, None, :]
    named_row = jnp.any(named, axis=1)
    before = jnp.arange(rows)[:, None] >= jnp.arange(rows)[None, :]
    upto = jnp.sum((before[:, :, None] & named_row[None, :, :]).astype(jnp.int32), axis=1)
    extra = named_row & (upto == CAP + 1)
    extra_weight = jnp.where(extra, jnp.sum(jnp.where(named, route_weight[:, :, None], 0.0), axis=1), 0.0)
    extra_rows = jnp.einsum(
        "tj,td->jd", extra.astype(BF), tokens, preferred_element_type=F32
    ).astype(BF)
    extra_rows = lax.all_gather(extra_rows, "dp", axis=0, tiled=True)
    extra_rows = lax.all_gather(extra_rows, "expert", axis=0, tiled=True)
    extra_parts = [
        ffn(
            [extra_rows],
            [extra_rows.shape[0]],
            which,
            weights,
            (hot == place * 2 + which).astype(jnp.int32),
        )[0]
        for which in range(2)
    ]
    extra_out = extra_parts[0] + extra_parts[1]
    extra_out = lax.psum_scatter(extra_out, "expert", scatter_dimension=0, tiled=True)
    extra_out = lax.psum_scatter(extra_out, "dp", scatter_dimension=0, tiled=True).astype(F32)

    returned = []
    for which in range(2):
        group = sum_dp(parts[which])
        returned += [group[0]] + [expert_move(group[d], dy=-d) for d in range(1, NY)]
    terms = scatter_line(*scatter_rows(lanes, pieces, returned, depth))
    total = terms[0].astype(F32)
    for term in terms[1:]:
        total = total + term.astype(F32)
    for j in range(2):
        total = total + extra_weight[:, j : j + 1] * extra_out[j : j + 1]
    return total.astype(BF), load_share


def solution(mesh):
    in_specs = (
        P(("dp", "expert"), None),
        P(("dp", "expert"), None),
        P(("dp", "expert"), None),
        P("expert", None, "dp"),
        P("expert", None, "dp"),
        P("expert", "dp", None),
        P("expert", None, "dp"),
        P("expert", None, "dp"),
        P("expert", "dp", None),
    )
    out_specs = (P(("dp", "expert"), None), P())
    return jax.shard_map(
        per_device, mesh=mesh, in_specs=in_specs, out_specs=out_specs, check_vma=False
    )
```

```python
import functools

import jax
import jax.numpy as jnp
from jax import lax
from jax.experimental import pallas as pl
from jax.experimental.pallas import tpu as pltpu
from jax.sharding import PartitionSpec as P

BLOCK = 128
CAP = 3
NY, NZ, NC, NX = 4, 8, 2, 4
SRC = NZ * NC
PIECE = SRC * CAP
META = 128
COLS = 512
STEPS = 4
EXTRA = 2 * NZ
BF = jnp.bfloat16
F32 = jnp.float32
VMEM = 48 * 1024 * 1024


def expert_move(value, dy=0, dz=0, flip=False, xor_y=0):
    pairs = []
    for y in range(NY):
        for z in range(NZ):
            for c in range(NC):
                to_y = (y + dy) % NY ^ xor_y
                to_z = (z + dz) % NZ
                to_c = c ^ 1 if flip else c
                pairs.append(((y * NZ + z) * NC + c, (to_y * NZ + to_z) * NC + to_c))
    return lax.ppermute(value, "expert", pairs)


def dp_move(value, dx=0, xor_x=0):
    return lax.ppermute(value, "dp", [(x, (x + dx) % NX ^ xor_x) for x in range(NX)])


def slot_values(metas, lanes):
    tokens = metas.shape[0]
    found = jnp.zeros((tokens, META), F32)
    for k in range(8):
        found += jnp.where(metas[:, k : k + 1] == lanes, 1.0, 0.0)
    row = lax.broadcasted_iota(jnp.int32, (tokens, tokens), 0)
    col = lax.broadcasted_iota(jnp.int32, (tokens, tokens), 1)
    earlier = jnp.where(((row >> 5) == (col >> 5)) & (col < row), 1.0, 0.0).astype(BF)
    rank = jnp.dot(earlier, found.astype(BF), preferred_element_type=F32)
    return found * (rank + 1.0)


def slot_parts(slots):
    lane = (slots * 1366) >> 16
    rest = slots - lane * PIECE
    return lane, rest >> 4, rest & 15


def gather_kernel(lanes_ref, *refs):
    pieces, near_ref, outs = refs[:SRC], refs[SRC], refs[SRC + 1 : SRC + 7]
    counts_ref, metas_ref = refs[SRC + 7 : SRC + 9]
    tokens, slots = SRC * 32, 8 * PIECE
    depth = near_ref.shape[1]
    metas = jnp.concatenate([p[:, depth : depth + META] for p in pieces], axis=0).astype(F32)
    metas_ref[...] = metas
    values = slot_values(metas, lanes_ref[0:1, :])
    every = lax.broadcasted_iota(jnp.int32, (1, META), 1).astype(F32)
    total = jnp.zeros((tokens, META), F32)
    for k in range(8):
        total += jnp.where(metas[:, k : k + 1] == every, 1.0, 0.0)
    counts_ref[...] = jnp.broadcast_to(jnp.sum(total, axis=0, keepdims=True), (8, META))
    slot_lane, _, _ = slot_parts(lax.broadcasted_iota(jnp.int32, (slots, META), 0))
    spread = jnp.where(
        slot_lane == lax.broadcasted_iota(jnp.int32, (slots, META), 1), 1.0, 0.0
    ).astype(BF)
    picked = lax.dot_general(
        spread, values.astype(BF), (((1,), (1,)), ((), ())), preferred_element_type=F32
    )
    _, rank, source = slot_parts(lax.broadcasted_iota(jnp.int32, (slots, tokens), 0))
    token = lax.broadcasted_iota(jnp.int32, (slots, tokens), 1)
    choose = jnp.where(
        (picked == (rank + 1).astype(F32)) & (source == (token >> 5)), 1.0, 0.0
    ).astype(BF)
    for start in range(0, depth, COLS):
        block = jnp.concatenate([p[:, start : start + COLS] for p in pieces], axis=0)
        rows = jnp.dot(choose, block, preferred_element_type=F32).astype(BF)
        for which in range(2):
            at = which * NY * PIECE
            near_ref[which * PIECE : (which + 1) * PIECE, start : start + COLS] = rows[at : at + PIECE]
            for d in range(1, NY):
                low = at + d * PIECE
                outs[which * 3 + d - 1][:, start : start + COLS] = rows[low : low + PIECE]


def pick_kernel(counts_ref, metas_ref, *refs):
    pieces, rows_ref, hot_ref = refs[:NZ], refs[NZ], refs[NZ + 1]
    tokens = NZ * 32
    depth = rows_ref.shape[1]
    every = lax.broadcasted_iota(jnp.int32, (1, META), 1).astype(F32)
    order = counts_ref[0:1, :] * META + (META - 1.0 - every)
    best = order == jnp.max(order, axis=1, keepdims=True)
    first = jnp.sum(jnp.where(best, every, 0.0), axis=1, keepdims=True)
    order = jnp.where(best, -1.0, order)
    best = order == jnp.max(order, axis=1, keepdims=True)
    second = jnp.sum(jnp.where(best, every, 0.0), axis=1, keepdims=True)
    row = lax.broadcasted_iota(jnp.int32, (8, META), 0)
    hot_ref[...] = jnp.where(row == 0, first, second)
    lanes = jnp.where(every == 0.0, first, jnp.where(every == 1.0, second, -1.0))
    values = slot_values(metas_ref[:tokens, :], lanes)
    slot = lax.broadcasted_iota(jnp.int32, (EXTRA, META), 0)
    spread = jnp.where(
        (slot & 1) == lax.broadcasted_iota(jnp.int32, (EXTRA, META), 1), 1.0, 0.0
    ).astype(BF)
    picked = lax.dot_general(
        spread, values.astype(BF), (((1,), (1,)), ((), ())), preferred_element_type=F32
    )
    slot = lax.broadcasted_iota(jnp.int32, (EXTRA, tokens), 0)
    token = lax.broadcasted_iota(jnp.int32, (EXTRA, tokens), 1)
    choose = jnp.where(
        (picked == CAP + 1.0) & ((slot >> 1) == (token >> 5)), 1.0, 0.0
    ).astype(BF)
    for start in range(0, depth, COLS):
        block = jnp.concatenate([p[:, start : start + COLS] for p in pieces], axis=0)
        rows_ref[:, start : start + COLS] = jnp.dot(
            choose, block, preferred_element_type=F32
        ).astype(BF)


def plan_kernel(lanes_ref, metas_ref, high_ref, low_ref, extra_high_ref, extra_low_ref):
    tokens, slots = SRC * 32, 8 * PIECE
    own = tokens // 2
    lanes = lanes_ref[0:1, :]
    metas = metas_ref[...]
    values = slot_values(metas, lanes).astype(BF)
    high = jnp.zeros((tokens, META), F32)
    low = jnp.zeros((tokens, META), F32)
    for k in range(8):
        match = metas[:, k : k + 1] == lanes
        high += jnp.where(match, metas[:, 8 + k : 9 + k], 0.0)
        low += jnp.where(match, metas[:, 16 + k : 17 + k], 0.0)
    high, low = high.astype(BF), low.astype(BF)
    slot_lane, _, _ = slot_parts(lax.broadcasted_iota(jnp.int32, (META, slots), 1))
    spread = jnp.where(
        slot_lane == lax.broadcasted_iota(jnp.int32, (META, slots), 0), 1.0, 0.0
    ).astype(BF)
    picked = jnp.dot(values, spread, preferred_element_type=F32)
    _, rank, source = slot_parts(lax.broadcasted_iota(jnp.int32, (tokens, slots), 1))
    token = lax.broadcasted_iota(jnp.int32, (tokens, slots), 0)
    there = (picked == (rank + 1).astype(F32)) & (source == (token >> 5))
    high_at = jnp.dot(high, spread, preferred_element_type=F32)
    low_at = jnp.dot(low, spread, preferred_element_type=F32)
    high_ref[...] = jnp.where(there, high_at, 0.0).astype(BF)
    low_ref[...] = jnp.where(there, low_at, 0.0).astype(BF)
    slot = lax.broadcasted_iota(jnp.int32, (META, META), 1)
    from_lane = lax.broadcasted_iota(jnp.int32, (META, META), 0)
    spread = jnp.where((from_lane == 8 + (slot & 1)) & (slot < EXTRA), 1.0, 0.0).astype(BF)
    picked = jnp.dot(values[:own], spread, preferred_element_type=F32)
    slot = lax.broadcasted_iota(jnp.int32, (own, META), 1)
    token = lax.broadcasted_iota(jnp.int32, (own, META), 0)
    there = (picked == CAP + 1.0) & ((slot >> 1) == (token >> 5))
    high_at = jnp.dot(high[:own], spread, preferred_element_type=F32)
    low_at = jnp.dot(low[:own], spread, preferred_element_type=F32)
    extra_high_ref[...] = jnp.where(there, high_at, 0.0).astype(BF)
    extra_low_ref[...] = jnp.where(there, low_at, 0.0).astype(BF)


def scatter_kernel(high_ref, low_ref, extra_high_ref, extra_low_ref, extra_ref, *refs):
    rows_in, (own_ref, other_ref) = refs[:8], refs[8:]
    half, depth = own_ref.shape
    high, low = high_ref[...], low_ref[...]
    extra_high, extra_low = extra_high_ref[...], extra_low_ref[...]
    for start in range(0, depth, COLS):
        block = jnp.concatenate([r[:, start : start + COLS] for r in rows_in], axis=0)
        sums = jnp.dot(high, block, preferred_element_type=F32)
        sums += jnp.dot(low, block, preferred_element_type=F32)
        extra = jnp.concatenate(
            [extra_ref[:, start : start + COLS], jnp.zeros((META - EXTRA, COLS), BF)], axis=0
        )
        more = jnp.dot(extra_high, extra, preferred_element_type=F32)
        more += jnp.dot(extra_low, extra, preferred_element_type=F32)
        own_ref[:, start : start + COLS] = (sums[:half] + more).astype(BF)
        other_ref[:, start : start + COLS] = sums[half:].astype(BF)


def merge_kernel(*refs):
    ins, out = refs[:3], refs[-1]
    for j in range(3):
        out[j * PIECE : (j + 1) * PIECE, :] = ins[j][...]


def whole(count):
    return [pl.BlockSpec(memory_space=pltpu.VMEM)] * count


def anywhere(count):
    return [pl.BlockSpec(memory_space=pl.ANY)] * count


def rough(flops, size):
    return pl.CostEstimate(flops=flops, bytes_accessed=size, transcendentals=0)


PARAMS = pltpu.CompilerParams(vmem_limit_bytes=VMEM)


def gather_rows(lanes, pieces, depth):
    shapes = [jax.ShapeDtypeStruct((2 * PIECE, depth), BF)]
    shapes += [jax.ShapeDtypeStruct((PIECE, depth), BF)] * 6
    shapes += [jax.ShapeDtypeStruct((8, META), F32), jax.ShapeDtypeStruct((SRC * 32, META), F32)]
    return pl.pallas_call(
        gather_kernel,
        out_shape=shapes,
        in_specs=whole(1 + SRC),
        out_specs=whole(9),
        compiler_params=PARAMS,
        cost_estimate=rough(2 * 384 * 512 * depth, 7 << 20),
        name="gather_rows",
    )(lanes, *pieces)


def pick_extra(counts, metas, pieces, depth):
    return pl.pallas_call(
        pick_kernel,
        out_shape=[
            jax.ShapeDtypeStruct((EXTRA, depth), BF),
            jax.ShapeDtypeStruct((8, META), F32),
        ],
        in_specs=whole(2 + NZ),
        out_specs=whole(2),
        compiler_params=PARAMS,
        cost_estimate=rough(2 * 16 * 256 * depth, 2 << 20),
        name="pick_extra",
    )(counts, metas, *pieces)


def plan_scatter(lanes, metas):
    shapes = [jax.ShapeDtypeStruct((SRC * 32, 8 * PIECE), BF)] * 2
    shapes += [jax.ShapeDtypeStruct((SRC * 16, META), BF)] * 2
    return pl.pallas_call(
        plan_kernel,
        out_shape=shapes,
        in_specs=whole(2),
        out_specs=whole(4),
        compiler_params=PARAMS,
        cost_estimate=rough(512 * 512 * 1024, 1 << 20),
        name="plan_scatter",
    )(lanes, metas)


def scatter_rows(plan, extra, rows, depth):
    return pl.pallas_call(
        scatter_kernel,
        out_shape=[jax.ShapeDtypeStruct((SRC * 16, depth), BF)] * 2,
        in_specs=whole(5 + 8),
        out_specs=whole(2),
        compiler_params=PARAMS,
        cost_estimate=rough(4 * 384 * 512 * depth, 10 << 20),
        name="scatter_rows",
    )(*plan, extra, *rows)


def merge(pieces, after):
    depth = pieces[0].shape[1]
    return pl.pallas_call(
        merge_kernel,
        out_shape=jax.ShapeDtypeStruct((3 * PIECE, depth), BF),
        in_specs=whole(3) + anywhere(len(after)),
        out_specs=whole(1)[0],
        compiler_params=PARAMS,
        cost_estimate=rough(0, 2 << 20),
        name="merge",
    )(*pieces, *after)


def deq_kernel(w_ref, s_ref, out_ref):
    rows, cols = w_ref.shape[1:]
    scales = s_ref[0]
    for r in range(rows // BLOCK):
        for c in range(cols // BLOCK):
            at = (0, slice(r * BLOCK, (r + 1) * BLOCK), slice(c * BLOCK, (c + 1) * BLOCK))
            out_ref[at] = (w_ref[at].astype(F32) * scales[r : r + 1, c : c + 1]).astype(BF)


def dequantize(weight, scale):
    count, rows, cols = weight.shape

    def block(array):
        return pl.BlockSpec((1,) + array.shape[1:], lambda i: (i, 0, 0))

    return pl.pallas_call(
        deq_kernel,
        grid=(count,),
        out_shape=jax.ShapeDtypeStruct(weight.shape, BF),
        in_specs=[block(weight), block(scale)],
        out_specs=block(weight),
        compiler_params=PARAMS,
        cost_estimate=rough(count * rows * cols, 4 * count * rows * cols),
        name="dequantize",
    )(weight, scale)


def silu(value):
    return value * (1.0 / (1.0 + jnp.exp(-value)))


def ffn_kernel(in_count, out_rows, skip, *refs):
    xs, (gate_w, up_w, down_w) = refs[:in_count], refs[in_count : in_count + 3]
    refs = refs[in_count + 3 + skip :]
    outs, (gate_acc, up_acc, hidden) = refs[: len(out_rows)], refs[len(out_rows) :]
    step = pl.program_id(0)

    @pl.when(step < STEPS)
    def _():
        x = jnp.concatenate([r[...] for r in xs], axis=0)
        gate = jnp.dot(x, gate_w[0], preferred_element_type=F32)
        up = jnp.dot(x, up_w[0], preferred_element_type=F32)

        @pl.when(step == 0)
        def _():
            gate_acc[...] = gate
            up_acc[...] = up

        @pl.when(step > 0)
        def _():
            gate_acc[...] += gate
            up_acc[...] += up

    @pl.when(step >= STEPS)
    def _():
        @pl.when(step == STEPS)
        def _():
            hidden[...] = (silu(gate_acc[...]) * up_acc[...]).astype(BF)

        result = jnp.dot(hidden[...], down_w[0], preferred_element_type=F32).astype(BF)
        at = 0
        for ref, count in zip(outs, out_rows):
            ref[...] = result[at : at + count]
            at += count


def early(i):
    return jnp.minimum(i, STEPS - 1)


def late(i):
    return jnp.maximum(i - STEPS, 0)


def ffn(xs, out_rows, which, weights, after):
    gate_w, up_w, down_w = weights
    depth, units = gate_w.shape[1:]
    wide = depth // STEPS
    total = sum(rows for _, rows, _ in xs)
    in_specs = [
        pl.BlockSpec((rows, wide), lambda i, place=place: (place, early(i))) for _, rows, place in xs
    ]
    in_specs += [pl.BlockSpec((1, wide, units), lambda i: (which, early(i), 0))] * 2
    in_specs += [pl.BlockSpec((1, units, wide), lambda i: (which, 0, late(i)))]
    return pl.pallas_call(
        functools.partial(ffn_kernel, len(xs), out_rows, len(after)),
        grid=(2 * STEPS,),
        out_shape=[jax.ShapeDtypeStruct((r, depth), BF) for r in out_rows],
        in_specs=in_specs + anywhere(len(after)),
        out_specs=[pl.BlockSpec((r, wide), lambda i: (0, late(i))) for r in out_rows],
        scratch_shapes=[
            pltpu.VMEM((total, units), F32),
            pltpu.VMEM((total, units), F32),
            pltpu.VMEM((total, units), BF),
        ],
        compiler_params=PARAMS,
        cost_estimate=rough(6 * total * units * depth, 4 * total * depth + 6 * units * depth),
        name="ffn",
    )(*[x for x, _, _ in xs], gate_w, up_w, down_w, *after)


def extra_kernel(skip, place_ref, own_in, other_in, gate_w, up_w, down_a, down_b, *refs):
    own_out, other_out, gate_acc, up_acc, hidden = refs[skip:]
    step = pl.program_id(0)
    units = gate_w.shape[2]

    @pl.when(step < 2 * STEPS)
    def _():
        x = jnp.concatenate([own_in[...], other_in[...]], axis=0)
        gate = jnp.dot(x, gate_w[0], preferred_element_type=F32)
        up = jnp.dot(x, up_w[0], preferred_element_type=F32)
        opening = (step == 0) | (step == STEPS)

        @pl.when(opening)
        def _():
            gate_acc[...] = gate
            up_acc[...] = up

        @pl.when(jnp.logical_not(opening))
        def _():
            gate_acc[...] += gate
            up_acc[...] += up

    for j in range(2):

        @pl.when(step == (j + 1) * STEPS - 1)
        def _(j=j):
            value = silu(gate_acc[...]) * up_acc[...]
            row = lax.broadcasted_iota(jnp.int32, value.shape, 0)
            keep = ((row & 1) == j) & (place_ref[2 + j] == 1)
            hidden[:, j * units : (j + 1) * units] = jnp.where(keep, value, 0.0).astype(BF)

    @pl.when(step >= 2 * STEPS)
    def _():
        down = jnp.concatenate([down_a[0], down_b[0]], axis=0)
        result = jnp.dot(hidden[...], down, preferred_element_type=F32).astype(BF)
        half = own_out.shape[0]
        own_out[...] = result[:half]
        other_out[...] = result[half:]


def extra_ffn(places, own, other, weights, after):
    gate_w, up_w, down_w = weights
    depth, units = gate_w.shape[1:]
    wide = depth // STEPS
    half = own.shape[0]

    def first(i):
        return jnp.where(i < 2 * STEPS, i & (STEPS - 1), STEPS - 1)

    def last(i):
        return jnp.maximum(i - 2 * STEPS, 0)

    def turn(i):
        return jnp.where(i < STEPS, 0, 1)

    rows_in = pl.BlockSpec((half, wide), lambda i, s: (0, first(i)))
    gate_in = pl.BlockSpec((1, wide, units), lambda i, s: (s[turn(i)], first(i), 0))
    rows_out = pl.BlockSpec((half, wide), lambda i, s: (0, last(i)))
    spec = pltpu.PrefetchScalarGridSpec(
        num_scalar_prefetch=1,
        grid=(3 * STEPS,),
        in_specs=[rows_in, rows_in, gate_in, gate_in]
        + [pl.BlockSpec((1, units, wide), lambda i, s, j=j: (s[j], 0, last(i))) for j in range(2)]
        + anywhere(len(after)),
        out_specs=[rows_out, rows_out],
        scratch_shapes=[
            pltpu.VMEM((2 * half, units), F32),
            pltpu.VMEM((2 * half, units), F32),
            pltpu.VMEM((2 * half, 2 * units), BF),
        ],
    )
    return pl.pallas_call(
        functools.partial(extra_kernel, len(after)),
        grid_spec=spec,
        out_shape=[jax.ShapeDtypeStruct((half, depth), BF)] * 2,
        compiler_params=PARAMS,
        cost_estimate=rough(20 * half * units * depth, 32 << 20),
        name="extra_ffn",
    )(places, own, other, gate_w, up_w, down_w, down_w, *after)


def add(*values):
    total = values[0].astype(F32)
    for value in values[1:]:
        total = total + value.astype(F32)
    return total.astype(BF)


def gather_line(own):
    pieces = [own] + [None] * (NZ - 1)
    up = down = own
    for step in range(1, NZ // 2 + 1):
        up = expert_move(up, dz=-1)
        pieces[step] = up
        if step < NZ // 2:
            down = expert_move(down, dz=1)
            pieces[NZ - step] = down
    return pieces + [expert_move(piece, flip=True) for piece in pieces]


def scatter_line(own, other):
    arrived = expert_move(other, flip=True)

    def term(dz):
        return own[dz * 32 : dz * 32 + 32], arrived[dz * 32 : dz * 32 + 32]

    up = add(*term(NZ // 2))
    for dz in range(NZ // 2 - 1, 0, -1):
        up = add(expert_move(up, dz=1), *term(dz))
    down = add(*term(NZ // 2 + 1))
    for dz in range(NZ // 2 + 2, NZ):
        down = add(expert_move(down, dz=-1), *term(dz))
    return [expert_move(up, dz=1), expert_move(down, dz=-1), *term(0)]


def spread_dp(block, cut):
    left = dp_move(block, 1)
    right = dp_move(block, -1)
    return [block, left, right, dp_move(left[:cut], 1), dp_move(right[cut:], -1)]


def sum_dp(parts):
    left_a, left_b, right_a, right_b, far_a, far_b, own = parts
    from_a = dp_move(far_a, -1)
    from_b = dp_move(far_b, 1)
    got_left_b = dp_move(left_b, -1)
    got_right_a = dp_move(right_a, 1)
    got_left_a = dp_move(add(left_a, from_a), -1)
    got_right_b = dp_move(add(right_b, from_b), 1)
    half = own.shape[0] // 2
    result = []
    for j in range(NY):
        low = j * PIECE
        if low < half:
            terms = (got_left_a[low : low + PIECE], got_right_a[low : low + PIECE])
        else:
            at = low - half
            terms = (got_left_b[at : at + PIECE], got_right_b[at : at + PIECE])
        result.append(add(own[low : low + PIECE], *terms))
    return result


def per_device(
    tokens,
    routes,
    route_weight,
    gate_weight,
    up_weight,
    down_weight,
    gate_scale,
    up_scale,
    down_scale,
):
    rows, depth = tokens.shape
    top = routes.shape[1]
    experts = gate_weight.shape[0] * NY * NZ * NC
    all_rows = rows * NX * NY * NZ * NC
    place = lax.axis_index("expert")
    y, line = place // (NZ * NC), place % (NZ * NC)

    high = lax.reduce_precision(route_weight, 8, 7)
    low = lax.reduce_precision(route_weight - high, 8, 7)
    meta = jnp.concatenate(
        [routes.astype(BF), high.astype(BF), low.astype(BF), jnp.zeros((rows, META - 3 * top), BF)],
        axis=1,
    )
    pieces = gather_line(jnp.concatenate([tokens, meta], axis=1))
    weights = (
        dequantize(gate_weight, gate_scale),
        dequantize(up_weight, up_scale),
        dequantize(down_weight, down_scale),
    )

    lane = jnp.arange(META, dtype=jnp.int32)
    lane_expert = ((((y + lane % NY) % NY) * (NZ * NC) + line) * 2 + lane // NY).astype(F32)
    lanes = jnp.broadcast_to(jnp.where(lane < 8, lane_expert, -1.0)[None], (8, META))
    near, *blocks, counts, metas = gather_rows(lanes, pieces, depth)
    near = spread_dp(near, PIECE)

    moved = [[expert_move(blocks[w * 3 + d - 1], dy=d) for d in range(1, NY)] for w in range(2)]
    counts = sum([expert_move(counts, dy=d) for d in range(1, NY)], counts)
    counts = sum([dp_move(counts, d) for d in range(1, NX)], counts)
    load_share = counts[0, :experts] * (experts / (all_rows * top))

    cut = 2 * PIECE - 32
    parts = []
    after = []
    half = NY * PIECE // 2
    spreads = []
    for which in range(2):
        spreads.append(spread_dp(merge(moved[which], after), cut))
        after = [spreads[0][1], spreads[0][2]]
    for which in range(2):
        far_spread = spreads[which]
        xs = [
            (near[1], PIECE, which),
            (far_spread[1], 3 * PIECE, 0),
            (near[2], PIECE, which),
            (far_spread[2], 3 * PIECE, 0),
            (near[3 + which], PIECE, 0),
            (far_spread[3], cut, 0),
            (far_spread[4], 3 * PIECE - cut, 0),
            (near[0], PIECE, which),
            (far_spread[0], 3 * PIECE, 0),
        ]
        parts.append(ffn(xs, [half] * 6 + [2 * half], which, weights, []))

    extra, hot = pick_extra(counts, metas, pieces[:NZ], depth)
    hot_id = hot[0:2, 0].astype(jnp.int32)
    places = jnp.concatenate([hot_id & 1, ((hot_id >> 1) == place).astype(jnp.int32)])
    spare = jnp.where(lane == 8, hot[0:1], jnp.where(lane == 9, hot[1:2], lanes))
    plan = plan_scatter(spare, metas)
    extra = jnp.concatenate([extra] + [dp_move(extra, d) for d in range(1, NX)], axis=0)
    extra = jnp.concatenate([extra] + [expert_move(extra, dy=d) for d in range(1, NY)], axis=0)
    own, other = extra_ffn(
        places, extra, expert_move(extra, flip=True), weights, [parts[1][-1], plan[0]]
    )
    extra = add(own, expert_move(other, flip=True))
    size = NX * EXTRA
    extra = add(
        extra[:size],
        *[expert_move(extra[d * size : (d + 1) * size], dy=-d) for d in range(1, NY)],
    )
    extra = add(
        extra[:EXTRA], *[dp_move(extra[d * EXTRA : (d + 1) * EXTRA], -d) for d in range(1, NX)]
    )

    returned = []
    for which in range(2):
        group = sum_dp(parts[which])
        returned += [group[0]] + [expert_move(group[d], dy=-d) for d in range(1, NY)]
    terms = scatter_line(*scatter_rows(plan, extra, returned, depth))
    return add(*terms), load_share


def solution(mesh):
    in_specs = (
        P(("dp", "expert"), None),
        P(("dp", "expert"), None),
        P(("dp", "expert"), None),
        P("expert", None, "dp"),
        P("expert", None, "dp"),
        P("expert", "dp", None),
        P("expert", None, "dp"),
        P("expert", None, "dp"),
        P("expert", "dp", None),
    )
    out_specs = (P(("dp", "expert"), None), P())
    return jax.shard_map(
        per_device, mesh=mesh, in_specs=in_specs, out_specs=out_specs, check_vma=False
    )
```

```python
import functools

import jax
import jax.numpy as jnp
from jax import lax
from jax.experimental import pallas as pl
from jax.experimental.pallas import tpu as pltpu
from jax.sharding import PartitionSpec as P

BLOCK = 128
CAP = 3
NY, NZ, NC, NX = 4, 8, 2, 4
SRC = NZ * NC
PIECE = SRC * CAP
META = 128
COLS = 512
STEPS = 4
EXTRA = 2 * NZ
BF = jnp.bfloat16
F32 = jnp.float32
VMEM = 24 * 1024 * 1024


def expert_move(value, dy=0, dz=0, flip=False, xor_y=0):
    pairs = []
    for y in range(NY):
        for z in range(NZ):
            for c in range(NC):
                to_y = (y + dy) % NY ^ xor_y
                to_z = (z + dz) % NZ
                to_c = c ^ 1 if flip else c
                pairs.append(((y * NZ + z) * NC + c, (to_y * NZ + to_z) * NC + to_c))
    return lax.ppermute(value, "expert", pairs)


def dp_move(value, dx=0, xor_x=0):
    return lax.ppermute(value, "dp", [(x, (x + dx) % NX ^ xor_x) for x in range(NX)])


def slot_values(metas, lanes):
    tokens = metas.shape[0]
    found = jnp.zeros((tokens, META), F32)
    for k in range(8):
        found += jnp.where(metas[:, k : k + 1] == lanes, 1.0, 0.0)
    row = lax.broadcasted_iota(jnp.int32, (tokens, tokens), 0)
    col = lax.broadcasted_iota(jnp.int32, (tokens, tokens), 1)
    earlier = jnp.where(((row >> 5) == (col >> 5)) & (col < row), 1.0, 0.0).astype(BF)
    rank = jnp.dot(earlier, found.astype(BF), preferred_element_type=F32)
    return found * (rank + 1.0)


def slot_parts(slots):
    lane = (slots * 1366) >> 16
    rest = slots - lane * PIECE
    return lane, rest >> 4, rest & 15


def gather_kernel(lanes_ref, *refs):
    pieces, near_ref, outs = refs[:SRC], refs[SRC], refs[SRC + 1 : SRC + 7]
    line_ref, metas_ref = refs[SRC + 7 : SRC + 9]
    tokens, slots = SRC * 32, 8 * PIECE
    depth = near_ref.shape[1]
    metas = jnp.concatenate([p[:, depth : depth + META] for p in pieces], axis=0).astype(F32)
    metas_ref[...] = metas
    values = slot_values(metas, lanes_ref[0:1, :])
    slot_lane, _, _ = slot_parts(lax.broadcasted_iota(jnp.int32, (slots, META), 0))
    spread = jnp.where(
        slot_lane == lax.broadcasted_iota(jnp.int32, (slots, META), 1), 1.0, 0.0
    ).astype(BF)
    picked = lax.dot_general(
        spread, values.astype(BF), (((1,), (1,)), ((), ())), preferred_element_type=F32
    )
    _, rank, source = slot_parts(lax.broadcasted_iota(jnp.int32, (slots, tokens), 0))
    token = lax.broadcasted_iota(jnp.int32, (slots, tokens), 1)
    choose = jnp.where(
        (picked == (rank + 1).astype(F32)) & (source == (token >> 5)), 1.0, 0.0
    ).astype(BF)
    for start in range(0, depth, COLS):
        block = jnp.concatenate([p[:, start : start + COLS] for p in pieces], axis=0)
        line_ref[:, start : start + COLS] = block[: tokens // 2]
        rows = jnp.dot(choose, block, preferred_element_type=F32).astype(BF)
        for which in range(2):
            at = which * NY * PIECE
            near_ref[which * PIECE : (which + 1) * PIECE, start : start + COLS] = rows[at : at + PIECE]
            for d in range(1, NY):
                low = at + d * PIECE
                outs[which * 3 + d - 1][:, start : start + COLS] = rows[low : low + PIECE]


def count_kernel(metas_ref, *refs):
    counts_ref = refs[-1]
    metas = metas_ref[...]
    every = lax.broadcasted_iota(jnp.int32, (1, META), 1).astype(F32)
    total = jnp.zeros(metas.shape, F32)
    for k in range(8):
        total += jnp.where(metas[:, k : k + 1] == every, 1.0, 0.0)
    counts_ref[...] = jnp.broadcast_to(jnp.sum(total, axis=0, keepdims=True), (8, META))


def relay_kernel(in_ref, after_ref, out_ref):
    out_ref[...] = in_ref[...]


def pick_kernel(counts_ref, metas_ref, line_ref, rows_ref, hot_ref):
    tokens = NZ * 32
    depth = rows_ref.shape[1]
    every = lax.broadcasted_iota(jnp.int32, (1, META), 1).astype(F32)
    order = counts_ref[0:1, :] * META + (META - 1.0 - every)
    best = order == jnp.max(order, axis=1, keepdims=True)
    first = jnp.sum(jnp.where(best, every, 0.0), axis=1, keepdims=True)
    order = jnp.where(best, -1.0, order)
    best = order == jnp.max(order, axis=1, keepdims=True)
    second = jnp.sum(jnp.where(best, every, 0.0), axis=1, keepdims=True)
    row = lax.broadcasted_iota(jnp.int32, (8, META), 0)
    hot_ref[...] = jnp.where(row == 0, first, second)
    lanes = jnp.where(every == 0.0, first, jnp.where(every == 1.0, second, -1.0))
    values = slot_values(metas_ref[:tokens, :], lanes)
    slot = lax.broadcasted_iota(jnp.int32, (EXTRA, META), 0)
    spread = jnp.where(
        (slot & 1) == lax.broadcasted_iota(jnp.int32, (EXTRA, META), 1), 1.0, 0.0
    ).astype(BF)
    picked = lax.dot_general(
        spread, values.astype(BF), (((1,), (1,)), ((), ())), preferred_element_type=F32
    )
    slot = lax.broadcasted_iota(jnp.int32, (EXTRA, tokens), 0)
    token = lax.broadcasted_iota(jnp.int32, (EXTRA, tokens), 1)
    choose = jnp.where(
        (picked == CAP + 1.0) & ((slot >> 1) == (token >> 5)), 1.0, 0.0
    ).astype(BF)
    for start in range(0, depth, COLS):
        rows_ref[:, start : start + COLS] = jnp.dot(
            choose, line_ref[:, start : start + COLS], preferred_element_type=F32
        ).astype(BF)


def plan_kernel(lanes_ref, metas_ref, high_ref, low_ref, extra_high_ref, extra_low_ref):
    tokens, slots = SRC * 32, 8 * PIECE
    own = tokens // 2
    lanes = lanes_ref[0:1, :]
    metas = metas_ref[...]
    values = slot_values(metas, lanes).astype(BF)
    high = jnp.zeros((tokens, META), F32)
    low = jnp.zeros((tokens, META), F32)
    for k in range(8):
        match = metas[:, k : k + 1] == lanes
        high += jnp.where(match, metas[:, 8 + k : 9 + k], 0.0)
        low += jnp.where(match, metas[:, 16 + k : 17 + k], 0.0)
    high, low = high.astype(BF), low.astype(BF)
    slot_lane, _, _ = slot_parts(lax.broadcasted_iota(jnp.int32, (META, slots), 1))
    spread = jnp.where(
        slot_lane == lax.broadcasted_iota(jnp.int32, (META, slots), 0), 1.0, 0.0
    ).astype(BF)
    picked = jnp.dot(values, spread, preferred_element_type=F32)
    _, rank, source = slot_parts(lax.broadcasted_iota(jnp.int32, (tokens, slots), 1))
    token = lax.broadcasted_iota(jnp.int32, (tokens, slots), 0)
    there = (picked == (rank + 1).astype(F32)) & (source == (token >> 5))
    high_at = jnp.dot(high, spread, preferred_element_type=F32)
    low_at = jnp.dot(low, spread, preferred_element_type=F32)
    high_ref[...] = jnp.where(there, high_at, 0.0).astype(BF)
    low_ref[...] = jnp.where(there, low_at, 0.0).astype(BF)
    slot = lax.broadcasted_iota(jnp.int32, (META, META), 1)
    from_lane = lax.broadcasted_iota(jnp.int32, (META, META), 0)
    spread = jnp.where((from_lane == 8 + (slot & 1)) & (slot < EXTRA), 1.0, 0.0).astype(BF)
    picked = jnp.dot(values[:own], spread, preferred_element_type=F32)
    slot = lax.broadcasted_iota(jnp.int32, (own, META), 1)
    token = lax.broadcasted_iota(jnp.int32, (own, META), 0)
    there = (picked == CAP + 1.0) & ((slot >> 1) == (token >> 5))
    high_at = jnp.dot(high[:own], spread, preferred_element_type=F32)
    low_at = jnp.dot(low[:own], spread, preferred_element_type=F32)
    extra_high_ref[...] = jnp.where(there, high_at, 0.0).astype(BF)
    extra_low_ref[...] = jnp.where(there, low_at, 0.0).astype(BF)


def scatter_kernel(high_ref, low_ref, extra_high_ref, extra_low_ref, extra_ref, *refs):
    rows_in, (own_ref, other_ref) = refs[:8], refs[8:]
    half, depth = own_ref.shape
    high, low = high_ref[...], low_ref[...]
    extra_high, extra_low = extra_high_ref[...], extra_low_ref[...]
    for start in range(0, depth, COLS):
        block = jnp.concatenate([r[:, start : start + COLS] for r in rows_in], axis=0)
        sums = jnp.dot(high, block, preferred_element_type=F32)
        sums += jnp.dot(low, block, preferred_element_type=F32)
        extra = jnp.concatenate(
            [extra_ref[:, start : start + COLS], jnp.zeros((META - EXTRA, COLS), BF)], axis=0
        )
        more = jnp.dot(extra_high, extra, preferred_element_type=F32)
        more += jnp.dot(extra_low, extra, preferred_element_type=F32)
        own_ref[:, start : start + COLS] = (sums[:half] + more).astype(BF)
        other_ref[:, start : start + COLS] = sums[half:].astype(BF)


def merge_kernel(*refs):
    ins, out = refs[:3], refs[-1]
    for j in range(3):
        out[j * PIECE : (j + 1) * PIECE, :] = ins[j][...]


def whole(count):
    return [pl.BlockSpec(memory_space=pltpu.VMEM)] * count


def anywhere(count):
    return [pl.BlockSpec(memory_space=pl.ANY)] * count


def rough(flops, size):
    return pl.CostEstimate(flops=flops, bytes_accessed=size, transcendentals=0)


PARAMS = pltpu.CompilerParams(vmem_limit_bytes=VMEM)


def gather_rows(lanes, pieces, depth):
    shapes = [jax.ShapeDtypeStruct((2 * PIECE, depth), BF)]
    shapes += [jax.ShapeDtypeStruct((PIECE, depth), BF)] * 6
    shapes += [
        jax.ShapeDtypeStruct((SRC * 16, depth), BF),
        jax.ShapeDtypeStruct((SRC * 32, META), F32),
    ]
    return pl.pallas_call(
        gather_kernel,
        out_shape=shapes,
        in_specs=whole(1 + SRC),
        out_specs=whole(9),
        compiler_params=PARAMS,
        cost_estimate=rough(2 * 384 * 512 * depth, 7 << 20),
        name="gather_rows",
    )(lanes, *pieces)


def count_rows(metas, after):
    return pl.pallas_call(
        count_kernel,
        out_shape=jax.ShapeDtypeStruct((8, META), F32),
        in_specs=whole(1) + anywhere(len(after)),
        out_specs=whole(1)[0],
        compiler_params=PARAMS,
        cost_estimate=rough(8 * 512 * 128, 1 << 18),
        name="count_rows",
    )(metas, *after)


def relay(rows, after):
    return pl.pallas_call(
        relay_kernel,
        out_shape=jax.ShapeDtypeStruct(rows.shape, rows.dtype),
        in_specs=whole(1) + anywhere(1),
        out_specs=whole(1)[0],
        compiler_params=PARAMS,
        cost_estimate=rough(0, 1 << 19),
        name="relay",
    )(rows, after)


def pick_extra(counts, metas, line):
    depth = line.shape[1]
    return pl.pallas_call(
        pick_kernel,
        out_shape=[
            jax.ShapeDtypeStruct((EXTRA, depth), BF),
            jax.ShapeDtypeStruct((8, META), F32),
        ],
        in_specs=whole(3),
        out_specs=whole(2),
        compiler_params=PARAMS,
        cost_estimate=rough(2 * 16 * 256 * depth, 2 << 20),
        name="pick_extra",
    )(counts, metas, line)


def plan_scatter(lanes, metas):
    shapes = [jax.ShapeDtypeStruct((SRC * 32, 8 * PIECE), BF)] * 2
    shapes += [jax.ShapeDtypeStruct((SRC * 16, META), BF)] * 2
    return pl.pallas_call(
        plan_kernel,
        out_shape=shapes,
        in_specs=whole(2),
        out_specs=whole(4),
        compiler_params=PARAMS,
        cost_estimate=rough(512 * 512 * 1024, 1 << 20),
        name="plan_scatter",
    )(lanes, metas)


def scatter_rows(plan, extra, rows, depth):
    return pl.pallas_call(
        scatter_kernel,
        out_shape=[jax.ShapeDtypeStruct((SRC * 16, depth), BF)] * 2,
        in_specs=whole(5 + 8),
        out_specs=whole(2),
        compiler_params=PARAMS,
        cost_estimate=rough(4 * 384 * 512 * depth, 10 << 20),
        name="scatter_rows",
    )(*plan, extra, *rows)


def merge(pieces, after):
    depth = pieces[0].shape[1]
    return pl.pallas_call(
        merge_kernel,
        out_shape=jax.ShapeDtypeStruct((3 * PIECE, depth), BF),
        in_specs=whole(3) + anywhere(len(after)),
        out_specs=whole(1)[0],
        compiler_params=PARAMS,
        cost_estimate=rough(0, 2 << 20),
        name="merge",
    )(*pieces, *after)


def deq_kernel(w_ref, s_ref, out_ref):
    rows, cols = w_ref.shape[1:]
    scales = s_ref[0]
    for r in range(rows // BLOCK):
        for c in range(cols // BLOCK):
            at = (0, slice(r * BLOCK, (r + 1) * BLOCK), slice(c * BLOCK, (c + 1) * BLOCK))
            out_ref[at] = (w_ref[at].astype(F32) * scales[r : r + 1, c : c + 1]).astype(BF)


def dequantize(weight, scale):
    count, rows, cols = weight.shape

    def block(array):
        return pl.BlockSpec((1,) + array.shape[1:], lambda i: (i, 0, 0))

    return pl.pallas_call(
        deq_kernel,
        grid=(count,),
        out_shape=jax.ShapeDtypeStruct(weight.shape, BF),
        in_specs=[block(weight), block(scale)],
        out_specs=block(weight),
        compiler_params=PARAMS,
        cost_estimate=rough(count * rows * cols, 4 * count * rows * cols),
        name="dequantize",
    )(weight, scale)


def silu(value):
    return value * (1.0 / (1.0 + jnp.exp(-value)))


def ffn_kernel(in_count, out_rows, skip, *refs):
    xs, (gate_w, up_w, down_w) = refs[:in_count], refs[in_count : in_count + 3]
    refs = refs[in_count + 3 + skip :]
    outs, (gate_acc, up_acc, hidden) = refs[: len(out_rows)], refs[len(out_rows) :]
    step = pl.program_id(0)

    @pl.when(step < STEPS)
    def _():
        x = jnp.concatenate([r[...] for r in xs], axis=0)
        gate = jnp.dot(x, gate_w[0], preferred_element_type=F32)
        up = jnp.dot(x, up_w[0], preferred_element_type=F32)

        @pl.when(step == 0)
        def _():
            gate_acc[...] = gate
            up_acc[...] = up

        @pl.when(step > 0)
        def _():
            gate_acc[...] += gate
            up_acc[...] += up

    @pl.when(step >= STEPS)
    def _():
        @pl.when(step == STEPS)
        def _():
            hidden[...] = (silu(gate_acc[...]) * up_acc[...]).astype(BF)

        result = jnp.dot(hidden[...], down_w[0], preferred_element_type=F32).astype(BF)
        at = 0
        for ref, count in zip(outs, out_rows):
            ref[...] = result[at : at + count]
            at += count


def early(i):
    return jnp.minimum(i, STEPS - 1)


def late(i):
    return jnp.maximum(i - STEPS, 0)


def ffn(xs, out_rows, which, weights, after):
    gate_w, up_w, down_w = weights
    depth, units = gate_w.shape[1:]
    wide = depth // STEPS
    total = sum(rows for _, rows, _ in xs)
    in_specs = [
        pl.BlockSpec((rows, wide), lambda i, place=place: (place, early(i))) for _, rows, place in xs
    ]
    in_specs += [pl.BlockSpec((1, wide, units), lambda i: (which, early(i), 0))] * 2
    in_specs += [pl.BlockSpec((1, units, wide), lambda i: (which, 0, late(i)))]
    return pl.pallas_call(
        functools.partial(ffn_kernel, len(xs), out_rows, len(after)),
        grid=(2 * STEPS,),
        out_shape=[jax.ShapeDtypeStruct((r, depth), BF) for r in out_rows],
        in_specs=in_specs + anywhere(len(after)),
        out_specs=[pl.BlockSpec((r, wide), lambda i: (0, late(i))) for r in out_rows],
        scratch_shapes=[
            pltpu.VMEM((total, units), F32),
            pltpu.VMEM((total, units), F32),
            pltpu.VMEM((total, units), BF),
        ],
        compiler_params=PARAMS,
        cost_estimate=rough(6 * total * units * depth, 4 * total * depth + 6 * units * depth),
        name="ffn",
    )(*[x for x, _, _ in xs], gate_w, up_w, down_w, *after)


def extra_kernel(skip, place_ref, own_in, other_in, gate_w, up_w, down_a, down_b, *refs):
    own_out, other_out, gate_acc, up_acc, hidden = refs[skip:]
    step = pl.program_id(0)
    units = gate_w.shape[2]

    @pl.when(step < 2 * STEPS)
    def _():
        x = jnp.concatenate([own_in[...], other_in[...]], axis=0)
        gate = jnp.dot(x, gate_w[0], preferred_element_type=F32)
        up = jnp.dot(x, up_w[0], preferred_element_type=F32)
        opening = (step == 0) | (step == STEPS)

        @pl.when(opening)
        def _():
            gate_acc[...] = gate
            up_acc[...] = up

        @pl.when(jnp.logical_not(opening))
        def _():
            gate_acc[...] += gate
            up_acc[...] += up

    for j in range(2):

        @pl.when(step == (j + 1) * STEPS - 1)
        def _(j=j):
            value = silu(gate_acc[...]) * up_acc[...]
            row = lax.broadcasted_iota(jnp.int32, value.shape, 0)
            keep = ((row & 1) == j) & (place_ref[2 + j] == 1)
            hidden[:, j * units : (j + 1) * units] = jnp.where(keep, value, 0.0).astype(BF)

    @pl.when(step >= 2 * STEPS)
    def _():
        down = jnp.concatenate([down_a[0], down_b[0]], axis=0)
        result = jnp.dot(hidden[...], down, preferred_element_type=F32).astype(BF)
        half = own_out.shape[0]
        own_out[...] = result[:half]
        other_out[...] = result[half:]


def extra_ffn(places, own, other, weights, after):
    gate_w, up_w, down_w = weights
    depth, units = gate_w.shape[1:]
    wide = depth // STEPS
    half = own.shape[0]

    def first(i):
        return jnp.where(i < 2 * STEPS, i & (STEPS - 1), STEPS - 1)

    def last(i):
        return jnp.maximum(i - 2 * STEPS, 0)

    def turn(i):
        return jnp.where(i < STEPS, 0, 1)

    rows_in = pl.BlockSpec((half, wide), lambda i, s: (0, first(i)))
    gate_in = pl.BlockSpec((1, wide, units), lambda i, s: (s[turn(i)], first(i), 0))
    rows_out = pl.BlockSpec((half, wide), lambda i, s: (0, last(i)))
    spec = pltpu.PrefetchScalarGridSpec(
        num_scalar_prefetch=1,
        grid=(3 * STEPS,),
        in_specs=[rows_in, rows_in, gate_in, gate_in]
        + [pl.BlockSpec((1, units, wide), lambda i, s, j=j: (s[j], 0, last(i))) for j in range(2)]
        + anywhere(len(after)),
        out_specs=[rows_out, rows_out],
        scratch_shapes=[
            pltpu.VMEM((2 * half, units), F32),
            pltpu.VMEM((2 * half, units), F32),
            pltpu.VMEM((2 * half, 2 * units), BF),
        ],
    )
    return pl.pallas_call(
        functools.partial(extra_kernel, len(after)),
        grid_spec=spec,
        out_shape=[jax.ShapeDtypeStruct((half, depth), BF)] * 2,
        compiler_params=PARAMS,
        cost_estimate=rough(20 * half * units * depth, 32 << 20),
        name="extra_ffn",
    )(places, own, other, gate_w, up_w, down_w, down_w, *after)


def add(*values):
    total = values[0].astype(F32)
    for value in values[1:]:
        total = total + value.astype(F32)
    return total.astype(BF)


def gather_line(own, after):
    pieces = [own] + [None] * (NZ - 1)
    up = down = own
    for step in range(1, NZ // 2 + 1):
        up = expert_move(up, dz=-1)
        pieces[step] = up
        if step < NZ // 2:
            down = expert_move(down, dz=1)
            pieces[NZ - step] = down
            up = relay(up, after[step - 1])
    return pieces + [expert_move(piece, flip=True) for piece in pieces]


def scatter_line(own, other):
    arrived = expert_move(other, flip=True)

    def term(dz):
        return own[dz * 32 : dz * 32 + 32], arrived[dz * 32 : dz * 32 + 32]

    up = add(*term(NZ // 2))
    for dz in range(NZ // 2 - 1, 0, -1):
        up = add(expert_move(up, dz=1), *term(dz))
    down = add(*term(NZ // 2 + 1))
    for dz in range(NZ // 2 + 2, NZ):
        down = add(expert_move(down, dz=-1), *term(dz))
    return [expert_move(up, dz=1), expert_move(down, dz=-1), *term(0)]


def spread_dp(block, cut):
    left = dp_move(block, 1)
    right = dp_move(block, -1)
    return [block, left, right, dp_move(left[:cut], 1), dp_move(right[cut:], -1)]


def sum_dp(parts):
    left_a, left_b, right_a, right_b, far_a, far_b, own = parts
    from_a = dp_move(far_a, -1)
    from_b = dp_move(far_b, 1)
    got_left_b = dp_move(left_b, -1)
    got_right_a = dp_move(right_a, 1)
    got_left_a = dp_move(add(left_a, from_a), -1)
    got_right_b = dp_move(add(right_b, from_b), 1)
    half = own.shape[0] // 2
    result = []
    for j in range(NY):
        low = j * PIECE
        if low < half:
            terms = (got_left_a[low : low + PIECE], got_right_a[low : low + PIECE])
        else:
            at = low - half
            terms = (got_left_b[at : at + PIECE], got_right_b[at : at + PIECE])
        result.append(add(own[low : low + PIECE], *terms))
    return result


def per_device(
    tokens,
    routes,
    route_weight,
    gate_weight,
    up_weight,
    down_weight,
    gate_scale,
    up_scale,
    down_scale,
):
    rows, depth = tokens.shape
    top = routes.shape[1]
    experts = gate_weight.shape[0] * NY * NZ * NC
    all_rows = rows * NX * NY * NZ * NC
    place = lax.axis_index("expert")
    y, line = place // (NZ * NC), place % (NZ * NC)

    high = lax.reduce_precision(route_weight, 8, 7)
    low = lax.reduce_precision(route_weight - high, 8, 7)
    meta = jnp.concatenate(
        [routes.astype(BF), high.astype(BF), low.astype(BF), jnp.zeros((rows, META - 3 * top), BF)],
        axis=1,
    )
    weights = (
        dequantize(gate_weight, gate_scale),
        dequantize(up_weight, up_scale),
        dequantize(down_weight, down_scale),
    )
    pieces = gather_line(jnp.concatenate([tokens, meta], axis=1), weights)

    lane = jnp.arange(META, dtype=jnp.int32)
    lane_expert = ((((y + lane % NY) % NY) * (NZ * NC) + line) * 2 + lane // NY).astype(F32)
    lanes = jnp.broadcast_to(jnp.where(lane < 8, lane_expert, -1.0)[None], (8, META))
    near, *blocks, tokens_line, metas = gather_rows(lanes, pieces, depth)
    near = spread_dp(near, PIECE)

    moved = [[expert_move(blocks[w * 3 + d - 1], dy=d) for d in range(1, NY)] for w in range(2)]
    counts = count_rows(metas, near[1:3])
    counts = sum([expert_move(counts, dy=d) for d in range(1, NY)], counts)
    counts = sum([dp_move(counts, d) for d in range(1, NX)], counts)
    load_share = counts[0, :experts] * (experts / (all_rows * top))

    extra, hot = pick_extra(counts, metas, tokens_line)
    hot_id = hot[0:2, 0].astype(jnp.int32)
    places = jnp.concatenate([hot_id & 1, ((hot_id >> 1) == place).astype(jnp.int32)])
    spare = jnp.where(lane == 8, hot[0:1], jnp.where(lane == 9, hot[1:2], lanes))
    plan = plan_scatter(spare, metas)
    extra = jnp.concatenate([extra] + [dp_move(extra, d) for d in range(1, NX)], axis=0)
    extra = jnp.concatenate([extra] + [expert_move(extra, dy=d) for d in range(1, NY)], axis=0)
    extra_other = expert_move(extra, flip=True)

    cut = 2 * PIECE - 32
    half = NY * PIECE // 2
    parts = []
    after = []
    spreads = []
    for which in range(2):
        spreads.append(spread_dp(merge(moved[which], after), cut))
        after = [spreads[0][1], spreads[0][2]]
    after = []
    for which in range(2):
        whole_spread = spreads[which]
        xs = [
            (near[1], PIECE, which),
            (whole_spread[1], 3 * PIECE, 0),
            (near[2], PIECE, which),
            (whole_spread[2], 3 * PIECE, 0),
            (near[3 + which], PIECE, 0),
            (whole_spread[3], cut, 0),
            (whole_spread[4], 3 * PIECE - cut, 0),
            (near[0], PIECE, which),
            (whole_spread[0], 3 * PIECE, 0),
        ]
        parts.append(ffn(xs, [half] * 6 + [2 * half], which, weights, after))
        if which == 0:
            own, other = extra_ffn(
                places, extra, extra_other, weights, [parts[0][-1], plan[0]]
            )
            after = [own]

    extra = add(own, expert_move(other, flip=True))
    size = NX * EXTRA
    extra = add(
        extra[:size],
        *[expert_move(extra[d * size : (d + 1) * size], dy=-d) for d in range(1, NY)],
    )
    extra = add(
        extra[:EXTRA], *[dp_move(extra[d * EXTRA : (d + 1) * EXTRA], -d) for d in range(1, NX)]
    )

    returned = []
    for which in range(2):
        group = sum_dp(parts[which])
        returned += [group[0]] + [expert_move(group[d], dy=-d) for d in range(1, NY)]
    terms = scatter_line(*scatter_rows(plan, extra, returned, depth))
    return add(*terms), load_share


def solution(mesh):
    in_specs = (
        P(("dp", "expert"), None),
        P(("dp", "expert"), None),
        P(("dp", "expert"), None),
        P("expert", None, "dp"),
        P("expert", None, "dp"),
        P("expert", "dp", None),
        P("expert", None, "dp"),
        P("expert", None, "dp"),
        P("expert", "dp", None),
    )
    out_specs = (P(("dp", "expert"), None), P())
    return jax.shard_map(
        per_device, mesh=mesh, in_specs=in_specs, out_specs=out_specs, check_vma=False
    )
```

```python
import functools

import jax
import jax.numpy as jnp
from jax import lax
from jax.experimental import pallas as pl
from jax.experimental.pallas import tpu as pltpu
from jax.sharding import PartitionSpec as P

BLOCK = 128
CAP = 3
NY, NZ, NC, NX = 4, 8, 2, 4
SRC = NZ * NC
PIECE = SRC * CAP
META = 128
COLS = 512
STEPS = 4
EXTRA = 2 * NZ
BF = jnp.bfloat16
F32 = jnp.float32
VMEM = 24 * 1024 * 1024


def expert_move(value, dy=0, dz=0, flip=False, xor_y=0):
    pairs = []
    for y in range(NY):
        for z in range(NZ):
            for c in range(NC):
                to_y = (y + dy) % NY ^ xor_y
                to_z = (z + dz) % NZ
                to_c = c ^ 1 if flip else c
                pairs.append(((y * NZ + z) * NC + c, (to_y * NZ + to_z) * NC + to_c))
    return lax.ppermute(value, "expert", pairs)


def dp_move(value, dx=0, xor_x=0):
    return lax.ppermute(value, "dp", [(x, (x + dx) % NX ^ xor_x) for x in range(NX)])


def slot_values(metas, lanes):
    tokens = metas.shape[0]
    found = jnp.zeros((tokens, META), F32)
    for k in range(8):
        found += jnp.where(metas[:, k : k + 1] == lanes, 1.0, 0.0)
    row = lax.broadcasted_iota(jnp.int32, (tokens, tokens), 0)
    col = lax.broadcasted_iota(jnp.int32, (tokens, tokens), 1)
    earlier = jnp.where(((row >> 5) == (col >> 5)) & (col < row), 1.0, 0.0).astype(BF)
    rank = jnp.dot(earlier, found.astype(BF), preferred_element_type=F32)
    return found * (rank + 1.0)


def slot_parts(slots):
    lane = (slots * 1366) >> 16
    rest = slots - lane * PIECE
    return lane, rest >> 4, rest & 15


def gather_kernel(lanes_ref, *refs):
    pieces, near_ref, outs = refs[:SRC], refs[SRC], refs[SRC + 1 : SRC + 7]
    line_ref, metas_ref, counts_ref = refs[SRC + 7 : SRC + 10]
    tokens, slots = SRC * 32, 8 * PIECE
    depth = near_ref.shape[1]
    metas = jnp.concatenate([p[:, depth : depth + META] for p in pieces], axis=0).astype(F32)
    metas_ref[...] = metas
    counted = jnp.concatenate([p[:, depth + META :] for p in pieces], axis=0).astype(F32)
    total = jnp.sum(counted, axis=0, keepdims=True) * (1.0 / 32.0)
    counts_ref[...] = jnp.broadcast_to(total, (8, META))
    for d in range(1, NY):
        outs[d - 1][:, depth:] = jnp.broadcast_to(total, (PIECE, META)).astype(BF)
    values = slot_values(metas, lanes_ref[0:1, :])
    slot_lane, _, _ = slot_parts(lax.broadcasted_iota(jnp.int32, (slots, META), 0))
    spread = jnp.where(
        slot_lane == lax.broadcasted_iota(jnp.int32, (slots, META), 1), 1.0, 0.0
    ).astype(BF)
    picked = lax.dot_general(
        spread, values.astype(BF), (((1,), (1,)), ((), ())), preferred_element_type=F32
    )
    _, rank, source = slot_parts(lax.broadcasted_iota(jnp.int32, (slots, tokens), 0))
    token = lax.broadcasted_iota(jnp.int32, (slots, tokens), 1)
    choose = jnp.where(
        (picked == (rank + 1).astype(F32)) & (source == (token >> 5)), 1.0, 0.0
    ).astype(BF)
    for start in range(0, depth, COLS):
        block = jnp.concatenate([p[:, start : start + COLS] for p in pieces], axis=0)
        line_ref[:, start : start + COLS] = block[: tokens // 2]
        rows = jnp.dot(choose, block, preferred_element_type=F32).astype(BF)
        for which in range(2):
            at = which * NY * PIECE
            near_ref[which * PIECE : (which + 1) * PIECE, start : start + COLS] = rows[at : at + PIECE]
            for d in range(1, NY):
                low = at + d * PIECE
                outs[which * 3 + d - 1][:, start : start + COLS] = rows[low : low + PIECE]


def relay_kernel(count, *refs):
    for in_ref, out_ref in zip(refs[:count], refs[-count:]):
        out_ref[...] = in_ref[...]


def cut_kernel(left_ref, right_ref, *refs):
    far_a, far_b = refs[-2:]
    far_a[...] = left_ref[: far_a.shape[0], :]
    far_b[...] = right_ref[far_a.shape[0] :, :]


def settle_kernel(own_ref, left_a, minus_ref, plus_ref, right_b, *refs):
    half = left_a.shape[0]
    for j, out in enumerate(refs[-NY:]):
        low = j * PIECE
        if low < half:
            left, right = left_a[low : low + PIECE, :], plus_ref[half + low : half + low + PIECE, :]
        else:
            at = low - half
            left, right = minus_ref[low : low + PIECE, :], right_b[at : at + PIECE, :]
        total = own_ref[low : low + PIECE, :].astype(F32) + left.astype(F32)
        out[...] = (total + right.astype(F32)).astype(BF)


def pick_kernel(counts_ref, metas_ref, line_ref, *refs):
    ins, (rows_ref, hot_ref, totals_ref) = refs[:3], refs[-3:]
    base = 3 * PIECE
    depth = rows_ref.shape[1]
    totals = counts_ref[0:1, :]
    for j in range(3):
        rows_ref[j * PIECE : (j + 1) * PIECE, :] = ins[j][:, :depth]
        totals = totals + ins[j][0:16, depth:].astype(F32)[0:1]
    totals_ref[...] = jnp.broadcast_to(totals, (8, META))
    tokens = NZ * 32
    every = lax.broadcasted_iota(jnp.int32, (1, META), 1).astype(F32)
    order = totals * META + (META - 1.0 - every)
    best = order == jnp.max(order, axis=1, keepdims=True)
    first = jnp.sum(jnp.where(best, every, 0.0), axis=1, keepdims=True)
    order = jnp.where(best, -1.0, order)
    best = order == jnp.max(order, axis=1, keepdims=True)
    second = jnp.sum(jnp.where(best, every, 0.0), axis=1, keepdims=True)
    row = lax.broadcasted_iota(jnp.int32, (8, META), 0)
    hot_ref[...] = jnp.where(row == 0, first, second)
    lanes = jnp.where(every == 0.0, first, jnp.where(every == 1.0, second, -1.0))
    values = slot_values(metas_ref[:tokens, :], lanes)
    slot = lax.broadcasted_iota(jnp.int32, (EXTRA, META), 0)
    spread = jnp.where(
        (slot & 1) == lax.broadcasted_iota(jnp.int32, (EXTRA, META), 1), 1.0, 0.0
    ).astype(BF)
    picked = lax.dot_general(
        spread, values.astype(BF), (((1,), (1,)), ((), ())), preferred_element_type=F32
    )
    slot = lax.broadcasted_iota(jnp.int32, (EXTRA, tokens), 0)
    token = lax.broadcasted_iota(jnp.int32, (EXTRA, tokens), 1)
    choose = jnp.where(
        (picked == CAP + 1.0) & ((slot >> 1) == (token >> 5)), 1.0, 0.0
    ).astype(BF)
    for start in range(0, depth, COLS):
        rows_ref[base:, start : start + COLS] = jnp.dot(
            choose, line_ref[:, start : start + COLS], preferred_element_type=F32
        ).astype(BF)


def plan_kernel(lanes_ref, metas_ref, high_ref, low_ref, extra_high_ref, extra_low_ref):
    tokens, slots = SRC * 32, 8 * PIECE
    own = tokens // 2
    lanes = lanes_ref[0:1, :]
    metas = metas_ref[...]
    values = slot_values(metas, lanes).astype(BF)
    high = jnp.zeros((tokens, META), F32)
    low = jnp.zeros((tokens, META), F32)
    for k in range(8):
        match = metas[:, k : k + 1] == lanes
        high += jnp.where(match, metas[:, 8 + k : 9 + k], 0.0)
        low += jnp.where(match, metas[:, 16 + k : 17 + k], 0.0)
    high, low = high.astype(BF), low.astype(BF)
    slot_lane, _, _ = slot_parts(lax.broadcasted_iota(jnp.int32, (META, slots), 1))
    spread = jnp.where(
        slot_lane == lax.broadcasted_iota(jnp.int32, (META, slots), 0), 1.0, 0.0
    ).astype(BF)
    picked = jnp.dot(values, spread, preferred_element_type=F32)
    _, rank, source = slot_parts(lax.broadcasted_iota(jnp.int32, (tokens, slots), 1))
    token = lax.broadcasted_iota(jnp.int32, (tokens, slots), 0)
    there = (picked == (rank + 1).astype(F32)) & (source == (token >> 5))
    high_at = jnp.dot(high, spread, preferred_element_type=F32)
    low_at = jnp.dot(low, spread, preferred_element_type=F32)
    high_ref[...] = jnp.where(there, high_at, 0.0).astype(BF)
    low_ref[...] = jnp.where(there, low_at, 0.0).astype(BF)
    slot = lax.broadcasted_iota(jnp.int32, (META, META), 1)
    from_lane = lax.broadcasted_iota(jnp.int32, (META, META), 0)
    spread = jnp.where((from_lane == 8 + (slot & 1)) & (slot < EXTRA), 1.0, 0.0).astype(BF)
    picked = jnp.dot(values[:own], spread, preferred_element_type=F32)
    slot = lax.broadcasted_iota(jnp.int32, (own, META), 1)
    token = lax.broadcasted_iota(jnp.int32, (own, META), 0)
    there = (picked == CAP + 1.0) & ((slot >> 1) == (token >> 5))
    high_at = jnp.dot(high[:own], spread, preferred_element_type=F32)
    low_at = jnp.dot(low[:own], spread, preferred_element_type=F32)
    extra_high_ref[...] = jnp.where(there, high_at, 0.0).astype(BF)
    extra_low_ref[...] = jnp.where(there, low_at, 0.0).astype(BF)


def scatter_kernel(own, skip, high_ref, low_ref, *refs):
    refs, out_ref = refs[: len(refs) - 1 - skip], refs[-1]
    extras, rows_in = refs[:-8], refs[-8:]
    half, depth = out_ref.shape
    at = 0 if own else half
    high, low = high_ref[at : at + half, :], low_ref[at : at + half, :]
    for start in range(0, depth, COLS):
        block = jnp.concatenate([r[:, start : start + COLS] for r in rows_in], axis=0)
        sums = jnp.dot(high, block, preferred_element_type=F32)
        sums += jnp.dot(low, block, preferred_element_type=F32)
        if own:
            extra_high, extra_low, extra_ref = extras
            extra = jnp.concatenate(
                [extra_ref[:, start : start + COLS], jnp.zeros((META - EXTRA, COLS), BF)], axis=0
            )
            sums += jnp.dot(extra_high[...], extra, preferred_element_type=F32)
            sums += jnp.dot(extra_low[...], extra, preferred_element_type=F32)
        out_ref[:, start : start + COLS] = sums.astype(BF)


def merge_kernel(*refs):
    ins, out = refs[:3], refs[-1]
    for j in range(3):
        out[j * PIECE : (j + 1) * PIECE, :] = ins[j][...]


def whole(count):
    return [pl.BlockSpec(memory_space=pltpu.VMEM)] * count


def anywhere(count):
    return [pl.BlockSpec(memory_space=pl.ANY)] * count


def rough(flops, size):
    return pl.CostEstimate(flops=flops // 64, bytes_accessed=size // 64, transcendentals=0)


PARAMS = pltpu.CompilerParams(vmem_limit_bytes=VMEM)


def gather_rows(lanes, pieces, depth):
    shapes = [jax.ShapeDtypeStruct((2 * PIECE, depth), BF)]
    shapes += [jax.ShapeDtypeStruct((PIECE, depth + META), BF)] * 3
    shapes += [jax.ShapeDtypeStruct((PIECE, depth), BF)] * 3
    shapes += [
        jax.ShapeDtypeStruct((SRC * 16, depth), BF),
        jax.ShapeDtypeStruct((SRC * 32, META), F32),
        jax.ShapeDtypeStruct((8, META), F32),
    ]
    return pl.pallas_call(
        gather_kernel,
        out_shape=shapes,
        in_specs=whole(1 + SRC),
        out_specs=whole(10),
        compiler_params=PARAMS,
        cost_estimate=rough(2 * 384 * 512 * depth, 7 << 20),
        name="gather_rows",
    )(lanes, *pieces)


def relay(arrays, after):
    count = len(arrays)
    return pl.pallas_call(
        functools.partial(relay_kernel, count),
        out_shape=[jax.ShapeDtypeStruct(a.shape, a.dtype) for a in arrays],
        in_specs=whole(count) + anywhere(len(after)),
        out_specs=whole(count),
        compiler_params=PARAMS,
        cost_estimate=rough(0, 1 << 19),
        name="relay",
    )(*arrays, *after)


def cut_far(left, right, cut, after):
    rows, depth = left.shape
    return pl.pallas_call(
        cut_kernel,
        out_shape=[jax.ShapeDtypeStruct((r, depth), BF) for r in (cut, rows - cut)],
        in_specs=whole(2) + anywhere(len(after)),
        out_specs=whole(2),
        compiler_params=PARAMS,
        cost_estimate=rough(0, 2 << 20),
        name="cut_far",
    )(left, right, *after)


def join_kernel(own_ref, left_ref, far_ref, right_ref, *refs):
    out = refs[-1]
    for j, ref in enumerate((own_ref, left_ref, far_ref, right_ref)):
        out[j * EXTRA : (j + 1) * EXTRA, :] = ref[ref.shape[0] - EXTRA :, :]


def join_extra(blocks, after):
    return pl.pallas_call(
        join_kernel,
        out_shape=jax.ShapeDtypeStruct((NX * EXTRA, blocks[0].shape[1]), BF),
        in_specs=whole(4) + anywhere(len(after)),
        out_specs=whole(1)[0],
        compiler_params=PARAMS,
        cost_estimate=rough(0, 1 << 19),
        name="join_extra",
    )(*blocks, *after)


def stack_kernel(count, *refs):
    rows, out = refs[0].shape[0], refs[-1]
    for j in range(count):
        out[j * rows : (j + 1) * rows, :] = refs[j][...]


def stack(arrays, after):
    rows, depth = arrays[0].shape
    return pl.pallas_call(
        functools.partial(stack_kernel, len(arrays)),
        out_shape=jax.ShapeDtypeStruct((len(arrays) * rows, depth), BF),
        in_specs=whole(len(arrays)) + anywhere(len(after)),
        out_specs=whole(1)[0],
        compiler_params=PARAMS,
        cost_estimate=rough(0, 4 << 20),
        name="stack",
    )(*arrays, *after)


def fold_kernel(left_a, minus, right_b, plus, left_out, right_out):
    half = left_a.shape[0]
    left_out[...] = (left_a[...].astype(F32) + minus[:half, :].astype(F32)).astype(BF)
    right_out[...] = (right_b[...].astype(F32) + plus[:half, :].astype(F32)).astype(BF)


def fold(left_a, minus, right_b, plus):
    return pl.pallas_call(
        fold_kernel,
        out_shape=[jax.ShapeDtypeStruct(left_a.shape, BF)] * 2,
        in_specs=whole(4),
        out_specs=whole(2),
        compiler_params=PARAMS,
        cost_estimate=rough(0, 4 << 20),
        name="fold",
    )(left_a, minus, right_b, plus)


def pair_kernel(a_ref, b_ref, *refs):
    refs[-1][...] = (a_ref[...].astype(F32) + b_ref[...].astype(F32)).astype(BF)


def pair_sum(a, b, after):
    return pl.pallas_call(
        pair_kernel,
        out_shape=jax.ShapeDtypeStruct(a.shape, BF),
        in_specs=whole(2) + anywhere(len(after)),
        out_specs=whole(1)[0],
        compiler_params=PARAMS,
        cost_estimate=rough(0, 4 << 20),
        name="pair_sum",
    )(a, b, *after)


def settle(own, terms, after):
    depth = own.shape[1]
    return pl.pallas_call(
        settle_kernel,
        out_shape=[jax.ShapeDtypeStruct((PIECE, depth), BF)] * NY,
        in_specs=whole(5) + anywhere(len(after)),
        out_specs=whole(NY),
        compiler_params=PARAMS,
        cost_estimate=rough(0, 5 << 20),
        name="settle",
    )(own, *terms, *after)


def merge_pick(counts, metas, line, pieces, after):
    depth = line.shape[1]
    return pl.pallas_call(
        pick_kernel,
        out_shape=[
            jax.ShapeDtypeStruct((3 * PIECE + EXTRA, depth), BF),
            jax.ShapeDtypeStruct((8, META), F32),
            jax.ShapeDtypeStruct((8, META), F32),
        ],
        in_specs=whole(6) + anywhere(len(after)),
        out_specs=whole(3),
        compiler_params=PARAMS,
        cost_estimate=rough(2 * 16 * 256 * depth, 2 << 20),
        name="merge_pick",
    )(counts, metas, line, *pieces, *after)


def plan_scatter(lanes, metas):
    shapes = [jax.ShapeDtypeStruct((SRC * 32, 8 * PIECE), BF)] * 2
    shapes += [jax.ShapeDtypeStruct((SRC * 16, META), BF)] * 2
    return pl.pallas_call(
        plan_kernel,
        out_shape=shapes,
        in_specs=whole(2),
        out_specs=whole(4),
        compiler_params=PARAMS,
        cost_estimate=rough(512 * 512 * 1024, 1 << 20),
        name="plan_scatter",
    )(lanes, metas)


def scatter_rows(own, plan, rows, after):
    depth = rows[0].shape[1]
    return pl.pallas_call(
        functools.partial(scatter_kernel, own, len(after)),
        out_shape=jax.ShapeDtypeStruct((SRC * 16, depth), BF),
        in_specs=whole(len(plan) + len(rows)) + anywhere(len(after)),
        out_specs=whole(1)[0],
        compiler_params=PARAMS,
        cost_estimate=rough(2 * 384 * 512 * depth, 5 << 20),
        name="scatter_rows",
    )(*plan, *rows, *after)


def merge(pieces, after):
    depth = pieces[0].shape[1]
    return pl.pallas_call(
        merge_kernel,
        out_shape=jax.ShapeDtypeStruct((3 * PIECE, depth), BF),
        in_specs=whole(3) + anywhere(len(after)),
        out_specs=whole(1)[0],
        compiler_params=PARAMS,
        cost_estimate=rough(0, 2 << 20),
        name="merge",
    )(*pieces, *after)


def deq_kernel(w_ref, s_ref, out_ref):
    rows, cols = w_ref.shape[1:]
    scales = s_ref[0]
    for r in range(rows // BLOCK):
        for c in range(cols // BLOCK):
            at = (0, slice(r * BLOCK, (r + 1) * BLOCK), slice(c * BLOCK, (c + 1) * BLOCK))
            out_ref[at] = (w_ref[at].astype(F32) * scales[r : r + 1, c : c + 1]).astype(BF)


def dequantize(weight, scale):
    count, rows, cols = weight.shape

    def block(array):
        return pl.BlockSpec((1,) + array.shape[1:], lambda i: (i, 0, 0))

    return pl.pallas_call(
        deq_kernel,
        grid=(count,),
        out_shape=jax.ShapeDtypeStruct(weight.shape, BF),
        in_specs=[block(weight), block(scale)],
        out_specs=block(weight),
        compiler_params=PARAMS,
        cost_estimate=rough(count * rows * cols, 4 * count * rows * cols),
        name="dequantize",
    )(weight, scale)


def silu(value):
    return value * (1.0 / (1.0 + jnp.exp(-value)))


def ffn_kernel(in_count, out_parts, skip, *refs):
    xs, (gate_w, up_w, down_w) = refs[:in_count], refs[in_count : in_count + 3]
    refs = refs[in_count + 3 + skip :]
    outs, (gate_acc, up_acc, hidden) = refs[: len(out_parts)], refs[len(out_parts) :]
    step = pl.program_id(0)

    @pl.when(step < STEPS)
    def _():
        x = jnp.concatenate([r[...] for r in xs], axis=0)
        gate = jnp.dot(x, gate_w[0], preferred_element_type=F32)
        up = jnp.dot(x, up_w[0], preferred_element_type=F32)

        @pl.when(step == 0)
        def _():
            gate_acc[...] = gate
            up_acc[...] = up

        @pl.when(step > 0)
        def _():
            gate_acc[...] += gate
            up_acc[...] += up

    @pl.when(step >= STEPS)
    def _():
        @pl.when(step == STEPS)
        def _():
            hidden[...] = (silu(gate_acc[...]) * up_acc[...]).astype(BF)

        result = jnp.dot(hidden[...], down_w[0], preferred_element_type=F32).astype(BF)
        for ref, parts in zip(outs, out_parts):
            at = 0
            for low, high in parts:
                ref[at : at + high - low, :] = result[low:high]
                at += high - low


def early(i):
    return jnp.minimum(i, STEPS - 1)


def late(i):
    return jnp.maximum(i - STEPS, 0)


def ffn(xs, out_parts, which, weights, after):
    gate_w, up_w, down_w = weights
    depth, units = gate_w.shape[1:]
    wide = depth // STEPS
    total = sum(rows for _, rows, _ in xs)
    out_rows = [sum(high - low for low, high in parts) for parts in out_parts]
    in_specs = [
        pl.BlockSpec((rows, wide), lambda i, place=place: (place, early(i))) for _, rows, place in xs
    ]
    in_specs += [pl.BlockSpec((1, wide, units), lambda i: (which, early(i), 0))] * 2
    in_specs += [pl.BlockSpec((1, units, wide), lambda i: (which, 0, late(i)))]
    return pl.pallas_call(
        functools.partial(ffn_kernel, len(xs), out_parts, len(after)),
        grid=(2 * STEPS,),
        out_shape=[jax.ShapeDtypeStruct((r, depth), BF) for r in out_rows],
        in_specs=in_specs + anywhere(len(after)),
        out_specs=[pl.BlockSpec((r, wide), lambda i: (0, late(i))) for r in out_rows],
        scratch_shapes=[
            pltpu.VMEM((total, units), F32),
            pltpu.VMEM((total, units), F32),
            pltpu.VMEM((total, units), BF),
        ],
        compiler_params=PARAMS,
        cost_estimate=rough(6 * total * units * depth, 4 * total * depth + 6 * units * depth),
        name="ffn",
    )(*[x for x, _, _ in xs], gate_w, up_w, down_w, *after)


def extra_kernel(skip, place_ref, own_in, other_in, gate_w, up_w, down_a, down_b, *refs):
    own_out, other_out, gate_acc, up_acc, hidden = refs[skip:]
    step = pl.program_id(0)
    units = gate_w.shape[2]

    @pl.when(step < 2 * STEPS)
    def _():
        x = jnp.concatenate([own_in[...], other_in[...]], axis=0)
        gate = jnp.dot(x, gate_w[0], preferred_element_type=F32)
        up = jnp.dot(x, up_w[0], preferred_element_type=F32)
        opening = (step == 0) | (step == STEPS)

        @pl.when(opening)
        def _():
            gate_acc[...] = gate
            up_acc[...] = up

        @pl.when(jnp.logical_not(opening))
        def _():
            gate_acc[...] += gate
            up_acc[...] += up

    for j in range(2):

        @pl.when(step == (j + 1) * STEPS - 1)
        def _(j=j):
            value = silu(gate_acc[...]) * up_acc[...]
            row = lax.broadcasted_iota(jnp.int32, value.shape, 0)
            keep = ((row & 1) == j) & (place_ref[2 + j] == 1)
            hidden[:, j * units : (j + 1) * units] = jnp.where(keep, value, 0.0).astype(BF)

    @pl.when(step >= 2 * STEPS)
    def _():
        down = jnp.concatenate([down_a[0], down_b[0]], axis=0)
        result = jnp.dot(hidden[...], down, preferred_element_type=F32).astype(BF)
        half = own_out.shape[0]
        own_out[...] = result[:half]
        other_out[...] = result[half:]


def extra_ffn(places, own, other, weights, after):
    gate_w, up_w, down_w = weights
    depth, units = gate_w.shape[1:]
    wide = depth // STEPS
    half = own.shape[0]

    def first(i):
        return jnp.where(i < 2 * STEPS, i & (STEPS - 1), STEPS - 1)

    def last(i):
        return jnp.maximum(i - 2 * STEPS, 0)

    def turn(i):
        return jnp.where(i < STEPS, 0, 1)

    rows_in = pl.BlockSpec((half, wide), lambda i, s: (0, first(i)))
    gate_in = pl.BlockSpec((1, wide, units), lambda i, s: (s[turn(i)], first(i), 0))
    rows_out = pl.BlockSpec((half, wide), lambda i, s: (0, last(i)))
    spec = pltpu.PrefetchScalarGridSpec(
        num_scalar_prefetch=1,
        grid=(3 * STEPS,),
        in_specs=[rows_in, rows_in, gate_in, gate_in]
        + [pl.BlockSpec((1, units, wide), lambda i, s, j=j: (s[j], 0, last(i))) for j in range(2)]
        + anywhere(len(after)),
        out_specs=[rows_out, rows_out],
        scratch_shapes=[
            pltpu.VMEM((2 * half, units), F32),
            pltpu.VMEM((2 * half, units), F32),
            pltpu.VMEM((2 * half, 2 * units), BF),
        ],
    )
    return pl.pallas_call(
        functools.partial(extra_kernel, len(after)),
        grid_spec=spec,
        out_shape=[jax.ShapeDtypeStruct((half, depth), BF)] * 2,
        compiler_params=PARAMS,
        cost_estimate=rough(20 * half * units * depth, 32 << 20),
        name="extra_ffn",
    )(places, own, other, gate_w, up_w, down_w, down_w, *after)


def add(*values):
    total = values[0].astype(F32)
    for value in values[1:]:
        total = total + value.astype(F32)
    return total.astype(BF)


def gather_line(own, after):
    pieces = [own] + [None] * (NZ - 1)
    up = down = own
    for step in range(1, NZ // 2 + 1):
        up = expert_move(up, dz=-1)
        pieces[step] = up
        if step < NZ // 2:
            down = expert_move(down, dz=1)
            pieces[NZ - step] = down
            up = relay([up], [after[step - 1]])[0]
    return pieces + [expert_move(piece, flip=True) for piece in pieces]


def scatter_line(own, other):
    arrived = expert_move(other, flip=True)

    def term(dz):
        return own[dz * 32 : dz * 32 + 32], arrived[dz * 32 : dz * 32 + 32]

    up = add(*term(NZ // 2))
    for dz in range(NZ // 2 - 1, 0, -1):
        up = add(expert_move(up, dz=1), *term(dz))
    down = add(*term(NZ // 2 + 1))
    for dz in range(NZ // 2 + 2, NZ):
        down = add(expert_move(down, dz=-1), *term(dz))
    return [expert_move(up, dz=1), expert_move(down, dz=-1), *term(0)]


def spread_dp(block, cut, after=()):
    left = dp_move(block, 1)
    right = dp_move(block, -1)
    far = cut_far(left, right, cut, after) if after else (left[:cut], right[cut:])
    return [block, left, right, dp_move(far[0], 1), dp_move(far[1], -1), *far]


def sum_dp_first(parts):
    minus, plus, left_a, right_b, own = parts
    got_minus = dp_move(minus, -1)
    got_plus = dp_move(plus, 1)
    left_a, right_b = fold(left_a, got_minus, right_b, got_plus)
    return left_a, got_minus, got_plus, right_b, own


def sum_dp_second(state, after):
    left_a, got_minus, got_plus, right_b, own = state
    got_left_a = dp_move(left_a, -1)
    got_right_b = dp_move(right_b, 1)
    return settle(own, (got_left_a, got_minus, got_plus, got_right_b), after), [got_left_a, got_right_b]


def per_device(
    tokens,
    routes,
    route_weight,
    gate_weight,
    up_weight,
    down_weight,
    gate_scale,
    up_scale,
    down_scale,
):
    rows, depth = tokens.shape
    top = routes.shape[1]
    experts = gate_weight.shape[0] * NY * NZ * NC
    all_rows = rows * NX * NY * NZ * NC
    place = lax.axis_index("expert")
    y, line = place // (NZ * NC), place % (NZ * NC)
    lane = jnp.arange(META, dtype=jnp.int32)

    named = (routes[:, :, None] == lane[None, None, :]).astype(F32)
    counts = jnp.broadcast_to(jnp.sum(named, axis=(0, 1))[None], (8, META))
    counts = sum([dp_move(counts, d) for d in range(1, NX)], counts)
    high = lax.reduce_precision(route_weight, 8, 7)
    low = lax.reduce_precision(route_weight - high, 8, 7)
    carried = jnp.concatenate(
        [
            tokens,
            routes.astype(BF),
            high.astype(BF),
            low.astype(BF),
            jnp.zeros((rows, META - 3 * top), BF),
            jnp.broadcast_to(counts[:1].astype(BF), (rows, META)),
        ],
        axis=1,
    )
    weights = (
        dequantize(gate_weight, gate_scale),
        dequantize(up_weight, up_scale),
        dequantize(down_weight, down_scale),
    )
    pieces = gather_line(carried, weights)

    lane_expert = ((((y + lane % NY) % NY) * (NZ * NC) + line) * 2 + lane // NY).astype(F32)
    lanes = jnp.broadcast_to(jnp.where(lane < 8, lane_expert, -1.0)[None], (8, META))
    near, *blocks, tokens_line, metas, counts = gather_rows(lanes, pieces, depth)
    near = spread_dp(near, PIECE)
    moved = [[expert_move(blocks[w * 3 + d - 1], dy=d) for d in range(1, NY)] for w in range(2)]

    first, hot, totals = merge_pick(counts, metas, tokens_line, moved[0], near[1:3])
    load_share = totals[0, :experts] * (experts / (all_rows * top))
    size = 3 * PIECE
    cuts = [(size + EXTRA) // 2, size - 4 * EXTRA]
    spreads = [spread_dp(first, cuts[0], moved[1])]
    spreads.append(spread_dp(merge(moved[1], spreads[0][5:]), cuts[1]))

    hot_id = hot[0:2, 0].astype(jnp.int32)
    places = jnp.concatenate([hot_id & 1, ((hot_id >> 1) == place).astype(jnp.int32)])
    spare = jnp.where(lane == 8, hot[0:1], jnp.where(lane == 9, hot[1:2], lanes))
    plan = plan_scatter(spare, metas)
    order = [spreads[0][i] for i in (0, 1, 4, 2)]
    extra = join_extra(order, [spreads[1][0], spreads[0][3], near[3], near[4]])
    extra = stack([extra] + [expert_move(extra, dy=d) for d in range(1, NY)], spreads[1][1:3])
    extra_other = expert_move(extra, flip=True)

    half = NY * PIECE // 2
    out_parts = [
        [(4 * half, 5 * half), (half, 2 * half)],
        [(5 * half, 6 * half), (2 * half, 3 * half)],
        [(0, half)],
        [(3 * half, 4 * half)],
        [(6 * half, 8 * half)],
    ]
    parts = []
    after = [extra, plan[0]]
    for which in range(2):
        cut, block = cuts[which], spreads[which]
        xs = [
            (near[1], PIECE, which),
            (block[1], size, 0),
            (near[2], PIECE, which),
            (block[2], size, 0),
            (near[3 + which], PIECE, 0),
            (block[3], cut, 0),
            (block[4], size - cut, 0),
            (near[0], PIECE, which),
            (block[0], size, 0),
        ]
        parts.append(list(ffn(xs, out_parts, which, weights, after)))
        if which == 0:
            parts[0][:2] = relay(parts[0][:2], [near[4], *spreads[1][3:5]])
            own, other = extra_ffn(places, extra, extra_other, weights, parts[0][:1])
            state = sum_dp_first(parts[0])
            extra = pair_sum(own, expert_move(other, flip=True), [])
            after = [own, state[0]]

    size = NX * EXTRA
    extra = add(
        extra[:size],
        *[expert_move(extra[d * size : (d + 1) * size], dy=-d) for d in range(1, NY)],
    )
    group, arrived = sum_dp_second(state, [extra])
    parts[1][:2] = relay(parts[1][:2], arrived)
    extra = add(
        extra[:EXTRA], *[dp_move(extra[d * EXTRA : (d + 1) * EXTRA], -d) for d in range(1, NX)]
    )
    returned = [group[0]] + [expert_move(group[d], dy=-d) for d in range(1, NY)]
    group, _ = sum_dp_second(sum_dp_first(parts[1]), returned)
    returned += [group[0]] + [expert_move(group[d], dy=-d) for d in range(1, NY)]
    other = scatter_rows(False, plan[:2], returned, [extra])
    own = scatter_rows(True, [*plan, extra], returned, [])
    terms = scatter_line(own, other)
    return add(*terms), load_share


def solution(mesh):
    in_specs = (
        P(("dp", "expert"), None),
        P(("dp", "expert"), None),
        P(("dp", "expert"), None),
        P("expert", None, "dp"),
        P("expert", None, "dp"),
        P("expert", "dp", None),
        P("expert", None, "dp"),
        P("expert", None, "dp"),
        P("expert", "dp", None),
    )
    out_specs = (P(("dp", "expert"), None), P())
    return jax.shard_map(
        per_device, mesh=mesh, in_specs=in_specs, out_specs=out_specs, check_vma=False
    )
```

```python
import functools

import jax
import jax.numpy as jnp
from jax import lax
from jax.experimental import pallas as pl
from jax.experimental.pallas import tpu as pltpu
from jax.sharding import PartitionSpec as P

BLOCK = 128
CAP = 3
NY, NZ, NC, NX = 4, 8, 2, 4
SRC = NZ * NC
PIECE = SRC * CAP
META = 128
COLS = 512
STEPS = 4
EXTRA = 2 * NZ
BF = jnp.bfloat16
F32 = jnp.float32
VMEM = 24 * 1024 * 1024


def expert_move(value, dy=0, dz=0, flip=False, xor_y=0):
    pairs = []
    for y in range(NY):
        for z in range(NZ):
            for c in range(NC):
                to_y = (y + dy) % NY ^ xor_y
                to_z = (z + dz) % NZ
                to_c = c ^ 1 if flip else c
                pairs.append(((y * NZ + z) * NC + c, (to_y * NZ + to_z) * NC + to_c))
    return lax.ppermute(value, "expert", pairs)


def dp_move(value, dx=0, xor_x=0):
    return lax.ppermute(value, "dp", [(x, (x + dx) % NX ^ xor_x) for x in range(NX)])


def slot_values(metas, lanes):
    tokens = metas.shape[0]
    found = jnp.zeros((tokens, META), F32)
    for k in range(8):
        found += jnp.where(metas[:, k : k + 1] == lanes, 1.0, 0.0)
    row = lax.broadcasted_iota(jnp.int32, (tokens, tokens), 0)
    col = lax.broadcasted_iota(jnp.int32, (tokens, tokens), 1)
    earlier = jnp.where(((row >> 5) == (col >> 5)) & (col < row), 1.0, 0.0).astype(BF)
    rank = jnp.dot(earlier, found.astype(BF), preferred_element_type=F32)
    return found * (rank + 1.0)


def slot_parts(slots):
    lane = (slots * 1366) >> 16
    rest = slots - lane * PIECE
    return lane, rest >> 4, rest & 15


def gather_kernel(lanes_ref, *refs):
    pieces, near_ref, outs = refs[:SRC], refs[SRC], refs[SRC + 1 : SRC + 7]
    line_ref, metas_ref, counts_ref = refs[SRC + 7 : SRC + 10]
    tokens, slots = SRC * 32, 8 * PIECE
    depth = near_ref.shape[1]
    metas = jnp.concatenate([p[:, depth : depth + META] for p in pieces], axis=0).astype(F32)
    metas_ref[...] = metas
    counted = jnp.concatenate([p[:, depth + META :] for p in pieces], axis=0).astype(F32)
    total = jnp.sum(counted, axis=0, keepdims=True) * (1.0 / 32.0)
    counts_ref[...] = jnp.broadcast_to(total, (8, META))
    for d in range(1, NY):
        outs[d - 1][:, depth:] = jnp.broadcast_to(total, (PIECE, META)).astype(BF)
    values = slot_values(metas, lanes_ref[0:1, :])
    slot_lane, _, _ = slot_parts(lax.broadcasted_iota(jnp.int32, (slots, META), 0))
    spread = jnp.where(
        slot_lane == lax.broadcasted_iota(jnp.int32, (slots, META), 1), 1.0, 0.0
    ).astype(BF)
    picked = lax.dot_general(
        spread, values.astype(BF), (((1,), (1,)), ((), ())), preferred_element_type=F32
    )
    _, rank, source = slot_parts(lax.broadcasted_iota(jnp.int32, (slots, tokens), 0))
    token = lax.broadcasted_iota(jnp.int32, (slots, tokens), 1)
    choose = jnp.where(
        (picked == (rank + 1).astype(F32)) & (source == (token >> 5)), 1.0, 0.0
    ).astype(BF)
    for start in range(0, depth, COLS):
        block = jnp.concatenate([p[:, start : start + COLS] for p in pieces], axis=0)
        line_ref[:, start : start + COLS] = block[: tokens // 2]
        rows = jnp.dot(choose, block, preferred_element_type=F32).astype(BF)
        for which in range(2):
            at = which * NY * PIECE
            near_ref[which * PIECE : (which + 1) * PIECE, start : start + COLS] = rows[at : at + PIECE]
            for d in range(1, NY):
                low = at + d * PIECE
                outs[which * 3 + d - 1][:, start : start + COLS] = rows[low : low + PIECE]


def relay_kernel(count, *refs):
    for in_ref, out_ref in zip(refs[:count], refs[-count:]):
        out_ref[...] = in_ref[...]


def cut_kernel(left_ref, right_ref, *refs):
    far_a, far_b = refs[-2:]
    far_a[...] = left_ref[: far_a.shape[0], :]
    far_b[...] = right_ref[far_a.shape[0] :, :]


def settle_kernel(own_ref, left_a, minus_ref, plus_ref, right_b, *refs):
    half = left_a.shape[0]
    for j, out in enumerate(refs[-NY:]):
        low = j * PIECE
        if low < half:
            left, right = left_a[low : low + PIECE, :], plus_ref[half + low : half + low + PIECE, :]
        else:
            at = low - half
            left, right = minus_ref[low : low + PIECE, :], right_b[at : at + PIECE, :]
        total = own_ref[low : low + PIECE, :].astype(F32) + left.astype(F32)
        out[...] = (total + right.astype(F32)).astype(BF)


def pick_kernel(counts_ref, metas_ref, line_ref, *refs):
    ins, (rows_ref, hot_ref, totals_ref) = refs[:3], refs[-3:]
    base = 3 * PIECE
    depth = rows_ref.shape[1]
    totals = counts_ref[0:1, :]
    for j in range(3):
        rows_ref[j * PIECE : (j + 1) * PIECE, :] = ins[j][:, :depth]
        totals = totals + ins[j][0:16, depth:].astype(F32)[0:1]
    totals_ref[...] = jnp.broadcast_to(totals, (8, META))
    tokens = NZ * 32
    every = lax.broadcasted_iota(jnp.int32, (1, META), 1).astype(F32)
    order = totals * META + (META - 1.0 - every)
    best = order == jnp.max(order, axis=1, keepdims=True)
    first = jnp.sum(jnp.where(best, every, 0.0), axis=1, keepdims=True)
    order = jnp.where(best, -1.0, order)
    best = order == jnp.max(order, axis=1, keepdims=True)
    second = jnp.sum(jnp.where(best, every, 0.0), axis=1, keepdims=True)
    row = lax.broadcasted_iota(jnp.int32, (8, META), 0)
    hot_ref[...] = jnp.where(row == 0, first, second)
    lanes = jnp.where(every == 0.0, first, jnp.where(every == 1.0, second, -1.0))
    values = slot_values(metas_ref[:tokens, :], lanes)
    slot = lax.broadcasted_iota(jnp.int32, (EXTRA, META), 0)
    spread = jnp.where(
        (slot & 1) == lax.broadcasted_iota(jnp.int32, (EXTRA, META), 1), 1.0, 0.0
    ).astype(BF)
    picked = lax.dot_general(
        spread, values.astype(BF), (((1,), (1,)), ((), ())), preferred_element_type=F32
    )
    slot = lax.broadcasted_iota(jnp.int32, (EXTRA, tokens), 0)
    token = lax.broadcasted_iota(jnp.int32, (EXTRA, tokens), 1)
    choose = jnp.where(
        (picked == CAP + 1.0) & ((slot >> 1) == (token >> 5)), 1.0, 0.0
    ).astype(BF)
    for start in range(0, depth, COLS):
        rows_ref[base:, start : start + COLS] = jnp.dot(
            choose, line_ref[:, start : start + COLS], preferred_element_type=F32
        ).astype(BF)


def plan_kernel(lanes_ref, metas_ref, high_ref, low_ref, extra_high_ref, extra_low_ref):
    tokens, slots = SRC * 32, 8 * PIECE
    own = tokens // 2
    lanes = lanes_ref[0:1, :]
    metas = metas_ref[...]
    values = slot_values(metas, lanes).astype(BF)
    high = jnp.zeros((tokens, META), F32)
    low = jnp.zeros((tokens, META), F32)
    for k in range(8):
        match = metas[:, k : k + 1] == lanes
        high += jnp.where(match, metas[:, 8 + k : 9 + k], 0.0)
        low += jnp.where(match, metas[:, 16 + k : 17 + k], 0.0)
    high, low = high.astype(BF), low.astype(BF)
    slot_lane, _, _ = slot_parts(lax.broadcasted_iota(jnp.int32, (META, slots), 1))
    spread = jnp.where(
        slot_lane == lax.broadcasted_iota(jnp.int32, (META, slots), 0), 1.0, 0.0
    ).astype(BF)
    picked = jnp.dot(values, spread, preferred_element_type=F32)
    _, rank, source = slot_parts(lax.broadcasted_iota(jnp.int32, (tokens, slots), 1))
    token = lax.broadcasted_iota(jnp.int32, (tokens, slots), 0)
    there = (picked == (rank + 1).astype(F32)) & (source == (token >> 5))
    high_at = jnp.dot(high, spread, preferred_element_type=F32)
    low_at = jnp.dot(low, spread, preferred_element_type=F32)
    high_ref[...] = jnp.where(there, high_at, 0.0).astype(BF)
    low_ref[...] = jnp.where(there, low_at, 0.0).astype(BF)
    slot = lax.broadcasted_iota(jnp.int32, (META, META), 1)
    from_lane = lax.broadcasted_iota(jnp.int32, (META, META), 0)
    spread = jnp.where((from_lane == 8 + (slot & 1)) & (slot < EXTRA), 1.0, 0.0).astype(BF)
    picked = jnp.dot(values[:own], spread, preferred_element_type=F32)
    slot = lax.broadcasted_iota(jnp.int32, (own, META), 1)
    token = lax.broadcasted_iota(jnp.int32, (own, META), 0)
    there = (picked == CAP + 1.0) & ((slot >> 1) == (token >> 5))
    high_at = jnp.dot(high[:own], spread, preferred_element_type=F32)
    low_at = jnp.dot(low[:own], spread, preferred_element_type=F32)
    extra_high_ref[...] = jnp.where(there, high_at, 0.0).astype(BF)
    extra_low_ref[...] = jnp.where(there, low_at, 0.0).astype(BF)


def scatter_kernel(own, skip, high_ref, low_ref, *refs):
    refs, out_ref = refs[: len(refs) - 1 - skip], refs[-1]
    extras, rows_in = refs[:-8], refs[-8:]
    half, depth = out_ref.shape
    at = 0 if own else half
    high, low = high_ref[at : at + half, :], low_ref[at : at + half, :]
    for start in range(0, depth, COLS):
        block = jnp.concatenate([r[:, start : start + COLS] for r in rows_in], axis=0)
        sums = jnp.dot(high, block, preferred_element_type=F32)
        sums += jnp.dot(low, block, preferred_element_type=F32)
        if own:
            extra_high, extra_low, extra_ref = extras
            extra = jnp.concatenate(
                [extra_ref[:, start : start + COLS], jnp.zeros((META - EXTRA, COLS), BF)], axis=0
            )
            sums += jnp.dot(extra_high[...], extra, preferred_element_type=F32)
            sums += jnp.dot(extra_low[...], extra, preferred_element_type=F32)
        out_ref[:, start : start + COLS] = sums.astype(BF)


def merge_kernel(*refs):
    ins, out = refs[:3], refs[-1]
    for j in range(3):
        out[j * PIECE : (j + 1) * PIECE, :] = ins[j][...]


def whole(count):
    return [pl.BlockSpec(memory_space=pltpu.VMEM)] * count


def anywhere(count):
    return [pl.BlockSpec(memory_space=pl.ANY)] * count


def rough(flops, size):
    return pl.CostEstimate(flops=flops // 64, bytes_accessed=size // 64, transcendentals=0)


PARAMS = pltpu.CompilerParams(vmem_limit_bytes=VMEM)


def gather_rows(lanes, pieces, depth):
    shapes = [jax.ShapeDtypeStruct((2 * PIECE, depth), BF)]
    shapes += [jax.ShapeDtypeStruct((PIECE, depth + META), BF)] * 3
    shapes += [jax.ShapeDtypeStruct((PIECE, depth), BF)] * 3
    shapes += [
        jax.ShapeDtypeStruct((SRC * 16, depth), BF),
        jax.ShapeDtypeStruct((SRC * 32, META), F32),
        jax.ShapeDtypeStruct((8, META), F32),
    ]
    return pl.pallas_call(
        gather_kernel,
        out_shape=shapes,
        in_specs=whole(1 + SRC),
        out_specs=whole(10),
        compiler_params=PARAMS,
        cost_estimate=rough(2 * 384 * 512 * depth, 7 << 20),
        name="gather_rows",
    )(lanes, *pieces)


def relay(arrays, after):
    count = len(arrays)
    return pl.pallas_call(
        functools.partial(relay_kernel, count),
        out_shape=[jax.ShapeDtypeStruct(a.shape, a.dtype) for a in arrays],
        in_specs=whole(count) + anywhere(len(after)),
        out_specs=whole(count),
        compiler_params=PARAMS,
        cost_estimate=rough(0, 1 << 19),
        name="relay",
    )(*arrays, *after)


def cut_far(left, right, cut, after):
    rows, depth = left.shape
    return pl.pallas_call(
        cut_kernel,
        out_shape=[jax.ShapeDtypeStruct((r, depth), BF) for r in (cut, rows - cut)],
        in_specs=whole(2) + anywhere(len(after)),
        out_specs=whole(2),
        compiler_params=PARAMS,
        cost_estimate=rough(0, 2 << 20),
        name="cut_far",
    )(left, right, *after)


def join_kernel(own_ref, left_ref, far_ref, right_ref, *refs):
    out = refs[-1]
    for j, ref in enumerate((own_ref, left_ref, far_ref, right_ref)):
        out[j * EXTRA : (j + 1) * EXTRA, :] = ref[ref.shape[0] - EXTRA :, :]


def join_extra(blocks, after):
    return pl.pallas_call(
        join_kernel,
        out_shape=jax.ShapeDtypeStruct((NX * EXTRA, blocks[0].shape[1]), BF),
        in_specs=whole(4) + anywhere(len(after)),
        out_specs=whole(1)[0],
        compiler_params=PARAMS,
        cost_estimate=rough(0, 1 << 19),
        name="join_extra",
    )(*blocks, *after)


def stack_kernel(count, *refs):
    rows, out = refs[0].shape[0], refs[-1]
    for j in range(count):
        out[j * rows : (j + 1) * rows, :] = refs[j][...]


def stack(arrays, after):
    rows, depth = arrays[0].shape
    return pl.pallas_call(
        functools.partial(stack_kernel, len(arrays)),
        out_shape=jax.ShapeDtypeStruct((len(arrays) * rows, depth), BF),
        in_specs=whole(len(arrays)) + anywhere(len(after)),
        out_specs=whole(1)[0],
        compiler_params=PARAMS,
        cost_estimate=rough(0, 4 << 20),
        name="stack",
    )(*arrays, *after)


def fold_kernel(left_a, minus, right_b, plus, left_out, right_out):
    half = left_a.shape[0]
    left_out[...] = (left_a[...].astype(F32) + minus[:half, :].astype(F32)).astype(BF)
    right_out[...] = (right_b[...].astype(F32) + plus[:half, :].astype(F32)).astype(BF)


def fold(left_a, minus, right_b, plus):
    return pl.pallas_call(
        fold_kernel,
        out_shape=[jax.ShapeDtypeStruct(left_a.shape, BF)] * 2,
        in_specs=whole(4),
        out_specs=whole(2),
        compiler_params=PARAMS,
        cost_estimate=rough(0, 4 << 20),
        name="fold",
    )(left_a, minus, right_b, plus)


def pair_kernel(a_ref, b_ref, *refs):
    refs[-1][...] = (a_ref[...].astype(F32) + b_ref[...].astype(F32)).astype(BF)


def pair_sum(a, b, after):
    return pl.pallas_call(
        pair_kernel,
        out_shape=jax.ShapeDtypeStruct(a.shape, BF),
        in_specs=whole(2) + anywhere(len(after)),
        out_specs=whole(1)[0],
        compiler_params=PARAMS,
        cost_estimate=rough(0, 4 << 20),
        name="pair_sum",
    )(a, b, *after)


def settle(own, terms, after):
    depth = own.shape[1]
    return pl.pallas_call(
        settle_kernel,
        out_shape=[jax.ShapeDtypeStruct((PIECE, depth), BF)] * NY,
        in_specs=whole(5) + anywhere(len(after)),
        out_specs=whole(NY),
        compiler_params=PARAMS,
        cost_estimate=rough(0, 5 << 20),
        name="settle",
    )(own, *terms, *after)


def merge_pick(counts, metas, line, pieces, after):
    depth = line.shape[1]
    return pl.pallas_call(
        pick_kernel,
        out_shape=[
            jax.ShapeDtypeStruct((3 * PIECE + EXTRA, depth), BF),
            jax.ShapeDtypeStruct((8, META), F32),
            jax.ShapeDtypeStruct((8, META), F32),
        ],
        in_specs=whole(6) + anywhere(len(after)),
        out_specs=whole(3),
        compiler_params=PARAMS,
        cost_estimate=rough(2 * 16 * 256 * depth, 2 << 20),
        name="merge_pick",
    )(counts, metas, line, *pieces, *after)


def plan_scatter(lanes, metas):
    shapes = [jax.ShapeDtypeStruct((SRC * 32, 8 * PIECE), BF)] * 2
    shapes += [jax.ShapeDtypeStruct((SRC * 16, META), BF)] * 2
    return pl.pallas_call(
        plan_kernel,
        out_shape=shapes,
        in_specs=whole(2),
        out_specs=whole(4),
        compiler_params=PARAMS,
        cost_estimate=rough(512 * 512 * 1024, 1 << 20),
        name="plan_scatter",
    )(lanes, metas)


def scatter_rows(own, plan, rows, after):
    depth = rows[0].shape[1]
    return pl.pallas_call(
        functools.partial(scatter_kernel, own, len(after)),
        out_shape=jax.ShapeDtypeStruct((SRC * 16, depth), BF),
        in_specs=whole(len(plan) + len(rows)) + anywhere(len(after)),
        out_specs=whole(1)[0],
        compiler_params=PARAMS,
        cost_estimate=rough(2 * 384 * 512 * depth, 5 << 20),
        name="scatter_rows",
    )(*plan, *rows, *after)


def merge(pieces, after):
    depth = pieces[0].shape[1]
    return pl.pallas_call(
        merge_kernel,
        out_shape=jax.ShapeDtypeStruct((3 * PIECE, depth), BF),
        in_specs=whole(3) + anywhere(len(after)),
        out_specs=whole(1)[0],
        compiler_params=PARAMS,
        cost_estimate=rough(0, 2 << 20),
        name="merge",
    )(*pieces, *after)


def deq_kernel(w_ref, s_ref, out_ref):
    rows, cols = w_ref.shape[1:]
    scales = s_ref[0]
    for r in range(rows // BLOCK):
        for c in range(cols // BLOCK):
            at = (0, slice(r * BLOCK, (r + 1) * BLOCK), slice(c * BLOCK, (c + 1) * BLOCK))
            out_ref[at] = (w_ref[at].astype(F32) * scales[r : r + 1, c : c + 1]).astype(BF)


def dequantize(weight, scale):
    count, rows, cols = weight.shape

    def block(array):
        return pl.BlockSpec((1,) + array.shape[1:], lambda i: (i, 0, 0))

    return pl.pallas_call(
        deq_kernel,
        grid=(count,),
        out_shape=jax.ShapeDtypeStruct(weight.shape, BF),
        in_specs=[block(weight), block(scale)],
        out_specs=block(weight),
        compiler_params=PARAMS,
        cost_estimate=rough(count * rows * cols, 4 * count * rows * cols),
        name="dequantize",
    )(weight, scale)


def silu(value):
    return value * (1.0 / (1.0 + jnp.exp(-value)))


def ffn_kernel(in_count, out_parts, skip, *refs):
    xs, (gate_w, up_w, down_w) = refs[:in_count], refs[in_count : in_count + 3]
    refs = refs[in_count + 3 + skip :]
    outs, (gate_acc, up_acc, hidden) = refs[: len(out_parts)], refs[len(out_parts) :]
    step = pl.program_id(0)

    @pl.when(step < STEPS)
    def _():
        x = jnp.concatenate([r[...] for r in xs], axis=0)
        gate = jnp.dot(x, gate_w[0], preferred_element_type=F32)
        up = jnp.dot(x, up_w[0], preferred_element_type=F32)

        @pl.when(step == 0)
        def _():
            gate_acc[...] = gate
            up_acc[...] = up

        @pl.when(step > 0)
        def _():
            gate_acc[...] += gate
            up_acc[...] += up

    @pl.when(step >= STEPS)
    def _():
        @pl.when(step == STEPS)
        def _():
            hidden[...] = (silu(gate_acc[...]) * up_acc[...]).astype(BF)

        result = jnp.dot(hidden[...], down_w[0], preferred_element_type=F32).astype(BF)
        for ref, parts in zip(outs, out_parts):
            at = 0
            for low, high in parts:
                ref[at : at + high - low, :] = result[low:high]
                at += high - low


def early(i):
    return jnp.minimum(i, STEPS - 1)


def late(i):
    return jnp.maximum(i - STEPS, 0)


def ffn(xs, out_parts, which, weights, after):
    gate_w, up_w, down_w = weights
    depth, units = gate_w.shape[1:]
    wide = depth // STEPS
    total = sum(rows for _, rows, _ in xs)
    out_rows = [sum(high - low for low, high in parts) for parts in out_parts]
    in_specs = [
        pl.BlockSpec((rows, wide), lambda i, place=place: (place, early(i))) for _, rows, place in xs
    ]
    in_specs += [pl.BlockSpec((1, wide, units), lambda i: (which, early(i), 0))] * 2
    in_specs += [pl.BlockSpec((1, units, wide), lambda i: (which, 0, late(i)))]
    return pl.pallas_call(
        functools.partial(ffn_kernel, len(xs), out_parts, len(after)),
        grid=(2 * STEPS,),
        out_shape=[jax.ShapeDtypeStruct((r, depth), BF) for r in out_rows],
        in_specs=in_specs + anywhere(len(after)),
        out_specs=[pl.BlockSpec((r, wide), lambda i: (0, late(i))) for r in out_rows],
        scratch_shapes=[
            pltpu.VMEM((total, units), F32),
            pltpu.VMEM((total, units), F32),
            pltpu.VMEM((total, units), BF),
        ],
        compiler_params=PARAMS,
        cost_estimate=rough(6 * total * units * depth, 4 * total * depth + 6 * units * depth),
        name="ffn",
    )(*[x for x, _, _ in xs], gate_w, up_w, down_w, *after)


def extra_kernel(skip, place_ref, own_in, other_in, gate_w, up_w, down_a, down_b, *refs):
    own_out, other_out, gate_acc, up_acc, hidden = refs[skip:]
    step = pl.program_id(0)
    units = gate_w.shape[2]

    @pl.when(step < 2 * STEPS)
    def _():
        x = jnp.concatenate([own_in[...], other_in[...]], axis=0)
        gate = jnp.dot(x, gate_w[0], preferred_element_type=F32)
        up = jnp.dot(x, up_w[0], preferred_element_type=F32)
        opening = (step == 0) | (step == STEPS)

        @pl.when(opening)
        def _():
            gate_acc[...] = gate
            up_acc[...] = up

        @pl.when(jnp.logical_not(opening))
        def _():
            gate_acc[...] += gate
            up_acc[...] += up

    for j in range(2):

        @pl.when(step == (j + 1) * STEPS - 1)
        def _(j=j):
            value = silu(gate_acc[...]) * up_acc[...]
            row = lax.broadcasted_iota(jnp.int32, value.shape, 0)
            keep = ((row & 1) == j) & (place_ref[2 + j] == 1)
            hidden[:, j * units : (j + 1) * units] = jnp.where(keep, value, 0.0).astype(BF)

    @pl.when(step >= 2 * STEPS)
    def _():
        down = jnp.concatenate([down_a[0], down_b[0]], axis=0)
        result = jnp.dot(hidden[...], down, preferred_element_type=F32).astype(BF)
        half = own_out.shape[0]
        own_out[...] = result[:half]
        other_out[...] = result[half:]


def extra_ffn(places, own, other, weights, after):
    gate_w, up_w, down_w = weights
    depth, units = gate_w.shape[1:]
    wide = depth // STEPS
    half = own.shape[0]

    def first(i):
        return jnp.where(i < 2 * STEPS, i & (STEPS - 1), STEPS - 1)

    def last(i):
        return jnp.maximum(i - 2 * STEPS, 0)

    def turn(i):
        return jnp.where(i < STEPS, 0, 1)

    rows_in = pl.BlockSpec((half, wide), lambda i, s: (0, first(i)))
    gate_in = pl.BlockSpec((1, wide, units), lambda i, s: (s[turn(i)], first(i), 0))
    rows_out = pl.BlockSpec((half, wide), lambda i, s: (0, last(i)))
    spec = pltpu.PrefetchScalarGridSpec(
        num_scalar_prefetch=1,
        grid=(3 * STEPS,),
        in_specs=[rows_in, rows_in, gate_in, gate_in]
        + [pl.BlockSpec((1, units, wide), lambda i, s, j=j: (s[j], 0, last(i))) for j in range(2)]
        + anywhere(len(after)),
        out_specs=[rows_out, rows_out],
        scratch_shapes=[
            pltpu.VMEM((2 * half, units), F32),
            pltpu.VMEM((2 * half, units), F32),
            pltpu.VMEM((2 * half, 2 * units), BF),
        ],
    )
    return pl.pallas_call(
        functools.partial(extra_kernel, len(after)),
        grid_spec=spec,
        out_shape=[jax.ShapeDtypeStruct((half, depth), BF)] * 2,
        compiler_params=PARAMS,
        cost_estimate=rough(20 * half * units * depth, 32 << 20),
        name="extra_ffn",
    )(places, own, other, gate_w, up_w, down_w, down_w, *after)


def add(*values):
    total = values[0].astype(F32)
    for value in values[1:]:
        total = total + value.astype(F32)
    return total.astype(BF)


def gather_line(own, after):
    pieces = [own] + [None] * (NZ - 1)
    up = down = own
    for step in range(1, NZ // 2 + 1):
        up = expert_move(up, dz=-1)
        pieces[step] = up
        if step < NZ // 2:
            down = expert_move(down, dz=1)
            pieces[NZ - step] = down
            up = relay([up], [after[step - 1]])[0]
    return pieces + [expert_move(piece, flip=True) for piece in pieces]


def scatter_line(own, other):
    arrived = expert_move(other, flip=True)

    def term(dz):
        return own[dz * 32 : dz * 32 + 32], arrived[dz * 32 : dz * 32 + 32]

    up = add(*term(NZ // 2))
    for dz in range(NZ // 2 - 1, 0, -1):
        up = add(expert_move(up, dz=1), *term(dz))
    down = add(*term(NZ // 2 + 1))
    for dz in range(NZ // 2 + 2, NZ):
        down = add(expert_move(down, dz=-1), *term(dz))
    return [expert_move(up, dz=1), expert_move(down, dz=-1), *term(0)]


def spread_dp(block, cut, after=()):
    left = dp_move(block, 1)
    right = dp_move(block, -1)
    far = cut_far(left, right, cut, after) if after else (left[:cut], right[cut:])
    return [block, left, right, dp_move(far[0], 1), dp_move(far[1], -1), *far]


def sum_dp_first(parts):
    minus, plus, left_a, right_b, own = parts
    got_minus = dp_move(minus, -1)
    got_plus = dp_move(plus, 1)
    left_a, right_b = fold(left_a, got_minus, right_b, got_plus)
    return left_a, got_minus, got_plus, right_b, own


def sum_dp_second(state, after):
    left_a, got_minus, got_plus, right_b, own = state
    got_left_a = dp_move(left_a, -1)
    got_right_b = dp_move(right_b, 1)
    return settle(own, (got_left_a, got_minus, got_plus, got_right_b), after), [got_left_a, got_right_b]


def per_device(
    tokens,
    routes,
    route_weight,
    gate_weight,
    up_weight,
    down_weight,
    gate_scale,
    up_scale,
    down_scale,
):
    rows, depth = tokens.shape
    top = routes.shape[1]
    experts = gate_weight.shape[0] * NY * NZ * NC
    all_rows = rows * NX * NY * NZ * NC
    place = lax.axis_index("expert")
    y, line = place // (NZ * NC), place % (NZ * NC)
    lane = jnp.arange(META, dtype=jnp.int32)

    named = (routes[:, :, None] == lane[None, None, :]).astype(F32)
    counts = jnp.broadcast_to(jnp.sum(named, axis=(0, 1))[None], (8, META))
    counts = sum([dp_move(counts, d) for d in range(1, NX)], counts)
    high = lax.reduce_precision(route_weight, 8, 7)
    low = lax.reduce_precision(route_weight - high, 8, 7)
    carried = jnp.concatenate(
        [
            tokens,
            routes.astype(BF),
            high.astype(BF),
            low.astype(BF),
            jnp.zeros((rows, META - 3 * top), BF),
            jnp.broadcast_to(counts[:1].astype(BF), (rows, META)),
        ],
        axis=1,
    )
    weights = (
        dequantize(gate_weight, gate_scale),
        dequantize(up_weight, up_scale),
        dequantize(down_weight, down_scale),
    )
    pieces = gather_line(carried, weights)

    lane_expert = ((((y + lane % NY) % NY) * (NZ * NC) + line) * 2 + lane // NY).astype(F32)
    lanes = jnp.broadcast_to(jnp.where(lane < 8, lane_expert, -1.0)[None], (8, META))
    near, *blocks, tokens_line, metas, counts = gather_rows(lanes, pieces, depth)
    near = spread_dp(near, PIECE)
    moved = [[expert_move(blocks[w * 3 + d - 1], dy=d) for d in range(1, NY)] for w in range(2)]

    first, hot, totals = merge_pick(counts, metas, tokens_line, moved[0], near[1:3])
    load_share = totals[0, :experts] * (experts / (all_rows * top))
    size = 3 * PIECE
    cuts = [(size + EXTRA) // 2, size - 4 * EXTRA]
    spreads = [spread_dp(first, cuts[0], [*moved[1], *near[3:5]])]
    spreads.append(spread_dp(merge(moved[1], spreads[0][5:]), cuts[1]))

    hot_id = hot[0:2, 0].astype(jnp.int32)
    places = jnp.concatenate([hot_id & 1, ((hot_id >> 1) == place).astype(jnp.int32)])
    spare = jnp.where(lane == 8, hot[0:1], jnp.where(lane == 9, hot[1:2], lanes))
    plan = plan_scatter(spare, metas)
    order = [spreads[0][i] for i in (0, 1, 4, 2)]
    extra = join_extra(order, [spreads[1][0], spreads[0][3]])
    extra = stack([extra] + [expert_move(extra, dy=d) for d in range(1, NY)], spreads[1][1:3])
    extra_other = expert_move(extra, flip=True)

    half = NY * PIECE // 2
    out_parts = [
        [(4 * half, 5 * half), (half, 2 * half)],
        [(5 * half, 6 * half), (2 * half, 3 * half)],
        [(0, half)],
        [(3 * half, 4 * half)],
        [(6 * half, 8 * half)],
    ]
    parts = []
    after = [extra, plan[0]]
    for which in range(2):
        cut, block = cuts[which], spreads[which]
        xs = [
            (near[1], PIECE, which),
            (block[1], size, 0),
            (near[2], PIECE, which),
            (block[2], size, 0),
            (near[3 + which], PIECE, 0),
            (block[3], cut, 0),
            (block[4], size - cut, 0),
            (near[0], PIECE, which),
            (block[0], size, 0),
        ]
        parts.append(list(ffn(xs, out_parts, which, weights, after)))
        if which == 0:
            parts[0][:2] = relay(parts[0][:2], [near[4], *spreads[1][3:5]])
            own, other = extra_ffn(places, extra, extra_other, weights, parts[0][:1])
            state = sum_dp_first(parts[0])
            extra = pair_sum(own, expert_move(other, flip=True), [])
            after = [own, state[0]]

    size = NX * EXTRA
    extra = add(
        extra[:size],
        *[expert_move(extra[d * size : (d + 1) * size], dy=-d) for d in range(1, NY)],
    )
    group, arrived = sum_dp_second(state, [extra])
    parts[1][:2] = relay(parts[1][:2], arrived)
    extra = add(
        extra[:EXTRA], *[dp_move(extra[d * EXTRA : (d + 1) * EXTRA], -d) for d in range(1, NX)]
    )
    returned = [group[0]] + [expert_move(group[d], dy=-d) for d in range(1, NY)]
    group, _ = sum_dp_second(sum_dp_first(parts[1]), returned)
    returned += [group[0]] + [expert_move(group[d], dy=-d) for d in range(1, NY)]
    other = scatter_rows(False, plan[:2], returned, [extra])
    own = scatter_rows(True, [*plan, extra], returned, [])
    terms = scatter_line(own, other)
    return add(*terms), load_share


def solution(mesh):
    in_specs = (
        P(("dp", "expert"), None),
        P(("dp", "expert"), None),
        P(("dp", "expert"), None),
        P("expert", None, "dp"),
        P("expert", None, "dp"),
        P("expert", "dp", None),
        P("expert", None, "dp"),
        P("expert", None, "dp"),
        P("expert", "dp", None),
    )
    out_specs = (P(("dp", "expert"), None), P())
    return jax.shard_map(
        per_device, mesh=mesh, in_specs=in_specs, out_specs=out_specs, check_vma=False
    )
```

```python
import functools

import jax
import jax.numpy as jnp
from jax import lax
from jax.experimental import pallas as pl
from jax.experimental.pallas import tpu as pltpu
from jax.sharding import PartitionSpec as P

BLOCK = 128
CAP = 3
NY, NZ, NC, NX = 4, 8, 2, 4
SRC = NZ * NC
PIECE = SRC * CAP
META = 128
COLS = 512
STEPS = 4
EXTRA = 2 * NZ
BF = jnp.bfloat16
F32 = jnp.float32
VMEM = 24 * 1024 * 1024


def expert_move(value, dy=0, dz=0, flip=False, xor_y=0):
    pairs = []
    for y in range(NY):
        for z in range(NZ):
            for c in range(NC):
                to_y = (y + dy) % NY ^ xor_y
                to_z = (z + dz) % NZ
                to_c = c ^ 1 if flip else c
                pairs.append(((y * NZ + z) * NC + c, (to_y * NZ + to_z) * NC + to_c))
    return lax.ppermute(value, "expert", pairs)


def dp_move(value, dx=0, xor_x=0):
    return lax.ppermute(value, "dp", [(x, (x + dx) % NX ^ xor_x) for x in range(NX)])


def slot_values(metas, lanes):
    tokens = metas.shape[0]
    found = jnp.zeros((tokens, META), F32)
    for k in range(8):
        found += jnp.where(metas[:, k : k + 1] == lanes, 1.0, 0.0)
    row = lax.broadcasted_iota(jnp.int32, (tokens, tokens), 0)
    col = lax.broadcasted_iota(jnp.int32, (tokens, tokens), 1)
    earlier = jnp.where(((row >> 5) == (col >> 5)) & (col < row), 1.0, 0.0).astype(BF)
    rank = jnp.dot(earlier, found.astype(BF), preferred_element_type=F32)
    return found * (rank + 1.0)


def slot_parts(slots):
    lane = (slots * 1366) >> 16
    rest = slots - lane * PIECE
    return lane, rest >> 4, rest & 15


def gather_kernel(lanes_ref, *refs):
    pieces, outs = refs[:SRC], refs[SRC : SRC + NY]
    line_ref, metas_ref, counts_ref = refs[SRC + NY :]
    tokens, slots = SRC * 32, 8 * PIECE
    depth = line_ref.shape[1]
    metas = jnp.concatenate([p[:, depth : depth + META] for p in pieces], axis=0).astype(F32)
    metas_ref[...] = metas
    counted = jnp.concatenate([p[:, depth + META :] for p in pieces], axis=0).astype(F32)
    total = jnp.sum(counted, axis=0, keepdims=True) * (1.0 / 32.0)
    counts_ref[...] = jnp.broadcast_to(total, (8, META))
    for d in (1, NY - 1):
        outs[d][:, depth:] = jnp.broadcast_to(total, (2 * PIECE, META)).astype(BF)
    values = slot_values(metas, lanes_ref[0:1, :])
    slot_lane, _, _ = slot_parts(lax.broadcasted_iota(jnp.int32, (slots, META), 0))
    spread = jnp.where(
        slot_lane == lax.broadcasted_iota(jnp.int32, (slots, META), 1), 1.0, 0.0
    ).astype(BF)
    picked = lax.dot_general(
        spread, values.astype(BF), (((1,), (1,)), ((), ())), preferred_element_type=F32
    )
    _, rank, source = slot_parts(lax.broadcasted_iota(jnp.int32, (slots, tokens), 0))
    token = lax.broadcasted_iota(jnp.int32, (slots, tokens), 1)
    choose = jnp.where(
        (picked == (rank + 1).astype(F32)) & (source == (token >> 5)), 1.0, 0.0
    ).astype(BF)
    for start in range(0, depth, COLS):
        block = jnp.concatenate([p[:, start : start + COLS] for p in pieces], axis=0)
        line_ref[:, start : start + COLS] = block[: tokens // 2]
        rows = jnp.dot(choose, block, preferred_element_type=F32).astype(BF)
        for which in range(2):
            for d in range(NY):
                low = (which * NY + d) * PIECE
                outs[d][which * PIECE : (which + 1) * PIECE, start : start + COLS] = rows[
                    low : low + PIECE
                ]


def relay_kernel(count, *refs):
    for in_ref, out_ref in zip(refs[:count], refs[-count:]):
        out_ref[...] = in_ref[...]


def cut_kernel(left_ref, right_ref, *refs):
    far_a, far_b = refs[-2:]
    far_a[...] = left_ref[: far_a.shape[0], :]
    far_b[...] = right_ref[far_a.shape[0] :, :]


def settle_kernel(own_ref, left_a, minus_ref, plus_ref, right_b, *refs):
    half = left_a.shape[0]
    for j, out in enumerate(refs[-NY:]):
        low = j * PIECE
        if low < half:
            left, right = left_a[low : low + PIECE, :], plus_ref[half + low : half + low + PIECE, :]
        else:
            at = low - half
            left, right = minus_ref[low : low + PIECE, :], right_b[at : at + PIECE, :]
        total = own_ref[low : low + PIECE, :].astype(F32) + left.astype(F32)
        out[...] = (total + right.astype(F32)).astype(BF)


def pick_kernel(counts_ref, far_counts_ref, metas_ref, line_ref, *refs):
    ins, (rows_ref, hot_ref, totals_ref) = refs[:2], refs[-3:]
    base = 4 * PIECE
    depth = rows_ref.shape[1]
    totals = counts_ref[0:1, :] + far_counts_ref[0:1, :]
    for j in range(2):
        rows_ref[2 * j * PIECE : 2 * (j + 1) * PIECE, :] = ins[j][:, :depth]
        totals = totals + ins[j][0:16, depth:].astype(F32)[0:1]
    totals_ref[...] = jnp.broadcast_to(totals, (8, META))
    tokens = NZ * 32
    every = lax.broadcasted_iota(jnp.int32, (1, META), 1).astype(F32)
    order = totals * META + (META - 1.0 - every)
    best = order == jnp.max(order, axis=1, keepdims=True)
    first = jnp.sum(jnp.where(best, every, 0.0), axis=1, keepdims=True)
    order = jnp.where(best, -1.0, order)
    best = order == jnp.max(order, axis=1, keepdims=True)
    second = jnp.sum(jnp.where(best, every, 0.0), axis=1, keepdims=True)
    row = lax.broadcasted_iota(jnp.int32, (8, META), 0)
    hot_ref[...] = jnp.where(row == 0, first, second)
    lanes = jnp.where(every == 0.0, first, jnp.where(every == 1.0, second, -1.0))
    values = slot_values(metas_ref[:tokens, :], lanes)
    slot = lax.broadcasted_iota(jnp.int32, (EXTRA, META), 0)
    spread = jnp.where(
        (slot & 1) == lax.broadcasted_iota(jnp.int32, (EXTRA, META), 1), 1.0, 0.0
    ).astype(BF)
    picked = lax.dot_general(
        spread, values.astype(BF), (((1,), (1,)), ((), ())), preferred_element_type=F32
    )
    slot = lax.broadcasted_iota(jnp.int32, (EXTRA, tokens), 0)
    token = lax.broadcasted_iota(jnp.int32, (EXTRA, tokens), 1)
    choose = jnp.where(
        (picked == CAP + 1.0) & ((slot >> 1) == (token >> 5)), 1.0, 0.0
    ).astype(BF)
    for start in range(0, depth, COLS):
        rows_ref[base:, start : start + COLS] = jnp.dot(
            choose, line_ref[:, start : start + COLS], preferred_element_type=F32
        ).astype(BF)


def plan_kernel(lanes_ref, metas_ref, high_ref, low_ref, extra_high_ref, extra_low_ref):
    tokens, slots = SRC * 32, 8 * PIECE
    own = tokens // 2
    lanes = lanes_ref[0:1, :]
    metas = metas_ref[...]
    values = slot_values(metas, lanes).astype(BF)
    high = jnp.zeros((tokens, META), F32)
    low = jnp.zeros((tokens, META), F32)
    for k in range(8):
        match = metas[:, k : k + 1] == lanes
        high += jnp.where(match, metas[:, 8 + k : 9 + k], 0.0)
        low += jnp.where(match, metas[:, 16 + k : 17 + k], 0.0)
    high, low = high.astype(BF), low.astype(BF)
    slot_lane, _, _ = slot_parts(lax.broadcasted_iota(jnp.int32, (META, slots), 1))
    spread = jnp.where(
        slot_lane == lax.broadcasted_iota(jnp.int32, (META, slots), 0), 1.0, 0.0
    ).astype(BF)
    picked = jnp.dot(values, spread, preferred_element_type=F32)
    _, rank, source = slot_parts(lax.broadcasted_iota(jnp.int32, (tokens, slots), 1))
    token = lax.broadcasted_iota(jnp.int32, (tokens, slots), 0)
    there = (picked == (rank + 1).astype(F32)) & (source == (token >> 5))
    high_at = jnp.dot(high, spread, preferred_element_type=F32)
    low_at = jnp.dot(low, spread, preferred_element_type=F32)
    high_ref[...] = jnp.where(there, high_at, 0.0).astype(BF)
    low_ref[...] = jnp.where(there, low_at, 0.0).astype(BF)
    slot = lax.broadcasted_iota(jnp.int32, (META, META), 1)
    from_lane = lax.broadcasted_iota(jnp.int32, (META, META), 0)
    spread = jnp.where((from_lane == 8 + (slot & 1)) & (slot < EXTRA), 1.0, 0.0).astype(BF)
    picked = jnp.dot(values[:own], spread, preferred_element_type=F32)
    slot = lax.broadcasted_iota(jnp.int32, (own, META), 1)
    token = lax.broadcasted_iota(jnp.int32, (own, META), 0)
    there = (picked == CAP + 1.0) & ((slot >> 1) == (token >> 5))
    high_at = jnp.dot(high[:own], spread, preferred_element_type=F32)
    low_at = jnp.dot(low[:own], spread, preferred_element_type=F32)
    extra_high_ref[...] = jnp.where(there, high_at, 0.0).astype(BF)
    extra_low_ref[...] = jnp.where(there, low_at, 0.0).astype(BF)


def scatter_kernel(own, skip, high_ref, low_ref, *refs):
    refs, out_ref = refs[: len(refs) - 1 - skip], refs[-1]
    extras, rows_in = refs[:-8], refs[-8:]
    half, depth = out_ref.shape
    at = 0 if own else half
    high, low = high_ref[at : at + half, :], low_ref[at : at + half, :]
    for start in range(0, depth, COLS):
        block = jnp.concatenate([r[:, start : start + COLS] for r in rows_in], axis=0)
        sums = jnp.dot(high, block, preferred_element_type=F32)
        sums += jnp.dot(low, block, preferred_element_type=F32)
        if own:
            extra_high, extra_low, extra_ref = extras
            extra = jnp.concatenate(
                [extra_ref[:, start : start + COLS], jnp.zeros((META - EXTRA, COLS), BF)], axis=0
            )
            sums += jnp.dot(extra_high[...], extra, preferred_element_type=F32)
            sums += jnp.dot(extra_low[...], extra, preferred_element_type=F32)
        out_ref[:, start : start + COLS] = sums.astype(BF)


def whole(count):
    return [pl.BlockSpec(memory_space=pltpu.VMEM)] * count


def anywhere(count):
    return [pl.BlockSpec(memory_space=pl.ANY)] * count


def rough(flops, size):
    return pl.CostEstimate(flops=flops // 64, bytes_accessed=size // 64, transcendentals=0)


PARAMS = pltpu.CompilerParams(vmem_limit_bytes=VMEM)


def gather_rows(lanes, pieces, depth):
    shapes = [
        jax.ShapeDtypeStruct((2 * PIECE, depth + (META if d in (1, NY - 1) else 0)), BF)
        for d in range(NY)
    ]
    shapes += [
        jax.ShapeDtypeStruct((SRC * 16, depth), BF),
        jax.ShapeDtypeStruct((SRC * 32, META), F32),
        jax.ShapeDtypeStruct((8, META), F32),
    ]
    return pl.pallas_call(
        gather_kernel,
        out_shape=shapes,
        in_specs=whole(1) + [pl.BlockSpec(pieces[0].shape, lambda: (0, 0))] * SRC,
        out_specs=whole(7),
        compiler_params=PARAMS,
        cost_estimate=rough(2 * 384 * 512 * depth, 7 << 20),
        name="gather_rows",
    )(lanes, *pieces)


def relay(arrays, after):
    count = len(arrays)
    return pl.pallas_call(
        functools.partial(relay_kernel, count),
        out_shape=[jax.ShapeDtypeStruct(a.shape, a.dtype) for a in arrays],
        in_specs=whole(count) + anywhere(len(after)),
        out_specs=whole(count),
        compiler_params=PARAMS,
        cost_estimate=rough(0, 1 << 19),
        name="relay",
    )(*arrays, *after)


def cut_far(left, right, cut, after):
    rows, depth = left.shape
    return pl.pallas_call(
        cut_kernel,
        out_shape=[jax.ShapeDtypeStruct((r, depth), BF) for r in (cut, rows - cut)],
        in_specs=whole(2) + anywhere(len(after)),
        out_specs=whole(2),
        compiler_params=PARAMS,
        cost_estimate=rough(0, 2 << 20),
        name="cut_far",
    )(left, right, *after)


def join_kernel(own_ref, left_ref, far_ref, right_ref, *refs):
    out = refs[-1]
    for j, ref in enumerate((own_ref, left_ref, far_ref, right_ref)):
        out[j * EXTRA : (j + 1) * EXTRA, :] = ref[ref.shape[0] - EXTRA :, :]


def join_extra(blocks, after):
    return pl.pallas_call(
        join_kernel,
        out_shape=jax.ShapeDtypeStruct((NX * EXTRA, blocks[0].shape[1]), BF),
        in_specs=whole(4) + anywhere(len(after)),
        out_specs=whole(1)[0],
        compiler_params=PARAMS,
        cost_estimate=rough(0, 1 << 19),
        name="join_extra",
    )(*blocks, *after)


def stack_kernel(count, *refs):
    rows, out = refs[0].shape[0], refs[-1]
    for j in range(count):
        out[j * rows : (j + 1) * rows, :] = refs[j][...]


def stack(arrays, after):
    rows, depth = arrays[0].shape
    return pl.pallas_call(
        functools.partial(stack_kernel, len(arrays)),
        out_shape=jax.ShapeDtypeStruct((len(arrays) * rows, depth), BF),
        in_specs=whole(len(arrays)) + anywhere(len(after)),
        out_specs=whole(1)[0],
        compiler_params=PARAMS,
        cost_estimate=rough(0, 4 << 20),
        name="stack",
    )(*arrays, *after)


def fold_kernel(left_a, minus, right_b, plus, left_out, right_out):
    half = left_a.shape[0]
    left_out[...] = (left_a[...].astype(F32) + minus[:half, :].astype(F32)).astype(BF)
    right_out[...] = (right_b[...].astype(F32) + plus[:half, :].astype(F32)).astype(BF)


def fold(left_a, minus, right_b, plus):
    return pl.pallas_call(
        fold_kernel,
        out_shape=[jax.ShapeDtypeStruct(left_a.shape, BF)] * 2,
        in_specs=whole(4),
        out_specs=whole(2),
        compiler_params=PARAMS,
        cost_estimate=rough(0, 4 << 20),
        name="fold",
    )(left_a, minus, right_b, plus)


def pair_kernel(a_ref, b_ref, *refs):
    refs[-1][...] = (a_ref[...].astype(F32) + b_ref[...].astype(F32)).astype(BF)


def pair_sum(a, b, after):
    return pl.pallas_call(
        pair_kernel,
        out_shape=jax.ShapeDtypeStruct(a.shape, BF),
        in_specs=whole(2) + anywhere(len(after)),
        out_specs=whole(1)[0],
        compiler_params=PARAMS,
        cost_estimate=rough(0, 4 << 20),
        name="pair_sum",
    )(a, b, *after)


def settle(own, terms, after):
    depth = own.shape[1]
    return pl.pallas_call(
        settle_kernel,
        out_shape=[jax.ShapeDtypeStruct((PIECE, depth), BF)] * NY,
        in_specs=whole(5) + anywhere(len(after)),
        out_specs=whole(NY),
        compiler_params=PARAMS,
        cost_estimate=rough(0, 5 << 20),
        name="settle",
    )(own, *terms, *after)


def merge_pick(counts, far_counts, metas, line, pieces, after):
    depth = line.shape[1]
    return pl.pallas_call(
        pick_kernel,
        out_shape=[
            jax.ShapeDtypeStruct((4 * PIECE + EXTRA, depth), BF),
            jax.ShapeDtypeStruct((8, META), F32),
            jax.ShapeDtypeStruct((8, META), F32),
        ],
        in_specs=whole(6) + anywhere(len(after)),
        out_specs=whole(3),
        compiler_params=PARAMS,
        cost_estimate=rough(2 * 16 * 256 * depth, 2 << 20),
        name="merge_pick",
    )(counts, far_counts, metas, line, *pieces, *after)


def plan_scatter(lanes, metas):
    shapes = [jax.ShapeDtypeStruct((SRC * 32, 8 * PIECE), BF)] * 2
    shapes += [jax.ShapeDtypeStruct((SRC * 16, META), BF)] * 2
    return pl.pallas_call(
        plan_kernel,
        out_shape=shapes,
        in_specs=whole(2),
        out_specs=whole(4),
        compiler_params=PARAMS,
        cost_estimate=rough(512 * 512 * 1024, 1 << 20),
        name="plan_scatter",
    )(lanes, metas)


def scatter_rows(own, plan, rows, after):
    depth = rows[0].shape[1]
    return pl.pallas_call(
        functools.partial(scatter_kernel, own, len(after)),
        out_shape=jax.ShapeDtypeStruct((SRC * 16, depth), BF),
        in_specs=whole(len(plan) + len(rows)) + anywhere(len(after)),
        out_specs=whole(1)[0],
        compiler_params=PARAMS,
        cost_estimate=rough(2 * 384 * 512 * depth, 5 << 20),
        name="scatter_rows",
    )(*plan, *rows, *after)


def deq_kernel(w_ref, s_ref, *refs):
    out_ref = refs[-1]
    rows, cols = w_ref.shape[1:]
    scales = s_ref[0]
    for r in range(rows // BLOCK):
        for c in range(cols // BLOCK):
            at = (0, slice(r * BLOCK, (r + 1) * BLOCK), slice(c * BLOCK, (c + 1) * BLOCK))
            out_ref[at] = (w_ref[at].astype(F32) * scales[r : r + 1, c : c + 1]).astype(BF)


def dequantize(weight, scale, after):
    count, rows, cols = weight.shape

    def block(array):
        return pl.BlockSpec((1,) + array.shape[1:], lambda i: (i, 0, 0))

    return pl.pallas_call(
        deq_kernel,
        grid=(count,),
        out_shape=jax.ShapeDtypeStruct(weight.shape, BF),
        in_specs=[block(weight), block(scale)] + anywhere(len(after)),
        out_specs=block(weight),
        compiler_params=PARAMS,
        cost_estimate=rough(count * rows * cols, 4 * count * rows * cols),
        name="dequantize",
    )(weight, scale, *after)


def silu(value):
    return value * (1.0 / (1.0 + jnp.exp(-value)))


def ffn_kernel(in_count, out_parts, skip, *refs):
    xs, (gate_w, up_w, down_w) = refs[:in_count], refs[in_count : in_count + 3]
    refs = refs[in_count + 3 + skip :]
    outs, (gate_acc, up_acc, hidden) = refs[: len(out_parts)], refs[len(out_parts) :]
    step = pl.program_id(0)

    @pl.when(step < STEPS)
    def _():
        x = jnp.concatenate([r[...] for r in xs], axis=0)
        gate = jnp.dot(x, gate_w[0], preferred_element_type=F32)
        up = jnp.dot(x, up_w[0], preferred_element_type=F32)

        @pl.when(step == 0)
        def _():
            gate_acc[...] = gate
            up_acc[...] = up

        @pl.when(step > 0)
        def _():
            gate_acc[...] += gate
            up_acc[...] += up

    @pl.when(step >= STEPS)
    def _():
        @pl.when(step == STEPS)
        def _():
            hidden[...] = (silu(gate_acc[...]) * up_acc[...]).astype(BF)

        result = jnp.dot(hidden[...], down_w[0], preferred_element_type=F32).astype(BF)
        for ref, parts in zip(outs, out_parts):
            at = 0
            for low, high in parts:
                ref[at : at + high - low, :] = result[low:high]
                at += high - low


def early(i):
    return jnp.minimum(i, STEPS - 1)


def late(i):
    return jnp.maximum(i - STEPS, 0)


def ffn(xs, out_parts, which, weights, after):
    gate_w, up_w, down_w = weights
    depth, units = gate_w.shape[1:]
    wide = depth // STEPS
    total = sum(rows for _, rows, _ in xs)
    out_rows = [sum(high - low for low, high in parts) for parts in out_parts]
    in_specs = [
        pl.BlockSpec((rows, wide), lambda i, place=place: (place, early(i))) for _, rows, place in xs
    ]
    in_specs += [pl.BlockSpec((1, wide, units), lambda i: (which, early(i), 0))] * 2
    in_specs += [pl.BlockSpec((1, units, wide), lambda i: (which, 0, late(i)))]
    return pl.pallas_call(
        functools.partial(ffn_kernel, len(xs), out_parts, len(after)),
        grid=(2 * STEPS,),
        out_shape=[jax.ShapeDtypeStruct((r, depth), BF) for r in out_rows],
        in_specs=in_specs + anywhere(len(after)),
        out_specs=[pl.BlockSpec((r, wide), lambda i: (0, late(i))) for r in out_rows],
        scratch_shapes=[
            pltpu.VMEM((total, units), F32),
            pltpu.VMEM((total, units), F32),
            pltpu.VMEM((total, units), BF),
        ],
        compiler_params=PARAMS,
        cost_estimate=rough(6 * total * units * depth, 4 * total * depth + 6 * units * depth),
        name="ffn",
    )(*[x for x, _, _ in xs], gate_w, up_w, down_w, *after)


def extra_kernel(skip, place_ref, own_in, other_in, gate_w, up_w, down_a, down_b, *refs):
    own_out, other_out, gate_acc, up_acc, hidden = refs[skip:]
    step = pl.program_id(0)
    units = gate_w.shape[2]

    @pl.when(step < 2 * STEPS)
    def _():
        x = jnp.concatenate([own_in[...], other_in[...]], axis=0)
        gate = jnp.dot(x, gate_w[0], preferred_element_type=F32)
        up = jnp.dot(x, up_w[0], preferred_element_type=F32)
        opening = (step == 0) | (step == STEPS)

        @pl.when(opening)
        def _():
            gate_acc[...] = gate
            up_acc[...] = up

        @pl.when(jnp.logical_not(opening))
        def _():
            gate_acc[...] += gate
            up_acc[...] += up

    for j in range(2):

        @pl.when(step == (j + 1) * STEPS - 1)
        def _(j=j):
            value = silu(gate_acc[...]) * up_acc[...]
            row = lax.broadcasted_iota(jnp.int32, value.shape, 0)
            keep = ((row & 1) == j) & (place_ref[2 + j] == 1)
            hidden[:, j * units : (j + 1) * units] = jnp.where(keep, value, 0.0).astype(BF)

    @pl.when(step >= 2 * STEPS)
    def _():
        down = jnp.concatenate([down_a[0], down_b[0]], axis=0)
        result = jnp.dot(hidden[...], down, preferred_element_type=F32).astype(BF)
        half = own_out.shape[0]
        own_out[...] = result[:half]
        other_out[...] = result[half:]


def extra_ffn(places, own, other, weights, after):
    gate_w, up_w, down_w = weights
    depth, units = gate_w.shape[1:]
    wide = depth // STEPS
    half = own.shape[0]

    def first(i):
        return jnp.where(i < 2 * STEPS, i & (STEPS - 1), STEPS - 1)

    def last(i):
        return jnp.maximum(i - 2 * STEPS, 0)

    def turn(i):
        return jnp.where(i < STEPS, 0, 1)

    rows_in = pl.BlockSpec((half, wide), lambda i, s: (0, first(i)))
    gate_in = pl.BlockSpec((1, wide, units), lambda i, s: (s[turn(i)], first(i), 0))
    rows_out = pl.BlockSpec((half, wide), lambda i, s: (0, last(i)))
    spec = pltpu.PrefetchScalarGridSpec(
        num_scalar_prefetch=1,
        grid=(3 * STEPS,),
        in_specs=[rows_in, rows_in, gate_in, gate_in]
        + [pl.BlockSpec((1, units, wide), lambda i, s, j=j: (s[j], 0, last(i))) for j in range(2)]
        + anywhere(len(after)),
        out_specs=[rows_out, rows_out],
        scratch_shapes=[
            pltpu.VMEM((2 * half, units), F32),
            pltpu.VMEM((2 * half, units), F32),
            pltpu.VMEM((2 * half, 2 * units), BF),
        ],
    )
    return pl.pallas_call(
        functools.partial(extra_kernel, len(after)),
        grid_spec=spec,
        out_shape=[jax.ShapeDtypeStruct((half, depth), BF)] * 2,
        compiler_params=PARAMS,
        cost_estimate=rough(20 * half * units * depth, 32 << 20),
        name="extra_ffn",
    )(places, own, other, gate_w, up_w, down_w, down_w, *after)


def add(*values):
    total = values[0].astype(F32)
    for value in values[1:]:
        total = total + value.astype(F32)
    return total.astype(BF)


def gather_line(own):
    pieces = [own] + [None] * (NZ - 1)
    up = down = own
    for step in range(1, NZ // 2 + 1):
        up = expert_move(up, dz=-1)
        pieces[step] = up
        if step < NZ // 2:
            down = expert_move(down, dz=1)
            pieces[NZ - step] = down
    return pieces + [expert_move(piece, flip=True) for piece in pieces]


def scatter_line(own, other):
    arrived = expert_move(other, flip=True)

    def term(dz):
        return own[dz * 32 : dz * 32 + 32], arrived[dz * 32 : dz * 32 + 32]

    up = add(*term(NZ // 2))
    for dz in range(NZ // 2 - 1, 0, -1):
        up = add(expert_move(up, dz=1), *term(dz))
    down = add(*term(NZ // 2 + 1))
    for dz in range(NZ // 2 + 2, NZ):
        down = add(expert_move(down, dz=-1), *term(dz))
    return [expert_move(up, dz=1), expert_move(down, dz=-1), *term(0)]


def spread_dp(block, cut, after=()):
    left = dp_move(block, 1)
    right = dp_move(block, -1)
    far = cut_far(left, right, cut, after) if after else (left[:cut], right[cut:])
    return [block, left, right, dp_move(far[0], 1), dp_move(far[1], -1), *far]


def sum_dp_first(parts):
    minus, plus, left_a, right_b, own = parts
    got_minus = dp_move(minus, -1)
    got_plus = dp_move(plus, 1)
    left_a, right_b = fold(left_a, got_minus, right_b, got_plus)
    return left_a, got_minus, got_plus, right_b, own


def sum_dp_second(state, after):
    left_a, got_minus, got_plus, right_b, own = state
    got_left_a = dp_move(left_a, -1)
    got_right_b = dp_move(right_b, 1)
    return settle(own, (got_left_a, got_minus, got_plus, got_right_b), after), [got_left_a, got_right_b]


def return_rows(group):
    own, one, three, two = group
    return [own, expert_move(one, dy=-1), expert_move(two, dy=-2), expert_move(three, dy=-3)]


def per_device(
    tokens,
    routes,
    route_weight,
    gate_weight,
    up_weight,
    down_weight,
    gate_scale,
    up_scale,
    down_scale,
):
    rows, depth = tokens.shape
    top = routes.shape[1]
    experts = gate_weight.shape[0] * NY * NZ * NC
    all_rows = rows * NX * NY * NZ * NC
    place = lax.axis_index("expert")
    y, line = place // (NZ * NC), place % (NZ * NC)
    lane = jnp.arange(META, dtype=jnp.int32)

    named = (routes[:, :, None] == lane[None, None, :]).astype(F32)
    counts = jnp.broadcast_to(jnp.sum(named, axis=(0, 1))[None], (8, META))
    counts = sum([dp_move(counts, d) for d in range(1, NX)], counts)
    high = lax.reduce_precision(route_weight, 8, 7)
    low = lax.reduce_precision(route_weight - high, 8, 7)
    carried = jnp.concatenate(
        [
            tokens,
            routes.astype(BF),
            high.astype(BF),
            low.astype(BF),
            jnp.zeros((rows, META - 3 * top), BF),
            jnp.broadcast_to(counts[:1].astype(BF), (rows, META)),
        ],
        axis=1,
    )
    pieces = gather_line(carried)

    lane_expert = ((((y + lane % NY) % NY) * (NZ * NC) + line) * 2 + lane // NY).astype(F32)
    lanes = jnp.broadcast_to(jnp.where(lane < 8, lane_expert, -1.0)[None], (8, META))
    near, *blocks, tokens_line, metas, counts = gather_rows(lanes, pieces, depth)
    near = spread_dp(near, PIECE)
    one, two, three = [expert_move(blocks[d - 1], dy=d) for d in range(1, NY)]
    far_counts = expert_move(counts, dy=2)
    weights = [
        dequantize(weight, scale, [metas])
        for weight, scale in (
            (gate_weight, gate_scale),
            (up_weight, up_scale),
            (down_weight, down_scale),
        )
    ]
    first, hot, totals = merge_pick(
        counts, far_counts, metas, tokens_line, [one, three], [*near[1:3], *weights]
    )
    load_share = totals[0, :experts] * (experts / (all_rows * top))
    first = spread_dp(first, 2 * PIECE, [two])
    second = spread_dp(relay([two], [first[5], *near[3:5]])[0], PIECE)

    hot_id = hot[0:2, 0].astype(jnp.int32)
    places = jnp.concatenate([hot_id & 1, ((hot_id >> 1) == place).astype(jnp.int32)])
    spare = jnp.where(lane == 8, hot[0:1], jnp.where(lane == 9, hot[1:2], lanes))
    plan = plan_scatter(spare, metas)
    extra = join_extra([first[i] for i in (0, 1, 4, 2)], [second[0], first[3]])
    extra = stack([extra] + [expert_move(extra, dy=d) for d in range(1, NY)], second[1:3])
    extra_other = expert_move(extra, flip=True)

    half = NY * PIECE // 2
    out_parts = [
        [(4 * half, 5 * half), (half, 2 * half)],
        [(5 * half, 6 * half), (2 * half, 3 * half)],
        [(0, half)],
        [(3 * half, 4 * half)],
        [(6 * half, 8 * half)],
    ]
    parts = []
    after = [extra, plan[0]]
    for which in range(2):
        sides = [
            [near[i], which, first[i], which, first[i], 2 + which, second[i], which]
            for i in (1, 2, 0)
        ]
        sides.insert(2, [near[3 + which], 0, first[3], which, first[4], which, second[3 + which], 0])
        xs = [(side[i], PIECE, side[i + 1]) for side in sides for i in range(0, 8, 2)]
        parts.append(list(ffn(xs, out_parts, which, weights, after)))
        if which == 0:
            parts[0][:2] = relay(parts[0][:2], second[3:5])
            own, other = extra_ffn(places, extra, extra_other, weights, parts[0][:1])
            state = sum_dp_first(parts[0])
            extra = pair_sum(own, expert_move(other, flip=True), [])
            after = [own, state[0]]

    size = NX * EXTRA
    extra = add(
        extra[:size],
        *[expert_move(extra[d * size : (d + 1) * size], dy=-d) for d in range(1, NY)],
    )
    group, arrived = sum_dp_second(state, [extra])
    parts[1][:2] = relay(parts[1][:2], arrived)
    extra = add(
        extra[:EXTRA], *[dp_move(extra[d * EXTRA : (d + 1) * EXTRA], -d) for d in range(1, NX)]
    )
    returned = return_rows(group)
    group, _ = sum_dp_second(sum_dp_first(parts[1]), returned)
    returned += return_rows(group)
    other = scatter_rows(False, plan[:2], returned, [extra])
    own = scatter_rows(True, [*plan, extra], returned, [])
    terms = scatter_line(own, other)
    return add(*terms), load_share


def solution(mesh):
    in_specs = (
        P(("dp", "expert"), None),
        P(("dp", "expert"), None),
        P(("dp", "expert"), None),
        P("expert", None, "dp"),
        P("expert", None, "dp"),
        P("expert", "dp", None),
        P("expert", None, "dp"),
        P("expert", None, "dp"),
        P("expert", "dp", None),
    )
    out_specs = (P(("dp", "expert"), None), P())
    return jax.shard_map(
        per_device, mesh=mesh, in_specs=in_specs, out_specs=out_specs, check_vma=False
    )
```

```python
import functools

import jax
import jax.numpy as jnp
from jax import lax
from jax.experimental import pallas as pl
from jax.experimental.pallas import tpu as pltpu
from jax.sharding import PartitionSpec as P

BLOCK = 128
CAP = 3
NY, NZ, NC, NX = 4, 8, 2, 4
SRC = NZ * NC
PIECE = SRC * CAP
META = 128
COLS = 512
STEPS = 4
EXTRA = 2 * NZ
BF = jnp.bfloat16
F32 = jnp.float32
VMEM = 24 * 1024 * 1024


def expert_move(value, dy=0, dz=0, flip=False, xor_y=0):
    pairs = []
    for y in range(NY):
        for z in range(NZ):
            for c in range(NC):
                to_y = (y + dy) % NY ^ xor_y
                to_z = (z + dz) % NZ
                to_c = c ^ 1 if flip else c
                pairs.append(((y * NZ + z) * NC + c, (to_y * NZ + to_z) * NC + to_c))
    return lax.ppermute(value, "expert", pairs)


def dp_move(value, dx=0, xor_x=0):
    return lax.ppermute(value, "dp", [(x, (x + dx) % NX ^ xor_x) for x in range(NX)])


def slot_values(metas, lanes):
    tokens = metas.shape[0]
    found = jnp.zeros((tokens, META), F32)
    for k in range(8):
        found += jnp.where(metas[:, k : k + 1] == lanes, 1.0, 0.0)
    row = lax.broadcasted_iota(jnp.int32, (tokens, tokens), 0)
    col = lax.broadcasted_iota(jnp.int32, (tokens, tokens), 1)
    earlier = jnp.where(((row >> 5) == (col >> 5)) & (col < row), 1.0, 0.0).astype(BF)
    rank = jnp.dot(earlier, found.astype(BF), preferred_element_type=F32)
    return found * (rank + 1.0)


def slot_parts(slots):
    lane = (slots * 1366) >> 16
    rest = slots - lane * PIECE
    return lane, rest >> 4, rest & 15


def gather_kernel(lanes_ref, *refs):
    pieces, outs = refs[:SRC], refs[SRC : SRC + NY]
    line_ref, metas_ref, counts_ref = refs[SRC + NY :]
    tokens, slots = SRC * 32, 8 * PIECE
    depth = line_ref.shape[1]
    metas = jnp.concatenate([p[:, depth : depth + META] for p in pieces], axis=0).astype(F32)
    metas_ref[...] = metas
    counted = jnp.concatenate([p[:, depth + META :] for p in pieces], axis=0).astype(F32)
    total = jnp.sum(counted, axis=0, keepdims=True) * (1.0 / 32.0)
    counts_ref[...] = jnp.broadcast_to(total, (8, META))
    for d in range(1, NY):
        outs[d][:, depth:] = jnp.broadcast_to(total, (2 * PIECE, META)).astype(BF)
    values = slot_values(metas, lanes_ref[0:1, :])
    slot_lane, _, _ = slot_parts(lax.broadcasted_iota(jnp.int32, (slots, META), 0))
    spread = jnp.where(
        slot_lane == lax.broadcasted_iota(jnp.int32, (slots, META), 1), 1.0, 0.0
    ).astype(BF)
    picked = lax.dot_general(
        spread, values.astype(BF), (((1,), (1,)), ((), ())), preferred_element_type=F32
    )
    _, rank, source = slot_parts(lax.broadcasted_iota(jnp.int32, (slots, tokens), 0))
    token = lax.broadcasted_iota(jnp.int32, (slots, tokens), 1)
    choose = jnp.where(
        (picked == (rank + 1).astype(F32)) & (source == (token >> 5)), 1.0, 0.0
    ).astype(BF)
    for start in range(0, depth, COLS):
        block = jnp.concatenate([p[:, start : start + COLS] for p in pieces], axis=0)
        line_ref[:, start : start + COLS] = block[: tokens // 2]
        rows = jnp.dot(choose, block, preferred_element_type=F32).astype(BF)
        for which in range(2):
            for d in range(NY):
                low = (which * NY + d) * PIECE
                outs[d][which * PIECE : (which + 1) * PIECE, start : start + COLS] = rows[
                    low : low + PIECE
                ]


def relay_kernel(count, *refs):
    for in_ref, out_ref in zip(refs[:count], refs[-count:]):
        out_ref[...] = in_ref[...]


def cut_kernel(left_ref, right_ref, *refs):
    far_a, far_b = refs[-2:]
    far_a[...] = left_ref[: far_a.shape[0], :]
    far_b[...] = right_ref[far_a.shape[0] :, :]


def settle_kernel(own_ref, left_a, minus_ref, plus_ref, right_b, *refs):
    half = left_a.shape[0]
    for j, out in enumerate(refs[-NY:]):
        low = j * PIECE
        if low < half:
            left, right = left_a[low : low + PIECE, :], plus_ref[half + low : half + low + PIECE, :]
        else:
            at = low - half
            left, right = minus_ref[low : low + PIECE, :], right_b[at : at + PIECE, :]
        total = own_ref[low : low + PIECE, :].astype(F32) + left.astype(F32)
        out[...] = (total + right.astype(F32)).astype(BF)


def pick_kernel(counts_ref, metas_ref, line_ref, *refs):
    two_ref, one_ref, three_ref = refs[:3]
    rows_ref, hot_ref, totals_ref = refs[-3:]
    depth = rows_ref.shape[1]
    totals = counts_ref[0:1, :] + two_ref[0:16, depth:].astype(F32)[0:1]
    for ref in (one_ref, three_ref):
        totals = totals + ref[0:16, depth:].astype(F32)[0:1]
    totals_ref[...] = jnp.broadcast_to(totals, (8, META))
    tokens = NZ * 32
    every = lax.broadcasted_iota(jnp.int32, (1, META), 1).astype(F32)
    order = totals * META + (META - 1.0 - every)
    best = order == jnp.max(order, axis=1, keepdims=True)
    first = jnp.sum(jnp.where(best, every, 0.0), axis=1, keepdims=True)
    order = jnp.where(best, -1.0, order)
    best = order == jnp.max(order, axis=1, keepdims=True)
    second = jnp.sum(jnp.where(best, every, 0.0), axis=1, keepdims=True)
    row = lax.broadcasted_iota(jnp.int32, (8, META), 0)
    hot_ref[...] = jnp.where(row == 0, first, second)
    lanes = jnp.where(every == 0.0, first, jnp.where(every == 1.0, second, -1.0))
    values = slot_values(metas_ref[:tokens, :], lanes)
    slot = lax.broadcasted_iota(jnp.int32, (EXTRA, META), 0)
    spread = jnp.where(
        (slot & 1) == lax.broadcasted_iota(jnp.int32, (EXTRA, META), 1), 1.0, 0.0
    ).astype(BF)
    picked = lax.dot_general(
        spread, values.astype(BF), (((1,), (1,)), ((), ())), preferred_element_type=F32
    )
    slot = lax.broadcasted_iota(jnp.int32, (EXTRA, tokens), 0)
    token = lax.broadcasted_iota(jnp.int32, (EXTRA, tokens), 1)
    choose = jnp.where(
        (picked == CAP + 1.0) & ((slot >> 1) == (token >> 5)), 1.0, 0.0
    ).astype(BF)
    for start in range(0, depth, COLS):
        rows_ref[:, start : start + COLS] = jnp.dot(
            choose, line_ref[:, start : start + COLS], preferred_element_type=F32
        ).astype(BF)


def plan_kernel(lanes_ref, metas_ref, high_ref, low_ref, extra_high_ref, extra_low_ref):
    tokens, slots = SRC * 32, 8 * PIECE
    own = tokens // 2
    lanes = lanes_ref[0:1, :]
    metas = metas_ref[...]
    values = slot_values(metas, lanes).astype(BF)
    high = jnp.zeros((tokens, META), F32)
    low = jnp.zeros((tokens, META), F32)
    for k in range(8):
        match = metas[:, k : k + 1] == lanes
        high += jnp.where(match, metas[:, 8 + k : 9 + k], 0.0)
        low += jnp.where(match, metas[:, 16 + k : 17 + k], 0.0)
    high, low = high.astype(BF), low.astype(BF)
    slot_lane, _, _ = slot_parts(lax.broadcasted_iota(jnp.int32, (META, slots), 1))
    spread = jnp.where(
        slot_lane == lax.broadcasted_iota(jnp.int32, (META, slots), 0), 1.0, 0.0
    ).astype(BF)
    picked = jnp.dot(values, spread, preferred_element_type=F32)
    _, rank, source = slot_parts(lax.broadcasted_iota(jnp.int32, (tokens, slots), 1))
    token = lax.broadcasted_iota(jnp.int32, (tokens, slots), 0)
    there = (picked == (rank + 1).astype(F32)) & (source == (token >> 5))
    high_at = jnp.dot(high, spread, preferred_element_type=F32)
    low_at = jnp.dot(low, spread, preferred_element_type=F32)
    high_ref[...] = jnp.where(there, high_at, 0.0).astype(BF)
    low_ref[...] = jnp.where(there, low_at, 0.0).astype(BF)
    slot = lax.broadcasted_iota(jnp.int32, (META, META), 1)
    from_lane = lax.broadcasted_iota(jnp.int32, (META, META), 0)
    spread = jnp.where((from_lane == 8 + (slot & 1)) & (slot < EXTRA), 1.0, 0.0).astype(BF)
    picked = jnp.dot(values[:own], spread, preferred_element_type=F32)
    slot = lax.broadcasted_iota(jnp.int32, (own, META), 1)
    token = lax.broadcasted_iota(jnp.int32, (own, META), 0)
    there = (picked == CAP + 1.0) & ((slot >> 1) == (token >> 5))
    high_at = jnp.dot(high[:own], spread, preferred_element_type=F32)
    low_at = jnp.dot(low[:own], spread, preferred_element_type=F32)
    extra_high_ref[...] = jnp.where(there, high_at, 0.0).astype(BF)
    extra_low_ref[...] = jnp.where(there, low_at, 0.0).astype(BF)


def scatter_kernel(own, skip, high_ref, low_ref, *refs):
    refs, out_ref = refs[: len(refs) - 1 - skip], refs[-1]
    extras, rows_in = refs[:-8], refs[-8:]
    half, depth = out_ref.shape
    at = 0 if own else half
    high, low = high_ref[at : at + half, :], low_ref[at : at + half, :]
    for start in range(0, depth, COLS):
        block = jnp.concatenate([r[:, start : start + COLS] for r in rows_in], axis=0)
        sums = jnp.dot(high, block, preferred_element_type=F32)
        sums += jnp.dot(low, block, preferred_element_type=F32)
        if own:
            extra_high, extra_low, extra_ref = extras
            extra = jnp.concatenate(
                [extra_ref[:, start : start + COLS], jnp.zeros((META - EXTRA, COLS), BF)], axis=0
            )
            sums += jnp.dot(extra_high[...], extra, preferred_element_type=F32)
            sums += jnp.dot(extra_low[...], extra, preferred_element_type=F32)
        out_ref[:, start : start + COLS] = sums.astype(BF)


def whole(count):
    return [pl.BlockSpec(memory_space=pltpu.VMEM)] * count


def anywhere(count):
    return [pl.BlockSpec(memory_space=pl.ANY)] * count


def rough(flops, size):
    return pl.CostEstimate(flops=flops // 64, bytes_accessed=size // 64, transcendentals=0)


PARAMS = pltpu.CompilerParams(vmem_limit_bytes=VMEM)


def gather_rows(lanes, pieces, depth):
    shapes = [
        jax.ShapeDtypeStruct((2 * PIECE, depth + (META if d else 0)), BF)
        for d in range(NY)
    ]
    shapes += [
        jax.ShapeDtypeStruct((SRC * 16, depth), BF),
        jax.ShapeDtypeStruct((SRC * 32, META), F32),
        jax.ShapeDtypeStruct((8, META), F32),
    ]
    return pl.pallas_call(
        gather_kernel,
        out_shape=shapes,
        in_specs=whole(1) + [pl.BlockSpec(pieces[0].shape, lambda: (0, 0))] * SRC,
        out_specs=whole(7),
        compiler_params=PARAMS,
        cost_estimate=rough(2 * 384 * 512 * depth, 7 << 20),
        name="gather_rows",
    )(lanes, *pieces)


def relay(arrays, after):
    count = len(arrays)
    return pl.pallas_call(
        functools.partial(relay_kernel, count),
        out_shape=[jax.ShapeDtypeStruct(a.shape, a.dtype) for a in arrays],
        in_specs=whole(count) + anywhere(len(after)),
        out_specs=whole(count),
        compiler_params=PARAMS,
        cost_estimate=rough(0, 1 << 19),
        name="relay",
    )(*arrays, *after)


def cut_far(left, right, cut, after):
    rows, depth = left.shape
    return pl.pallas_call(
        cut_kernel,
        out_shape=[jax.ShapeDtypeStruct((r, depth), BF) for r in (cut, rows - cut)],
        in_specs=whole(2) + anywhere(len(after)),
        out_specs=whole(2),
        compiler_params=PARAMS,
        cost_estimate=rough(0, 2 << 20),
        name="cut_far",
    )(left, right, *after)


def stack_kernel(count, *refs):
    rows, out = refs[0].shape[0], refs[-1]
    for j in range(count):
        out[j * rows : (j + 1) * rows, :] = refs[j][:, : out.shape[1]]


def stack(arrays, depth, after):
    rows = arrays[0].shape[0]
    return pl.pallas_call(
        functools.partial(stack_kernel, len(arrays)),
        out_shape=jax.ShapeDtypeStruct((len(arrays) * rows, depth), BF),
        in_specs=whole(len(arrays)) + anywhere(len(after)),
        out_specs=whole(1)[0],
        compiler_params=PARAMS,
        cost_estimate=rough(0, 4 << 20),
        name="stack",
    )(*arrays, *after)


def fold_kernel(left_a, minus, right_b, plus, left_out, right_out):
    half = left_a.shape[0]
    left_out[...] = (left_a[...].astype(F32) + minus[:half, :].astype(F32)).astype(BF)
    right_out[...] = (right_b[...].astype(F32) + plus[:half, :].astype(F32)).astype(BF)


def fold(left_a, minus, right_b, plus):
    return pl.pallas_call(
        fold_kernel,
        out_shape=[jax.ShapeDtypeStruct(left_a.shape, BF)] * 2,
        in_specs=whole(4),
        out_specs=whole(2),
        compiler_params=PARAMS,
        cost_estimate=rough(0, 4 << 20),
        name="fold",
    )(left_a, minus, right_b, plus)


def pair_kernel(a_ref, b_ref, *refs):
    refs[-1][...] = (a_ref[...].astype(F32) + b_ref[...].astype(F32)).astype(BF)


def pair_sum(a, b, after):
    return pl.pallas_call(
        pair_kernel,
        out_shape=jax.ShapeDtypeStruct(a.shape, BF),
        in_specs=whole(2) + anywhere(len(after)),
        out_specs=whole(1)[0],
        compiler_params=PARAMS,
        cost_estimate=rough(0, 4 << 20),
        name="pair_sum",
    )(a, b, *after)


def settle(own, terms, after):
    depth = own.shape[1]
    return pl.pallas_call(
        settle_kernel,
        out_shape=[jax.ShapeDtypeStruct((PIECE, depth), BF)] * NY,
        in_specs=whole(5) + anywhere(len(after)),
        out_specs=whole(NY),
        compiler_params=PARAMS,
        cost_estimate=rough(0, 5 << 20),
        name="settle",
    )(own, *terms, *after)


def pick_extra(counts, metas, line, two, one, three, after):
    depth = line.shape[1]
    return pl.pallas_call(
        pick_kernel,
        out_shape=[
            jax.ShapeDtypeStruct((EXTRA, depth), BF),
            jax.ShapeDtypeStruct((8, META), F32),
            jax.ShapeDtypeStruct((8, META), F32),
        ],
        in_specs=whole(6) + anywhere(len(after)),
        out_specs=whole(3),
        compiler_params=PARAMS,
        cost_estimate=rough(2 * 16 * 256 * depth, 2 << 20),
        name="pick_extra",
    )(counts, metas, line, two, one, three, *after)


def plan_scatter(lanes, metas):
    shapes = [jax.ShapeDtypeStruct((SRC * 32, 8 * PIECE), BF)] * 2
    shapes += [jax.ShapeDtypeStruct((SRC * 16, META), BF)] * 2
    return pl.pallas_call(
        plan_kernel,
        out_shape=shapes,
        in_specs=whole(2),
        out_specs=whole(4),
        compiler_params=PARAMS,
        cost_estimate=rough(512 * 512 * 1024, 1 << 20),
        name="plan_scatter",
    )(lanes, metas)


def scatter_rows(own, plan, rows, after):
    depth = rows[0].shape[1]
    return pl.pallas_call(
        functools.partial(scatter_kernel, own, len(after)),
        out_shape=jax.ShapeDtypeStruct((SRC * 16, depth), BF),
        in_specs=whole(len(plan) + len(rows)) + anywhere(len(after)),
        out_specs=whole(1)[0],
        compiler_params=PARAMS,
        cost_estimate=rough(2 * 384 * 512 * depth, 5 << 20),
        name="scatter_rows",
    )(*plan, *rows, *after)


def deq_kernel(w_ref, s_ref, *refs):
    out_ref = refs[-1]
    rows, cols = w_ref.shape[1:]
    scales = s_ref[0]
    for r in range(rows // BLOCK):
        for c in range(cols // BLOCK):
            at = (0, slice(r * BLOCK, (r + 1) * BLOCK), slice(c * BLOCK, (c + 1) * BLOCK))
            out_ref[at] = (w_ref[at].astype(F32) * scales[r : r + 1, c : c + 1]).astype(BF)


def dequantize(weight, scale, after):
    count, rows, cols = weight.shape

    def block(array):
        return pl.BlockSpec((1,) + array.shape[1:], lambda i: (i, 0, 0))

    return pl.pallas_call(
        deq_kernel,
        grid=(count,),
        out_shape=jax.ShapeDtypeStruct(weight.shape, BF),
        in_specs=[block(weight), block(scale)] + anywhere(len(after)),
        out_specs=block(weight),
        compiler_params=PARAMS,
        cost_estimate=rough(count * rows * cols, 4 * count * rows * cols),
        name="dequantize",
    )(weight, scale, *after)


def silu(value):
    return value * (1.0 / (1.0 + jnp.exp(-value)))


def ffn_kernel(in_count, out_parts, skip, *refs):
    xs, (gate_w, up_w, down_w) = refs[:in_count], refs[in_count : in_count + 3]
    refs = refs[in_count + 3 + skip :]
    outs, (gate_acc, up_acc, hidden) = refs[: len(out_parts)], refs[len(out_parts) :]
    step = pl.program_id(0)

    @pl.when(step < STEPS)
    def _():
        x = jnp.concatenate([r[...] for r in xs], axis=0)
        gate = jnp.dot(x, gate_w[0], preferred_element_type=F32)
        up = jnp.dot(x, up_w[0], preferred_element_type=F32)

        @pl.when(step == 0)
        def _():
            gate_acc[...] = gate
            up_acc[...] = up

        @pl.when(step > 0)
        def _():
            gate_acc[...] += gate
            up_acc[...] += up

    @pl.when(step >= STEPS)
    def _():
        @pl.when(step == STEPS)
        def _():
            hidden[...] = (silu(gate_acc[...]) * up_acc[...]).astype(BF)

        result = jnp.dot(hidden[...], down_w[0], preferred_element_type=F32).astype(BF)
        for ref, parts in zip(outs, out_parts):
            at = 0
            for low, high in parts:
                ref[at : at + high - low, :] = result[low:high]
                at += high - low


def early(i):
    return jnp.minimum(i, STEPS - 1)


def late(i):
    return jnp.maximum(i - STEPS, 0)


def ffn(xs, out_parts, which, weights, after):
    gate_w, up_w, down_w = weights
    depth, units = gate_w.shape[1:]
    wide = depth // STEPS
    total = sum(rows for _, rows, _ in xs)
    out_rows = [sum(high - low for low, high in parts) for parts in out_parts]
    in_specs = [
        pl.BlockSpec((rows, wide), lambda i, place=place: (place, early(i))) for _, rows, place in xs
    ]
    in_specs += [pl.BlockSpec((1, wide, units), lambda i: (which, early(i), 0))] * 2
    in_specs += [pl.BlockSpec((1, units, wide), lambda i: (which, 0, late(i)))]
    return pl.pallas_call(
        functools.partial(ffn_kernel, len(xs), out_parts, len(after)),
        grid=(2 * STEPS,),
        out_shape=[jax.ShapeDtypeStruct((r, depth), BF) for r in out_rows],
        in_specs=in_specs + anywhere(len(after)),
        out_specs=[pl.BlockSpec((r, wide), lambda i: (0, late(i))) for r in out_rows],
        scratch_shapes=[
            pltpu.VMEM((total, units), F32),
            pltpu.VMEM((total, units), F32),
            pltpu.VMEM((total, units), BF),
        ],
        compiler_params=PARAMS,
        cost_estimate=rough(6 * total * units * depth, 4 * total * depth + 6 * units * depth),
        name="ffn",
    )(*[x for x, _, _ in xs], gate_w, up_w, down_w, *after)


def extra_kernel(skip, place_ref, own_in, other_in, gate_w, up_w, down_a, down_b, *refs):
    own_out, other_out, gate_acc, up_acc, hidden = refs[skip:]
    step = pl.program_id(0)
    units = gate_w.shape[2]

    @pl.when(step < 2 * STEPS)
    def _():
        x = jnp.concatenate([own_in[...], other_in[...]], axis=0)
        gate = jnp.dot(x, gate_w[0], preferred_element_type=F32)
        up = jnp.dot(x, up_w[0], preferred_element_type=F32)
        opening = (step == 0) | (step == STEPS)

        @pl.when(opening)
        def _():
            gate_acc[...] = gate
            up_acc[...] = up

        @pl.when(jnp.logical_not(opening))
        def _():
            gate_acc[...] += gate
            up_acc[...] += up

    for j in range(2):

        @pl.when(step == (j + 1) * STEPS - 1)
        def _(j=j):
            value = silu(gate_acc[...]) * up_acc[...]
            row = lax.broadcasted_iota(jnp.int32, value.shape, 0)
            keep = ((row & 1) == j) & (place_ref[2 + j] == 1)
            hidden[:, j * units : (j + 1) * units] = jnp.where(keep, value, 0.0).astype(BF)

    @pl.when(step >= 2 * STEPS)
    def _():
        down = jnp.concatenate([down_a[0], down_b[0]], axis=0)
        result = jnp.dot(hidden[...], down, preferred_element_type=F32).astype(BF)
        half = own_out.shape[0]
        own_out[...] = result[:half]
        other_out[...] = result[half:]


def extra_ffn(places, own, other, weights, after):
    gate_w, up_w, down_w = weights
    depth, units = gate_w.shape[1:]
    wide = depth // STEPS
    half = own.shape[0]

    def first(i):
        return jnp.where(i < 2 * STEPS, i & (STEPS - 1), STEPS - 1)

    def last(i):
        return jnp.maximum(i - 2 * STEPS, 0)

    def turn(i):
        return jnp.where(i < STEPS, 0, 1)

    rows_in = pl.BlockSpec((half, wide), lambda i, s: (0, first(i)))
    gate_in = pl.BlockSpec((1, wide, units), lambda i, s: (s[turn(i)], first(i), 0))
    rows_out = pl.BlockSpec((half, wide), lambda i, s: (0, last(i)))
    spec = pltpu.PrefetchScalarGridSpec(
        num_scalar_prefetch=1,
        grid=(3 * STEPS,),
        in_specs=[rows_in, rows_in, gate_in, gate_in]
        + [pl.BlockSpec((1, units, wide), lambda i, s, j=j: (s[j], 0, last(i))) for j in range(2)]
        + anywhere(len(after)),
        out_specs=[rows_out, rows_out],
        scratch_shapes=[
            pltpu.VMEM((2 * half, units), F32),
            pltpu.VMEM((2 * half, units), F32),
            pltpu.VMEM((2 * half, 2 * units), BF),
        ],
    )
    return pl.pallas_call(
        functools.partial(extra_kernel, len(after)),
        grid_spec=spec,
        out_shape=[jax.ShapeDtypeStruct((half, depth), BF)] * 2,
        compiler_params=PARAMS,
        cost_estimate=rough(20 * half * units * depth, 32 << 20),
        name="extra_ffn",
    )(places, own, other, gate_w, up_w, down_w, down_w, *after)


def add(*values):
    total = values[0].astype(F32)
    for value in values[1:]:
        total = total + value.astype(F32)
    return total.astype(BF)


def gather_line(own):
    pieces = [own] + [None] * (NZ - 1)
    up = down = own
    for step in range(1, NZ // 2 + 1):
        up = expert_move(up, dz=-1)
        pieces[step] = up
        if step < NZ // 2:
            down = expert_move(down, dz=1)
            pieces[NZ - step] = down
    return pieces + [expert_move(piece, flip=True) for piece in pieces]


def scatter_line(own, other):
    arrived = expert_move(other, flip=True)

    def term(dz):
        return own[dz * 32 : dz * 32 + 32], arrived[dz * 32 : dz * 32 + 32]

    up = add(*term(NZ // 2))
    for dz in range(NZ // 2 - 1, 0, -1):
        up = add(expert_move(up, dz=1), *term(dz))
    down = add(*term(NZ // 2 + 1))
    for dz in range(NZ // 2 + 2, NZ):
        down = add(expert_move(down, dz=-1), *term(dz))
    return [expert_move(up, dz=1), expert_move(down, dz=-1), *term(0)]


def spread_dp(block, cut, after=()):
    left = dp_move(block, 1)
    right = dp_move(block, -1)
    far = cut_far(left, right, cut, after) if after else (left[:cut], right[cut:])
    return [block, left, right, dp_move(far[0], 1), dp_move(far[1], -1), *far]


def sum_dp_first(parts):
    minus, plus, left_a, right_b, own = parts
    got_minus = dp_move(minus, -1)
    got_plus = dp_move(plus, 1)
    left_a, right_b = fold(left_a, got_minus, right_b, got_plus)
    return left_a, got_minus, got_plus, right_b, own


def sum_dp_second(state, after):
    left_a, got_minus, got_plus, right_b, own = state
    got_left_a = dp_move(left_a, -1)
    got_right_b = dp_move(right_b, 1)
    return settle(own, (got_left_a, got_minus, got_plus, got_right_b), after), [got_left_a, got_right_b]


def return_rows(group):
    own, one, three, two = group
    return [own, expert_move(one, dy=-1), expert_move(two, dy=-2), expert_move(three, dy=-3)]


def per_device(
    tokens,
    routes,
    route_weight,
    gate_weight,
    up_weight,
    down_weight,
    gate_scale,
    up_scale,
    down_scale,
):
    rows, depth = tokens.shape
    top = routes.shape[1]
    experts = gate_weight.shape[0] * NY * NZ * NC
    all_rows = rows * NX * NY * NZ * NC
    place = lax.axis_index("expert")
    y, line = place // (NZ * NC), place % (NZ * NC)
    lane = jnp.arange(META, dtype=jnp.int32)

    named = (routes[:, :, None] == lane[None, None, :]).astype(F32)
    counts = jnp.broadcast_to(jnp.sum(named, axis=(0, 1))[None], (8, META))
    counts = sum([dp_move(counts, d) for d in range(1, NX)], counts)
    high = lax.reduce_precision(route_weight, 8, 7)
    low = lax.reduce_precision(route_weight - high, 8, 7)
    carried = jnp.concatenate(
        [
            tokens,
            routes.astype(BF),
            high.astype(BF),
            low.astype(BF),
            jnp.zeros((rows, META - 3 * top), BF),
            jnp.broadcast_to(counts[:1].astype(BF), (rows, META)),
        ],
        axis=1,
    )
    pieces = gather_line(carried)

    lane_expert = ((((y + lane % NY) % NY) * (NZ * NC) + line) * 2 + lane // NY).astype(F32)
    lanes = jnp.broadcast_to(jnp.where(lane < 8, lane_expert, -1.0)[None], (8, META))
    near, *blocks, tokens_line, metas, counts = gather_rows(lanes, pieces, depth)
    near = spread_dp(near, PIECE)
    one, two, three = [expert_move(blocks[d - 1], dy=d) for d in range(1, NY)]
    weights = [
        dequantize(weight, scale, [metas])
        for weight, scale in (
            (gate_weight, gate_scale),
            (up_weight, up_scale),
            (down_weight, down_scale),
        )
    ]
    first = stack([one, three], depth, [*near[3:5], *weights])
    extra, hot, totals = pick_extra(counts, metas, tokens_line, two, one, three, [])
    load_share = totals[0, :experts] * (experts / (all_rows * top))
    first = spread_dp(first, 2 * PIECE, [extra])
    extra = stack([extra] + [dp_move(extra, d) for d in range(1, NX)], depth, first[5:6])
    second = spread_dp(stack([two], depth, [extra]), PIECE)
    extra = stack([extra] + [expert_move(extra, dy=d) for d in range(1, NY)], depth, [*first[3:5], *second[1:3]])
    extra_other = expert_move(extra, flip=True)

    hot_id = hot[0:2, 0].astype(jnp.int32)
    places = jnp.concatenate([hot_id & 1, ((hot_id >> 1) == place).astype(jnp.int32)])
    spare = jnp.where(lane == 8, hot[0:1], jnp.where(lane == 9, hot[1:2], lanes))
    plan = plan_scatter(spare, metas)
    half = NY * PIECE // 2
    out_parts = [
        [(4 * half, 5 * half), (half, 2 * half)],
        [(5 * half, 6 * half), (2 * half, 3 * half)],
        [(0, half)],
        [(3 * half, 4 * half)],
        [(6 * half, 8 * half)],
    ]
    parts = []
    after = [extra, plan[0]]
    for which in range(2):
        sides = [
            [near[i], which, first[i], which, first[i], 2 + which, second[i], which]
            for i in (1, 2, 0)
        ]
        sides.insert(2, [near[3 + which], 0, first[3], which, first[4], which, second[3 + which], 0])
        xs = [(side[i], PIECE, side[i + 1]) for side in sides for i in range(0, 8, 2)]
        parts.append(list(ffn(xs, out_parts, which, weights, after)))
        if which == 0:
            parts[0][:2] = relay(parts[0][:2], second[3:5])
            own, other = extra_ffn(places, extra, extra_other, weights, parts[0][:1])
            state = sum_dp_first(parts[0])
            extra = pair_sum(own, expert_move(other, flip=True), [])
            after = [own, state[0]]

    size = NX * EXTRA
    extra = add(
        extra[:size],
        *[expert_move(extra[d * size : (d + 1) * size], dy=-d) for d in range(1, NY)],
    )
    group, arrived = sum_dp_second(state, [extra])
    parts[1][:2] = relay(parts[1][:2], arrived)
    extra = add(
        extra[:EXTRA], *[dp_move(extra[d * EXTRA : (d + 1) * EXTRA], -d) for d in range(1, NX)]
    )
    returned = return_rows(group)
    group, _ = sum_dp_second(sum_dp_first(parts[1]), returned)
    returned += return_rows(group)
    other = scatter_rows(False, plan[:2], returned, [extra])
    own = scatter_rows(True, [*plan, extra], returned, [])
    terms = scatter_line(own, other)
    return add(*terms), load_share


def solution(mesh):
    in_specs = (
        P(("dp", "expert"), None),
        P(("dp", "expert"), None),
        P(("dp", "expert"), None),
        P("expert", None, "dp"),
        P("expert", None, "dp"),
        P("expert", "dp", None),
        P("expert", None, "dp"),
        P("expert", None, "dp"),
        P("expert", "dp", None),
    )
    out_specs = (P(("dp", "expert"), None), P())
    return jax.shard_map(
        per_device, mesh=mesh, in_specs=in_specs, out_specs=out_specs, check_vma=False
    )
```

```python
import functools

import jax
import jax.numpy as jnp
from jax import lax
from jax.experimental import pallas as pl
from jax.experimental.pallas import tpu as pltpu
from jax.sharding import PartitionSpec as P

BLOCK = 128
CAP = 3
NY, NZ, NC, NX = 4, 8, 2, 4
SRC = NZ * NC
PIECE = SRC * CAP
META = 128
COLS = 512
STEPS = 4
EXTRA = 2 * NZ
BF = jnp.bfloat16
F32 = jnp.float32
VMEM = 24 * 1024 * 1024


def expert_move(value, dy=0, dz=0, flip=False, xor_y=0):
    pairs = []
    for y in range(NY):
        for z in range(NZ):
            for c in range(NC):
                to_y = (y + dy) % NY ^ xor_y
                to_z = (z + dz) % NZ
                to_c = c ^ 1 if flip else c
                pairs.append(((y * NZ + z) * NC + c, (to_y * NZ + to_z) * NC + to_c))
    return lax.ppermute(value, "expert", pairs)


def dp_move(value, dx=0, xor_x=0):
    return lax.ppermute(value, "dp", [(x, (x + dx) % NX ^ xor_x) for x in range(NX)])


def slot_values(metas, lanes):
    tokens = metas.shape[0]
    found = jnp.zeros((tokens, META), F32)
    for k in range(8):
        found += jnp.where(metas[:, k : k + 1] == lanes, 1.0, 0.0)
    row = lax.broadcasted_iota(jnp.int32, (tokens, tokens), 0)
    col = lax.broadcasted_iota(jnp.int32, (tokens, tokens), 1)
    earlier = jnp.where(((row >> 5) == (col >> 5)) & (col < row), 1.0, 0.0).astype(BF)
    rank = jnp.dot(earlier, found.astype(BF), preferred_element_type=F32)
    return found * (rank + 1.0)


def slot_parts(slots):
    lane = (slots * 1366) >> 16
    rest = slots - lane * PIECE
    return lane, rest >> 4, rest & 15


def gather_kernel(lanes_ref, *refs):
    pieces, near_ref, outs = refs[:SRC], refs[SRC], refs[SRC + 1 : SRC + 7]
    line_ref, metas_ref, counts_ref = refs[SRC + 7 : SRC + 10]
    tokens, slots = SRC * 32, 8 * PIECE
    depth = near_ref.shape[1]
    metas = jnp.concatenate([p[:, depth : depth + META] for p in pieces], axis=0).astype(F32)
    metas_ref[...] = metas
    counted = jnp.concatenate([p[:, depth + META :] for p in pieces], axis=0).astype(F32)
    total = jnp.sum(counted, axis=0, keepdims=True) * (1.0 / 32.0)
    counts_ref[...] = jnp.broadcast_to(total, (8, META))
    for d in range(1, NY):
        outs[d - 1][:, depth:] = jnp.broadcast_to(total, (PIECE, META)).astype(BF)
    values = slot_values(metas, lanes_ref[0:1, :])
    slot_lane, _, _ = slot_parts(lax.broadcasted_iota(jnp.int32, (slots, META), 0))
    spread = jnp.where(
        slot_lane == lax.broadcasted_iota(jnp.int32, (slots, META), 1), 1.0, 0.0
    ).astype(BF)
    picked = lax.dot_general(
        spread, values.astype(BF), (((1,), (1,)), ((), ())), preferred_element_type=F32
    )
    _, rank, source = slot_parts(lax.broadcasted_iota(jnp.int32, (slots, tokens), 0))
    token = lax.broadcasted_iota(jnp.int32, (slots, tokens), 1)
    choose = jnp.where(
        (picked == (rank + 1).astype(F32)) & (source == (token >> 5)), 1.0, 0.0
    ).astype(BF)
    for start in range(0, depth, COLS):
        block = jnp.concatenate([p[:, start : start + COLS] for p in pieces], axis=0)
        line_ref[:, start : start + COLS] = block[: tokens // 2]
        rows = jnp.dot(choose, block, preferred_element_type=F32).astype(BF)
        for which in range(2):
            at = which * NY * PIECE
            near_ref[which * PIECE : (which + 1) * PIECE, start : start + COLS] = rows[at : at + PIECE]
            for d in range(1, NY):
                low = at + d * PIECE
                outs[which * 3 + d - 1][:, start : start + COLS] = rows[low : low + PIECE]


def relay_kernel(count, *refs):
    for in_ref, out_ref in zip(refs[:count], refs[-count:]):
        out_ref[...] = in_ref[...]


def cut_kernel(left_ref, right_ref, *refs):
    far_a, far_b = refs[-2:]
    far_a[...] = left_ref[: far_a.shape[0], :]
    far_b[...] = right_ref[far_a.shape[0] :, :]


def settle_kernel(own_ref, left_a, minus_ref, plus_ref, right_b, *refs):
    half = left_a.shape[0]
    for j, out in enumerate(refs[-NY:]):
        low = j * PIECE
        if low < half:
            left, right = left_a[low : low + PIECE, :], plus_ref[half + low : half + low + PIECE, :]
        else:
            at = low - half
            left, right = minus_ref[low : low + PIECE, :], right_b[at : at + PIECE, :]
        total = own_ref[low : low + PIECE, :].astype(F32) + left.astype(F32)
        out[...] = (total + right.astype(F32)).astype(BF)


def pack_kernel(tokens_ref, routes_ref, weight_ref, counts_ref, out_ref):
    rows, depth = tokens_ref.shape
    top = routes_ref.shape[0]
    weight = weight_ref[...]
    high = weight.astype(BF).astype(F32)
    lines = [routes_ref[...].astype(F32), high, weight - high, jnp.zeros((META - 3 * top, rows), F32)]
    lines = jnp.concatenate(lines, axis=0).astype(BF)
    row = lax.broadcasted_iota(jnp.int32, (rows, rows), 0)
    same = jnp.where(row == lax.broadcasted_iota(jnp.int32, (rows, rows), 1), 1.0, 0.0).astype(BF)
    out_ref[:, :depth] = tokens_ref[...]
    out_ref[:, depth : depth + META] = lax.dot_general(
        same, lines, (((1,), (1,)), ((), ())), preferred_element_type=F32
    ).astype(BF)
    out_ref[:, depth + META :] = jnp.broadcast_to(counts_ref[0:1, :], (rows, META)).astype(BF)


def pack(tokens, routes, weight, counts):
    rows, depth = tokens.shape
    return pl.pallas_call(
        pack_kernel,
        out_shape=jax.ShapeDtypeStruct((rows, depth + 2 * META), BF),
        in_specs=whole(4),
        out_specs=whole(1)[0],
        compiler_params=PARAMS,
        cost_estimate=rough(0, 1 << 19),
        name="pack",
    )(tokens, routes, weight, counts)


def pick_kernel(counts_ref, metas_ref, line_ref, *refs):
    ins, (rows_ref, hot_ref, totals_ref) = refs[:3], refs[-3:]
    base = 3 * PIECE
    depth = rows_ref.shape[1]
    totals = counts_ref[0:1, :]
    for j in range(3):
        rows_ref[j * PIECE : (j + 1) * PIECE, :] = ins[j][:, :depth]
        totals = totals + ins[j][0:16, depth:].astype(F32)[0:1]
    totals_ref[...] = jnp.broadcast_to(totals, (8, META))
    tokens = NZ * 32
    every = lax.broadcasted_iota(jnp.int32, (1, META), 1).astype(F32)
    order = totals * META + (META - 1.0 - every)
    best = order == jnp.max(order, axis=1, keepdims=True)
    first = jnp.sum(jnp.where(best, every, 0.0), axis=1, keepdims=True)
    order = jnp.where(best, -1.0, order)
    best = order == jnp.max(order, axis=1, keepdims=True)
    second = jnp.sum(jnp.where(best, every, 0.0), axis=1, keepdims=True)
    row = lax.broadcasted_iota(jnp.int32, (8, META), 0)
    hot_ref[...] = jnp.where(row == 0, first, second)
    lanes = jnp.where(every == 0.0, first, jnp.where(every == 1.0, second, -1.0))
    values = slot_values(metas_ref[:tokens, :], lanes)
    slot = lax.broadcasted_iota(jnp.int32, (EXTRA, META), 0)
    spread = jnp.where(
        (slot & 1) == lax.broadcasted_iota(jnp.int32, (EXTRA, META), 1), 1.0, 0.0
    ).astype(BF)
    picked = lax.dot_general(
        spread, values.astype(BF), (((1,), (1,)), ((), ())), preferred_element_type=F32
    )
    slot = lax.broadcasted_iota(jnp.int32, (EXTRA, tokens), 0)
    token = lax.broadcasted_iota(jnp.int32, (EXTRA, tokens), 1)
    choose = jnp.where(
        (picked == CAP + 1.0) & ((slot >> 1) == (token >> 5)), 1.0, 0.0
    ).astype(BF)
    for start in range(0, depth, COLS):
        rows_ref[base:, start : start + COLS] = jnp.dot(
            choose, line_ref[:, start : start + COLS], preferred_element_type=F32
        ).astype(BF)


def plan_kernel(lanes_ref, metas_ref, high_ref, low_ref, extra_high_ref, extra_low_ref):
    tokens, slots = SRC * 32, 8 * PIECE
    own = tokens // 2
    lanes = lanes_ref[0:1, :]
    metas = metas_ref[...]
    values = slot_values(metas, lanes).astype(BF)
    high = jnp.zeros((tokens, META), F32)
    low = jnp.zeros((tokens, META), F32)
    for k in range(8):
        match = metas[:, k : k + 1] == lanes
        high += jnp.where(match, metas[:, 8 + k : 9 + k], 0.0)
        low += jnp.where(match, metas[:, 16 + k : 17 + k], 0.0)
    high, low = high.astype(BF), low.astype(BF)
    slot_lane, _, _ = slot_parts(lax.broadcasted_iota(jnp.int32, (META, slots), 1))
    spread = jnp.where(
        slot_lane == lax.broadcasted_iota(jnp.int32, (META, slots), 0), 1.0, 0.0
    ).astype(BF)
    picked = jnp.dot(values, spread, preferred_element_type=F32)
    _, rank, source = slot_parts(lax.broadcasted_iota(jnp.int32, (tokens, slots), 1))
    token = lax.broadcasted_iota(jnp.int32, (tokens, slots), 0)
    there = (picked == (rank + 1).astype(F32)) & (source == (token >> 5))
    high_at = jnp.dot(high, spread, preferred_element_type=F32)
    low_at = jnp.dot(low, spread, preferred_element_type=F32)
    high_ref[...] = jnp.where(there, high_at, 0.0).astype(BF)
    low_ref[...] = jnp.where(there, low_at, 0.0).astype(BF)
    slot = lax.broadcasted_iota(jnp.int32, (META, META), 1)
    from_lane = lax.broadcasted_iota(jnp.int32, (META, META), 0)
    spread = jnp.where((from_lane == 8 + (slot & 1)) & (slot < EXTRA), 1.0, 0.0).astype(BF)
    picked = jnp.dot(values[:own], spread, preferred_element_type=F32)
    slot = lax.broadcasted_iota(jnp.int32, (own, META), 1)
    token = lax.broadcasted_iota(jnp.int32, (own, META), 0)
    there = (picked == CAP + 1.0) & ((slot >> 1) == (token >> 5))
    high_at = jnp.dot(high[:own], spread, preferred_element_type=F32)
    low_at = jnp.dot(low[:own], spread, preferred_element_type=F32)
    extra_high_ref[...] = jnp.where(there, high_at, 0.0).astype(BF)
    extra_low_ref[...] = jnp.where(there, low_at, 0.0).astype(BF)


def scatter_kernel(own, skip, high_ref, low_ref, *refs):
    refs, out_ref = refs[: len(refs) - 1 - skip], refs[-1]
    extras, rows_in = refs[:-8], refs[-8:]
    half, depth = out_ref.shape
    at = 0 if own else half
    high, low = high_ref[at : at + half, :], low_ref[at : at + half, :]
    for start in range(0, depth, COLS):
        block = jnp.concatenate([r[:, start : start + COLS] for r in rows_in], axis=0)
        sums = jnp.dot(high, block, preferred_element_type=F32)
        sums += jnp.dot(low, block, preferred_element_type=F32)
        if own:
            extra_high, extra_low, extra_ref = extras
            extra = jnp.concatenate(
                [extra_ref[:, start : start + COLS], jnp.zeros((META - EXTRA, COLS), BF)], axis=0
            )
            sums += jnp.dot(extra_high[...], extra, preferred_element_type=F32)
            sums += jnp.dot(extra_low[...], extra, preferred_element_type=F32)
        out_ref[:, start : start + COLS] = sums.astype(BF)


def merge_kernel(*refs):
    ins, out = refs[:3], refs[-1]
    for j in range(3):
        out[j * PIECE : (j + 1) * PIECE, :] = ins[j][...]


def whole(count):
    return [pl.BlockSpec(memory_space=pltpu.VMEM)] * count


def anywhere(count):
    return [pl.BlockSpec(memory_space=pl.ANY)] * count


def rough(flops, size):
    return pl.CostEstimate(flops=flops // 64, bytes_accessed=size // 64, transcendentals=0)


PARAMS = pltpu.CompilerParams(vmem_limit_bytes=VMEM)


def gather_rows(lanes, pieces, depth):
    shapes = [jax.ShapeDtypeStruct((2 * PIECE, depth), BF)]
    shapes += [jax.ShapeDtypeStruct((PIECE, depth + META), BF)] * 3
    shapes += [jax.ShapeDtypeStruct((PIECE, depth), BF)] * 3
    shapes += [
        jax.ShapeDtypeStruct((SRC * 16, depth), BF),
        jax.ShapeDtypeStruct((SRC * 32, META), F32),
        jax.ShapeDtypeStruct((8, META), F32),
    ]
    return pl.pallas_call(
        gather_kernel,
        out_shape=shapes,
        in_specs=whole(1 + SRC),
        out_specs=whole(10),
        compiler_params=PARAMS,
        cost_estimate=rough(2 * 384 * 512 * depth, 7 << 20),
        name="gather_rows",
    )(lanes, *pieces)


def relay(arrays, after):
    count = len(arrays)
    return pl.pallas_call(
        functools.partial(relay_kernel, count),
        out_shape=[jax.ShapeDtypeStruct(a.shape, a.dtype) for a in arrays],
        in_specs=whole(count) + anywhere(len(after)),
        out_specs=whole(count),
        compiler_params=PARAMS,
        cost_estimate=rough(0, 1 << 19),
        name="relay",
    )(*arrays, *after)


def cut_far(left, right, cut, after):
    rows, depth = left.shape
    return pl.pallas_call(
        cut_kernel,
        out_shape=[jax.ShapeDtypeStruct((r, depth), BF) for r in (cut, rows - cut)],
        in_specs=whole(2) + anywhere(len(after)),
        out_specs=whole(2),
        compiler_params=PARAMS,
        cost_estimate=rough(0, 2 << 20),
        name="cut_far",
    )(left, right, *after)


def join_kernel(own_ref, left_ref, far_ref, right_ref, *refs):
    out = refs[-1]
    for j, ref in enumerate((own_ref, left_ref, far_ref, right_ref)):
        out[j * EXTRA : (j + 1) * EXTRA, :] = ref[ref.shape[0] - EXTRA :, :]


def join_extra(blocks, after):
    return pl.pallas_call(
        join_kernel,
        out_shape=jax.ShapeDtypeStruct((NX * EXTRA, blocks[0].shape[1]), BF),
        in_specs=whole(4) + anywhere(len(after)),
        out_specs=whole(1)[0],
        compiler_params=PARAMS,
        cost_estimate=rough(0, 1 << 19),
        name="join_extra",
    )(*blocks, *after)


def stack_kernel(count, *refs):
    rows, out = refs[0].shape[0], refs[-1]
    for j in range(count):
        out[j * rows : (j + 1) * rows, :] = refs[j][...]


def stack(arrays, after):
    rows, depth = arrays[0].shape
    return pl.pallas_call(
        functools.partial(stack_kernel, len(arrays)),
        out_shape=jax.ShapeDtypeStruct((len(arrays) * rows, depth), BF),
        in_specs=whole(len(arrays)) + anywhere(len(after)),
        out_specs=whole(1)[0],
        compiler_params=PARAMS,
        cost_estimate=rough(0, 4 << 20),
        name="stack",
    )(*arrays, *after)


def fold_kernel(left_a, minus, right_b, plus, left_out, right_out):
    half = left_a.shape[0]
    left_out[...] = (left_a[...].astype(F32) + minus[:half, :].astype(F32)).astype(BF)
    right_out[...] = (right_b[...].astype(F32) + plus[:half, :].astype(F32)).astype(BF)


def fold(left_a, minus, right_b, plus):
    return pl.pallas_call(
        fold_kernel,
        out_shape=[jax.ShapeDtypeStruct(left_a.shape, BF)] * 2,
        in_specs=whole(4),
        out_specs=whole(2),
        compiler_params=PARAMS,
        cost_estimate=rough(0, 4 << 20),
        name="fold",
    )(left_a, minus, right_b, plus)


def pair_kernel(a_ref, b_ref, *refs):
    refs[-1][...] = (a_ref[...].astype(F32) + b_ref[...].astype(F32)).astype(BF)


def pair_sum(a, b, after):
    return pl.pallas_call(
        pair_kernel,
        out_shape=jax.ShapeDtypeStruct(a.shape, BF),
        in_specs=whole(2) + anywhere(len(after)),
        out_specs=whole(1)[0],
        compiler_params=PARAMS,
        cost_estimate=rough(0, 4 << 20),
        name="pair_sum",
    )(a, b, *after)


def settle(own, terms, after):
    depth = own.shape[1]
    return pl.pallas_call(
        settle_kernel,
        out_shape=[jax.ShapeDtypeStruct((PIECE, depth), BF)] * NY,
        in_specs=whole(5) + anywhere(len(after)),
        out_specs=whole(NY),
        compiler_params=PARAMS,
        cost_estimate=rough(0, 5 << 20),
        name="settle",
    )(own, *terms, *after)


def merge_pick(counts, metas, line, pieces, after):
    depth = line.shape[1]
    return pl.pallas_call(
        pick_kernel,
        out_shape=[
            jax.ShapeDtypeStruct((3 * PIECE + EXTRA, depth), BF),
            jax.ShapeDtypeStruct((8, META), F32),
            jax.ShapeDtypeStruct((8, META), F32),
        ],
        in_specs=whole(6) + anywhere(len(after)),
        out_specs=whole(3),
        compiler_params=PARAMS,
        cost_estimate=rough(2 * 16 * 256 * depth, 2 << 20),
        name="merge_pick",
    )(counts, metas, line, *pieces, *after)


def plan_scatter(lanes, metas):
    shapes = [jax.ShapeDtypeStruct((SRC * 32, 8 * PIECE), BF)] * 2
    shapes += [jax.ShapeDtypeStruct((SRC * 16, META), BF)] * 2
    return pl.pallas_call(
        plan_kernel,
        out_shape=shapes,
        in_specs=whole(2),
        out_specs=whole(4),
        compiler_params=PARAMS,
        cost_estimate=rough(512 * 512 * 1024, 1 << 20),
        name="plan_scatter",
    )(lanes, metas)


def scatter_rows(own, plan, rows, after):
    depth = rows[0].shape[1]
    return pl.pallas_call(
        functools.partial(scatter_kernel, own, len(after)),
        out_shape=jax.ShapeDtypeStruct((SRC * 16, depth), BF),
        in_specs=whole(len(plan) + len(rows)) + anywhere(len(after)),
        out_specs=whole(1)[0],
        compiler_params=PARAMS,
        cost_estimate=rough(2 * 384 * 512 * depth, 5 << 20),
        name="scatter_rows",
    )(*plan, *rows, *after)


def merge(pieces, after):
    depth = pieces[0].shape[1]
    return pl.pallas_call(
        merge_kernel,
        out_shape=jax.ShapeDtypeStruct((3 * PIECE, depth), BF),
        in_specs=whole(3) + anywhere(len(after)),
        out_specs=whole(1)[0],
        compiler_params=PARAMS,
        cost_estimate=rough(0, 2 << 20),
        name="merge",
    )(*pieces, *after)


def deq_kernel(w_ref, s_ref, out_ref):
    rows, cols = w_ref.shape[1:]
    scales = s_ref[0]
    for r in range(rows // BLOCK):
        for c in range(cols // BLOCK):
            at = (0, slice(r * BLOCK, (r + 1) * BLOCK), slice(c * BLOCK, (c + 1) * BLOCK))
            out_ref[at] = (w_ref[at].astype(F32) * scales[r : r + 1, c : c + 1]).astype(BF)


def dequantize(weight, scale):
    count, rows, cols = weight.shape

    def block(array):
        return pl.BlockSpec((1,) + array.shape[1:], lambda i: (i, 0, 0))

    return pl.pallas_call(
        deq_kernel,
        grid=(count,),
        out_shape=jax.ShapeDtypeStruct(weight.shape, BF),
        in_specs=[block(weight), block(scale)],
        out_specs=block(weight),
        compiler_params=PARAMS,
        cost_estimate=rough(count * rows * cols, 4 * count * rows * cols),
        name="dequantize",
    )(weight, scale)


def silu(value):
    return value * (1.0 / (1.0 + jnp.exp(-value)))


def ffn_kernel(in_count, out_parts, skip, *refs):
    xs, (gate_w, up_w, down_w) = refs[:in_count], refs[in_count : in_count + 3]
    refs = refs[in_count + 3 + skip :]
    outs, (gate_acc, up_acc, hidden) = refs[: len(out_parts)], refs[len(out_parts) :]
    step = pl.program_id(0)

    @pl.when(step < STEPS)
    def _():
        x = jnp.concatenate([r[...] for r in xs], axis=0)
        gate = jnp.dot(x, gate_w[0], preferred_element_type=F32)
        up = jnp.dot(x, up_w[0], preferred_element_type=F32)

        @pl.when(step == 0)
        def _():
            gate_acc[...] = gate
            up_acc[...] = up

        @pl.when(step > 0)
        def _():
            gate_acc[...] += gate
            up_acc[...] += up

    @pl.when(step >= STEPS)
    def _():
        @pl.when(step == STEPS)
        def _():
            hidden[...] = (silu(gate_acc[...]) * up_acc[...]).astype(BF)

        result = jnp.dot(hidden[...], down_w[0], preferred_element_type=F32).astype(BF)
        for ref, parts in zip(outs, out_parts):
            at = 0
            for low, high in parts:
                ref[at : at + high - low, :] = result[low:high]
                at += high - low


def early(i):
    return jnp.minimum(i, STEPS - 1)


def late(i):
    return jnp.maximum(i - STEPS, 0)


def ffn(xs, out_parts, which, weights, after):
    gate_w, up_w, down_w = weights
    depth, units = gate_w.shape[1:]
    wide = depth // STEPS
    total = sum(rows for _, rows, _ in xs)
    out_rows = [sum(high - low for low, high in parts) for parts in out_parts]
    in_specs = [
        pl.BlockSpec((rows, wide), lambda i, place=place: (place, early(i))) for _, rows, place in xs
    ]
    in_specs += [pl.BlockSpec((1, wide, units), lambda i: (which, early(i), 0))] * 2
    in_specs += [pl.BlockSpec((1, units, wide), lambda i: (which, 0, late(i)))]
    return pl.pallas_call(
        functools.partial(ffn_kernel, len(xs), out_parts, len(after)),
        grid=(2 * STEPS,),
        out_shape=[jax.ShapeDtypeStruct((r, depth), BF) for r in out_rows],
        in_specs=in_specs + anywhere(len(after)),
        out_specs=[pl.BlockSpec((r, wide), lambda i: (0, late(i))) for r in out_rows],
        scratch_shapes=[
            pltpu.VMEM((total, units), F32),
            pltpu.VMEM((total, units), F32),
            pltpu.VMEM((total, units), BF),
        ],
        compiler_params=PARAMS,
        cost_estimate=rough(6 * total * units * depth, 4 * total * depth + 6 * units * depth),
        name="ffn",
    )(*[x for x, _, _ in xs], gate_w, up_w, down_w, *after)


def extra_kernel(skip, place_ref, own_in, other_in, gate_w, up_w, down_a, down_b, *refs):
    own_out, other_out, gate_acc, up_acc, hidden = refs[skip:]
    step = pl.program_id(0)
    units = gate_w.shape[2]

    @pl.when(step < 2 * STEPS)
    def _():
        x = jnp.concatenate([own_in[...], other_in[...]], axis=0)
        gate = jnp.dot(x, gate_w[0], preferred_element_type=F32)
        up = jnp.dot(x, up_w[0], preferred_element_type=F32)
        opening = (step == 0) | (step == STEPS)

        @pl.when(opening)
        def _():
            gate_acc[...] = gate
            up_acc[...] = up

        @pl.when(jnp.logical_not(opening))
        def _():
            gate_acc[...] += gate
            up_acc[...] += up

    for j in range(2):

        @pl.when(step == (j + 1) * STEPS - 1)
        def _(j=j):
            value = silu(gate_acc[...]) * up_acc[...]
            row = lax.broadcasted_iota(jnp.int32, value.shape, 0)
            keep = ((row & 1) == j) & (place_ref[2 + j] == 1)
            hidden[:, j * units : (j + 1) * units] = jnp.where(keep, value, 0.0).astype(BF)

    @pl.when(step >= 2 * STEPS)
    def _():
        down = jnp.concatenate([down_a[0], down_b[0]], axis=0)
        result = jnp.dot(hidden[...], down, preferred_element_type=F32).astype(BF)
        half = own_out.shape[0]
        own_out[...] = result[:half]
        other_out[...] = result[half:]


def extra_ffn(places, own, other, weights, after):
    gate_w, up_w, down_w = weights
    depth, units = gate_w.shape[1:]
    wide = depth // STEPS
    half = own.shape[0]

    def first(i):
        return jnp.where(i < 2 * STEPS, i & (STEPS - 1), STEPS - 1)

    def last(i):
        return jnp.maximum(i - 2 * STEPS, 0)

    def turn(i):
        return jnp.where(i < STEPS, 0, 1)

    rows_in = pl.BlockSpec((half, wide), lambda i, s: (0, first(i)))
    gate_in = pl.BlockSpec((1, wide, units), lambda i, s: (s[turn(i)], first(i), 0))
    rows_out = pl.BlockSpec((half, wide), lambda i, s: (0, last(i)))
    spec = pltpu.PrefetchScalarGridSpec(
        num_scalar_prefetch=1,
        grid=(3 * STEPS,),
        in_specs=[rows_in, rows_in, gate_in, gate_in]
        + [pl.BlockSpec((1, units, wide), lambda i, s, j=j: (s[j], 0, last(i))) for j in range(2)]
        + anywhere(len(after)),
        out_specs=[rows_out, rows_out],
        scratch_shapes=[
            pltpu.VMEM((2 * half, units), F32),
            pltpu.VMEM((2 * half, units), F32),
            pltpu.VMEM((2 * half, 2 * units), BF),
        ],
    )
    return pl.pallas_call(
        functools.partial(extra_kernel, len(after)),
        grid_spec=spec,
        out_shape=[jax.ShapeDtypeStruct((half, depth), BF)] * 2,
        compiler_params=PARAMS,
        cost_estimate=rough(20 * half * units * depth, 32 << 20),
        name="extra_ffn",
    )(places, own, other, gate_w, up_w, down_w, down_w, *after)


def add(*values):
    total = values[0].astype(F32)
    for value in values[1:]:
        total = total + value.astype(F32)
    return total.astype(BF)


def gather_line(own, after):
    pieces = [own] + [None] * (NZ - 1)
    up = down = own
    for step in range(1, NZ // 2 + 1):
        up = expert_move(up, dz=-1)
        pieces[step] = up
        if step < NZ // 2:
            down = expert_move(down, dz=1)
            pieces[NZ - step] = down
            up = relay([up], [after[step - 1]])[0]
    return pieces + [expert_move(piece, flip=True) for piece in pieces]


def scatter_line(own, other):
    arrived = expert_move(other, flip=True)

    def term(dz):
        return own[dz * 32 : dz * 32 + 32], arrived[dz * 32 : dz * 32 + 32]

    up = add(*term(NZ // 2))
    for dz in range(NZ // 2 - 1, 0, -1):
        up = add(expert_move(up, dz=1), *term(dz))
    down = add(*term(NZ // 2 + 1))
    for dz in range(NZ // 2 + 2, NZ):
        down = add(expert_move(down, dz=-1), *term(dz))
    return [expert_move(up, dz=1), expert_move(down, dz=-1), *term(0)]


def spread_dp(block, cut, after=()):
    left = dp_move(block, 1)
    right = dp_move(block, -1)
    far = cut_far(left, right, cut, after) if after else (left[:cut], right[cut:])
    return [block, left, right, dp_move(far[0], 1), dp_move(far[1], -1), *far]


def sum_dp_first(parts):
    minus, plus, left_a, right_b, own = parts
    got_minus = dp_move(minus, -1)
    got_plus = dp_move(plus, 1)
    left_a, right_b = fold(left_a, got_minus, right_b, got_plus)
    return left_a, got_minus, got_plus, right_b, own


def sum_dp_second(state, after):
    left_a, got_minus, got_plus, right_b, own = state
    got_left_a = dp_move(left_a, -1)
    got_right_b = dp_move(right_b, 1)
    return settle(own, (got_left_a, got_minus, got_plus, got_right_b), after), [got_left_a, got_right_b]


def per_device(
    tokens,
    routes,
    route_weight,
    gate_weight,
    up_weight,
    down_weight,
    gate_scale,
    up_scale,
    down_scale,
):
    rows, depth = tokens.shape
    top = routes.shape[1]
    experts = gate_weight.shape[0] * NY * NZ * NC
    all_rows = rows * NX * NY * NZ * NC
    place = lax.axis_index("expert")
    y, line = place // (NZ * NC), place % (NZ * NC)
    lane = jnp.arange(META, dtype=jnp.int32)

    named = (routes[:, :, None] == lane[None, None, :]).astype(F32)
    counts = jnp.broadcast_to(jnp.sum(named, axis=(0, 1))[None], (8, META))
    counts = sum([dp_move(counts, d) for d in range(1, NX)], counts)
    carried = pack(tokens, routes.T, route_weight.T, counts)
    weights = (
        dequantize(gate_weight, gate_scale),
        dequantize(up_weight, up_scale),
        dequantize(down_weight, down_scale),
    )
    pieces = gather_line(carried, weights)

    lane_expert = ((((y + lane % NY) % NY) * (NZ * NC) + line) * 2 + lane // NY).astype(F32)
    lanes = jnp.broadcast_to(jnp.where(lane < 8, lane_expert, -1.0)[None], (8, META))
    near, *blocks, tokens_line, metas, counts = gather_rows(lanes, pieces, depth)
    near = spread_dp(near, PIECE)
    moved = [[expert_move(blocks[w * 3 + d - 1], dy=d) for d in range(1, NY)] for w in range(2)]

    first, hot, totals = merge_pick(counts, metas, tokens_line, moved[0], near[1:3])
    load_share = totals[0, :experts] * (experts / (all_rows * top))
    hot_id = hot[0:2, 0].astype(jnp.int32)
    places = jnp.concatenate([hot_id & 1, ((hot_id >> 1) == place).astype(jnp.int32)])
    spare = jnp.where(lane == 8, hot[0:1], jnp.where(lane == 9, hot[1:2], lanes))
    plan = plan_scatter(spare, metas)
    size = 3 * PIECE
    cuts = [(size + EXTRA) // 2, size - 4 * EXTRA]
    spreads = [spread_dp(first, cuts[0], [*moved[1], *near[3:5], plan[0]])]
    spreads.append(spread_dp(merge(moved[1], spreads[0][5:]), cuts[1]))

    order = [spreads[0][i] for i in (0, 1, 4, 2)]
    extra = join_extra(order, [spreads[1][0], spreads[0][3]])
    extra = stack([extra] + [expert_move(extra, dy=d) for d in range(1, NY)], spreads[1][1:3])
    extra_other = expert_move(extra, flip=True)

    half = NY * PIECE // 2
    out_parts = [
        [(4 * half, 5 * half), (half, 2 * half)],
        [(5 * half, 6 * half), (2 * half, 3 * half)],
        [(0, half)],
        [(3 * half, 4 * half)],
        [(6 * half, 8 * half)],
    ]
    parts = []
    after = [extra, plan[0]]
    for which in range(2):
        cut, block = cuts[which], spreads[which]
        xs = [
            (near[1], PIECE, which),
            (block[1], size, 0),
            (near[2], PIECE, which),
            (block[2], size, 0),
            (near[3 + which], PIECE, 0),
            (block[3], cut, 0),
            (block[4], size - cut, 0),
            (near[0], PIECE, which),
            (block[0], size, 0),
        ]
        parts.append(list(ffn(xs, out_parts, which, weights, after)))
        if which == 0:
            parts[0][:2] = relay(parts[0][:2], [near[4], *spreads[1][3:5]])
            own, other = extra_ffn(places, extra, extra_other, weights, parts[0][:1])
            state = sum_dp_first(parts[0])
            extra = pair_sum(own, expert_move(other, flip=True), [])
            after = [own, state[0]]

    size = NX * EXTRA
    extra = add(
        extra[:size],
        *[expert_move(extra[d * size : (d + 1) * size], dy=-d) for d in range(1, NY)],
    )
    group, arrived = sum_dp_second(state, [extra])
    parts[1][:2] = relay(parts[1][:2], arrived)
    extra = add(
        extra[:EXTRA], *[dp_move(extra[d * EXTRA : (d + 1) * EXTRA], -d) for d in range(1, NX)]
    )
    returned = [group[0]] + [expert_move(group[d], dy=-d) for d in range(1, NY)]
    group, _ = sum_dp_second(sum_dp_first(parts[1]), returned)
    returned += [group[0]] + [expert_move(group[d], dy=-d) for d in range(1, NY)]
    other = scatter_rows(False, plan[:2], returned, [extra])
    own = scatter_rows(True, [*plan, extra], returned, [])
    terms = scatter_line(own, other)
    return add(*terms), load_share


def solution(mesh):
    in_specs = (
        P(("dp", "expert"), None),
        P(("dp", "expert"), None),
        P(("dp", "expert"), None),
        P("expert", None, "dp"),
        P("expert", None, "dp"),
        P("expert", "dp", None),
        P("expert", None, "dp"),
        P("expert", None, "dp"),
        P("expert", "dp", None),
    )
    out_specs = (P(("dp", "expert"), None), P())
    return jax.shard_map(
        per_device, mesh=mesh, in_specs=in_specs, out_specs=out_specs, check_vma=False
    )
```
